32 devices in a mesh: groups: 2 (over x), seq: 16 (over z, y, core).
Axes of the slice: x: 2, y: 2, z: 4, core: 2. Of those that a mesh axis runs over, the one named last changes fastest.
Arguments:
- tokens: bfloat16 [8192, 2048], P(('groups', 'seq')), parts along dimension 0, may hold values from -60 to 60
- w_query: bfloat16 [2048, 1024], P('seq'), may hold values from -0.125 to 0.125
- w_keyval: bfloat16 [2048, 2048], P('seq'), may hold values from -0.125 to 0.125
- global_off: int32 [32], P(('groups', 'seq')), parts along dimension 0, may hold values from 0 to 255
- rand_dev: int32 [128, 8, 3], P('groups'), parts along dimension 0, may hold values from 0 to 15, all different within a row; in each aligned block of 32 rows (0 to 31, 32 to 63, ..., all dimensions but the last counted through in order) at most 9 rows name the same one
- rand_sub: int32 [128, 8, 3], P('groups'), parts along dimension 0, may hold values from 0 to 3
Outputs:
- context: bfloat16 [8192, 1024], P(('groups', 'seq')), parts along dimension 0
The draws below stay inside these ranges and needn't reach their ends.
There are 2 independent parts, one for each index of `groups`. The reference program is written for one: setup_inputs(seed, part) draws one part's arguments, and reference() takes and returns one part's arrays. A program takes and returns all parts, laid end to end along the dimension named above; an argument that names none is the same for every part. Nothing has to cross between parts.
Inputs may be any that keep to these rules, and one draw needn't show every extreme that they name: Over the 4 query blocks of one shard and all heads, no shard is named by more than 9 entries of rand_dev, and this bound is reached in every draw; the 3 entries of one query block and head name different shards.
All inputs are finite; a program needn't handle non-finite values.
Results may differ from the reference program's by a relative error of at most 0.0045.
The reference program's roundings to bfloat16 on the way (of `query`, `keyval` and `weights`) count: a program that leaves them out, or rounds other values in their place, can miss the bound.
Values may be sent and summed in bfloat16 or wider, within the bound.
A program may use at most 128 MiB of HBM per device.

```python
import math
import jax
import jax.numpy as jnp
import numpy as np
from jax import lax

D = 2048
H = 8
HD = 128
BLOCK = 64
R = 3
GLOB_DEV = 1
BLK_DEV = 4
TOK_DEV = 256
NB = 64
TOKENS = 4096
G = 16
CAP = 9
N_SEQ = 16


def draw_tokens(key, part):
    base = jnp.clip(jax.random.normal(key, (TOKENS, D), jnp.float32), -6.0, 6.0)
    return base.astype(jnp.bfloat16)


def touch_ends(entries, stream_key, low, top_value):
    longest = entries.shape.index(max(entries.shape))
    spots = []
    for shift in (0, 1):
        where = [jax.random.randint(jax.random.fold_in(stream_key, axis), (), 0, length) for axis, length in enumerate(entries.shape)]
        where[longest] = (where[longest] + shift) % entries.shape[longest]
        spots.append(tuple(where))
    return entries.at[spots[0]].set(low).at[spots[1]].set(top_value)


def block_scale(key, dims, cuts, smallest, largest):
    level = 1.0
    for axis_at, shards_of in cuts:
        steps = jax.random.uniform(jax.random.fold_in(jax.random.fold_in(key, 6), axis_at), (shards_of,), jnp.float32, smallest / len(cuts), largest / len(cuts))
        level = level * jnp.repeat(jnp.exp(steps), dims[axis_at] // shards_of).reshape((-1,) + (1,) * (len(dims) - 1 - axis_at))
    return level


def shared_out(rng, own, number, rows, count, top, reach, slope):
    ranking = jax.random.permutation(rng, count)
    packed, ordinary = portions_of(count, rows * top, reach, slope, True), portions_of(count, rows * top, reach, slope, False)
    places = jnp.arange(count)

    def named(tallies, rotation):
        used = int((tallies > 0).sum())
        fixed = max(1, used // 4)
        shifted = fixed + (places - fixed + rotation * (used - fixed)) % max(1, count - fixed)
        return jnp.zeros((count,), jnp.int32).at[ranking[jnp.where(places < fixed, places, shifted)]].set(jnp.asarray(tallies, jnp.int32))

    tallies = jnp.where(number % 4 == 0, named(packed, number // 4), named(ordinary, number - number // 4 - 1))
    mixed = jax.random.permutation(jax.random.fold_in(own, 3), count)
    donor, receiver = mixed[0:count // 2 * 2:2], mixed[1:count // 2 * 2:2]
    margin = jnp.minimum(tallies[donor] - 1, reach - tallies[receiver]) // 2
    margin = jnp.where((donor == ranking[0]) | (receiver == ranking[0]) | (tallies[receiver] == 0), 0, jnp.maximum(margin, 0))
    shifted = jax.random.randint(jax.random.fold_in(own, 4), (count // 2,), 0, 1 << 20) % (margin + 1)
    tallies = tallies.at[donor].add(-shifted).at[receiver].add(shifted)
    items = jnp.searchsorted(jnp.cumsum(tallies), jnp.arange(rows * top), side="right").astype(jnp.int32)
    table = items.reshape(top, rows).T
    table = table[jax.random.permutation(jax.random.fold_in(own, 1), rows)]
    rotation = jax.random.randint(jax.random.fold_in(own, 2), (rows, 1), 0, top)
    return jnp.take_along_axis(table, (jnp.arange(top)[None, :] + rotation) % top, axis=1)


def portions_of(number_of, total, limit, slope, full):
    weights = [(1 << 20) // math.isqrt(grade ** slope) + 1 for grade in range(1, number_of + 1)]
    largest = limit if full else min(limit, max(-(-total // number_of), total * weights[0] // sum(weights)))
    least = 1 if total - largest >= number_of - 1 else 0
    counts, spare = [largest] + [least] * (number_of - 1), total - largest - least * (number_of - 1)
    while spare > 0:
        free = [i for i in range(1, number_of) if counts[i] < largest] or [i for i in range(1, number_of) if counts[i] < limit]
        mass, remaining = sum([weights[i] for i in free]), spare
        for i in free:
            more = min(limit - counts[i], max(1, remaining * weights[i] // mass), spare)
            counts[i] = counts[i] + more
            spare = spare - more
    return np.array(counts)


def gaussian(rng, extent, scale, reach, shards=(), held_as=jnp.bfloat16):
    array = scale * jax.random.normal(rng, extent, jnp.float32)
    if shards:
        array = array * block_scale(rng, extent, shards, -0.22, 0.18)
    return jnp.clip(array, -reach, reach).astype(held_as)


def setup_inputs(seed: int = 0, part: int = 0) -> dict:
    seeds = jax.random.split(jax.random.key(seed), 7)
    own_keys = jax.random.split(jax.random.fold_in(seeds[6], part), 7)
    tokens = draw_tokens(jax.random.fold_in(jax.random.fold_in(seeds[6], part), 71), part)
    w_query = gaussian(seeds[1], (D, H * HD), D ** -0.5, 0.125, ((0, 16),))
    w_keyval = gaussian(seeds[2], (D, 2 * H * HD), D ** -0.5, 0.125, ((0, 16),))
    global_off = touch_ends(jax.random.randint(own_keys[3], (G,), 0, TOK_DEV), jax.random.fold_in(own_keys[3], 1), 0, TOK_DEV - 1).astype(jnp.int32)
    rand_dev_keys = jax.random.split(jax.random.fold_in(own_keys[4], 1), NB * H // (BLK_DEV * H))
    rand_dev_turns = jax.random.permutation(jax.random.fold_in(own_keys[4], 3), NB * H // (BLK_DEV * H))
    rand_dev = jax.vmap(lambda own, number: shared_out(jax.random.fold_in(own_keys[4], 2), own, number, BLK_DEV * H, N_SEQ, R, CAP, 1))(rand_dev_keys, rand_dev_turns).reshape((NB, H, R))
    rand_sub = touch_ends(jax.random.randint(own_keys[5], (NB, H, R), 0, BLK_DEV), jax.random.fold_in(own_keys[5], 1), 0, BLK_DEV - 1).astype(jnp.int32)
    return dict(tokens=tokens, w_query=w_query, w_keyval=w_keyval, global_off=global_off, rand_dev=rand_dev, rand_sub=rand_sub)


def reference(tokens, w_query, w_keyval, global_off, rand_dev, rand_sub):
    def project(rows):
        query = jnp.dot(rows, w_query, preferred_element_type=jnp.float32).astype(jnp.bfloat16)
        keyval = jnp.dot(rows, w_keyval, preferred_element_type=jnp.float32).astype(jnp.bfloat16)
        return query, keyval

    query, keyval = lax.map(project, tokens.reshape(N_SEQ, TOK_DEV, D))
    query = query.reshape(NB, BLOCK, H, HD)
    keyval = keyval.reshape(NB, BLOCK, 2, H, HD)
    positions = (jnp.arange(G, dtype=jnp.int32) // GLOB_DEV) * TOK_DEV + global_off
    glob = keyval.reshape(TOKENS, 2, H, HD)[positions].astype(jnp.float32)
    block_ids = rand_dev * BLK_DEV + rand_sub
    zero_blk = jnp.zeros((1, BLOCK, 2, H, HD), keyval.dtype)
    padded = jnp.concatenate([zero_blk, keyval, zero_blk], axis=0)
    head_ids = jnp.arange(H, dtype=jnp.int32)[None, :, None]
    scale = HD ** -0.5

    def attend(index):
        start = (index * BLK_DEV).astype(jnp.int32)
        qry = lax.dynamic_slice_in_dim(query, start, BLK_DEV, 0).astype(jnp.float32)
        win = jnp.concatenate([lax.dynamic_slice_in_dim(padded, start + j, BLK_DEV, 0) for j in range(3)], axis=1).astype(jnp.float32)
        ids = lax.dynamic_slice_in_dim(block_ids, start, BLK_DEV, 0)
        fetched = keyval[ids, :, :, head_ids, :].astype(jnp.float32)
        s_win = jnp.einsum('bqhd,bkhd->bhqk', qry, win[:, :, 0]) * scale
        s_rnd = jnp.einsum('bqhd,bhrkd->bhqrk', qry, fetched[:, :, :, :, 0]).reshape(BLK_DEV, H, BLOCK, R * BLOCK) * scale
        s_glb = jnp.einsum('bqhd,ghd->bhqg', qry, glob[:, 0]) * scale
        blk = start + jnp.arange(BLK_DEV, dtype=jnp.int32)
        left_ok = jnp.repeat((blk > 0)[:, None], BLOCK, axis=1)
        right_ok = jnp.repeat((blk < NB - 1)[:, None], BLOCK, axis=1)
        mid_ok = jnp.ones((BLK_DEV, BLOCK), dtype=bool)
        win_ok = jnp.concatenate([left_ok, mid_ok, right_ok], axis=1)
        s_win = jnp.where(win_ok[:, None, None, :], s_win, -jnp.inf)
        scores = jnp.concatenate([s_win, s_rnd, s_glb], axis=3)
        top = jnp.max(scores, axis=3, keepdims=True)
        expo = jnp.exp(scores - top)
        weights = (expo / jnp.sum(expo, axis=3, keepdims=True)).astype(jnp.bfloat16).astype(jnp.float32)
        w_win = weights[..., :3 * BLOCK]
        w_rnd = weights[..., 3 * BLOCK:3 * BLOCK + R * BLOCK].reshape(BLK_DEV, H, BLOCK, R, BLOCK)
        w_glb = weights[..., 3 * BLOCK + R * BLOCK:]
        ctx = jnp.einsum('bhqk,bkhd->bqhd', w_win, win[:, :, 1])
        ctx = ctx + jnp.einsum('bhqrk,bhrkd->bqhd', w_rnd, fetched[:, :, :, :, 1])
        ctx = ctx + jnp.einsum('bhqg,ghd->bqhd', w_glb, glob[:, 1])
        return ctx.astype(jnp.bfloat16)

    context = lax.map(attend, jnp.arange(N_SEQ, dtype=jnp.int32))
    return context.reshape(TOKENS, H * HD)
```

```python
import functools

import jax
import jax.numpy as jnp
from jax import lax
from jax.experimental import pallas as pl
from jax.experimental.pallas import tpu as pltpu
from jax.sharding import PartitionSpec as P

H = 8
HD = 128
BLOCK = 64
R = 3
BLK_DEV = 4
LANES = 4
MESH = pl.DeviceIdType.MESH


def padded_2(block, sides, width):
    for axis, dim in sides:
        count = lax.axis_size(axis)
        forward = [(i, i + 1) for i in range(count - 1)]
        backward = [(target, source) for source, target in forward]
        low = lax.ppermute(
            lax.slice_in_dim(block, block.shape[dim] - width, None, axis=dim), axis, forward
        )
        high = lax.ppermute(lax.slice_in_dim(block, 0, width, axis=dim), axis, backward)
        block = jnp.concatenate([low, block, high], axis=dim)
    return block


def fold_rows(left, piece):
    return jnp.dot(left, piece, preferred_element_type=jnp.float32)


def local(tokens, w_query, w_keyval, global_off, rand_dev, rand_sub):
    ntok = tokens.shape[0]
    nseq = lax.axis_size("seq")
    me_index = lax.axis_index("seq")
    nblk = ntok // BLOCK
    inner = H * HD
    glob_rows = lax.all_gather(jnp.take(tokens, global_off, axis=0), "seq", axis=0, tiled=True)
    left_kv = jnp.concatenate([tokens, glob_rows], axis=0)
    query = fold_rows(tokens, lax.all_gather(w_query, "seq", axis=0, tiled=True))
    keyval = fold_rows(left_kv, lax.all_gather(w_keyval, "seq", axis=0, tiled=True))
    query = query.astype(jnp.bfloat16)
    keyval = keyval.astype(jnp.bfloat16)
    glob_kv = keyval[ntok:]
    keyval = keyval[:ntok]
    glob_kv = glob_kv.reshape(glob_kv.shape[0], 2, H, HD)
    padded = padded_2(keyval, (("seq", 0),), BLOCK)
    window = jnp.concatenate(
        [padded[j * BLOCK : j * BLOCK + ntok].reshape(nblk, BLOCK, 2, H, HD) for j in range(3)],
        axis=1,
    )
    capacity = max(2, 3 * BLK_DEV * H * R // (2 * nseq))
    nreq = nblk * H * R
    dev_all = rand_dev.reshape(nseq, nreq)
    sub_all = rand_sub.reshape(nseq, nreq)
    match = (dev_all == me_index).astype(jnp.int32)
    slot_all = jnp.cumsum(match, axis=1) - 1
    head_of = jnp.arange(nreq, dtype=jnp.int32) // R % H
    code_all = head_of[None, :] * nblk + sub_all
    picked = (match[:, None, :] == 1) & (
        slot_all[:, None, :] == jnp.arange(capacity, dtype=jnp.int32)[None, :, None]
    )
    source = jnp.sum(jnp.where(picked, code_all[:, None, :], 0), axis=2)
    tiles = (
        keyval.reshape(nblk, BLOCK, 2, H, HD)
        .transpose(3, 0, 1, 2, 4)
        .reshape(H * nblk, BLOCK, 2 * HD)
    )
    outgoing = jnp.take(tiles, source, axis=0)
    incoming = lax.all_to_all(outgoing, "seq", split_axis=0, concat_axis=0, tiled=True)
    my_dev = lax.dynamic_slice_in_dim(rand_dev, me_index * nblk, nblk, 0).reshape(nreq)
    onehot = (my_dev[:, None] == jnp.arange(nseq, dtype=jnp.int32)[None, :]).astype(jnp.int32)
    my_slot = jnp.sum(onehot * (jnp.cumsum(onehot, axis=0) - 1), axis=1)
    flat_index = my_dev * capacity + my_slot
    fetched = jnp.take(incoming.reshape(nseq * capacity, BLOCK, 2 * HD), flat_index, axis=0)
    fetched = fetched.reshape(nblk, H, R, BLOCK, 2, HD)
    scale = HD ** (-0.5)
    qry = query.reshape(nblk, BLOCK, H, HD)
    s_win = (
        jnp.einsum("bqhd,bkhd->bhqk", qry, window[:, :, 0], preferred_element_type=jnp.float32)
        * scale
    )
    s_rnd = (
        jnp.einsum(
            "bqhd,bhrkd->bhqrk", qry, fetched[:, :, :, :, 0], preferred_element_type=jnp.float32
        ).reshape(nblk, H, BLOCK, R * BLOCK)
        * scale
    )
    s_glb = (
        jnp.einsum("bqhd,ghd->bhqg", qry, glob_kv[:, 0], preferred_element_type=jnp.float32) * scale
    )
    blk_ids = me_index * nblk + jnp.arange(nblk, dtype=jnp.int32)
    left_ok = jnp.repeat((blk_ids > 0)[:, None], BLOCK, axis=1)
    right_ok = jnp.repeat((blk_ids < nseq * nblk - 1)[:, None], BLOCK, axis=1)
    middle_ok = jnp.ones((nblk, BLOCK), dtype=bool)
    window_ok = jnp.concatenate([left_ok, middle_ok, right_ok], axis=1)
    s_win = jnp.where(window_ok[:, None, None, :], s_win, -jnp.inf)
    scores = jnp.concatenate([s_win, s_rnd, s_glb], axis=3)
    highest = jnp.max(scores, axis=3, keepdims=True)
    expo = jnp.exp(scores - highest)
    weights = (expo / jnp.sum(expo, axis=3, keepdims=True)).astype(jnp.bfloat16)
    w_win = weights[..., : 3 * BLOCK]
    w_rnd = weights[..., 3 * BLOCK : 3 * BLOCK + R * BLOCK].reshape(nblk, H, BLOCK, R, BLOCK)
    w_glb = weights[..., 3 * BLOCK + R * BLOCK :]
    ctx = jnp.einsum("bhqk,bkhd->bqhd", w_win, window[:, :, 1], preferred_element_type=jnp.float32)
    ctx = ctx + jnp.einsum(
        "bhqrk,bhrkd->bqhd", w_rnd, fetched[:, :, :, :, 1], preferred_element_type=jnp.float32
    )
    ctx = ctx + jnp.einsum(
        "bhqg,ghd->bqhd", w_glb, glob_kv[:, 1], preferred_element_type=jnp.float32
    )
    return ctx.reshape(ntok, inner).astype(jnp.bfloat16)


def fused_kernel(
    planes, tok_hbm, wq_hbm, wkv_hbm, off_ref, blocks_ref, out_ref,
    tok, wts, qry, kv, events, ctx,
    local_sem, w_send, w_recv, wx_send, wx_recv, wl_send, wl_recv,
    t_send, t_recv, k_send, k_recv, e_send, e_recv, c_send, c_recv,
):
    ntok = tok_hbm.shape[0]
    slot_rows = tok.shape[1]
    extra = slot_rows - ntok
    nblk = ntok // BLOCK
    heads = H // planes
    cols = heads * HD
    half = wts.shape[3]
    x = lax.axis_index("groups")
    me = lax.axis_index("seq")
    z = me // LANES
    lane = me % LANES
    core_lane = lane + 1 - 2 * (lane % 2)
    y_lane = (lane + 2) % LANES
    diag_lane = (core_lane + 2) % LANES

    def at(plane, where):
        return {"seq": plane * LANES + where}

    x_peer = {"groups": 1 - x}
    core_peer = at(z, core_lane)
    y_peer = at(z, y_lane)
    diag_peer = at(z, diag_lane)

    def remote(src, dst, send, recv, peer):
        return pltpu.make_async_remote_copy(
            src_ref=src, dst_ref=dst, send_sem=send, recv_sem=recv, device_id=peer,
            device_id_type=MESH,
        )

    own_tok = pltpu.make_async_copy(tok_hbm, tok.at[z, pl.ds(0, ntok)], local_sem.at[0])
    own_tok.start()

    def weight_parts(plane):
        rows = pl.ds(pl.multiple_of(x * half, half), half)
        start = pl.multiple_of(plane * cols, cols)
        return (
            wq_hbm.at[rows, pl.ds(start, cols)],
            wkv_hbm.at[rows, pl.ds(start, cols)],
            wkv_hbm.at[rows, pl.ds(pl.multiple_of(H * HD + plane * cols, cols), cols)],
        )

    own_w = []
    for part, src in enumerate(weight_parts(z)):
        copy = pltpu.make_async_copy(
            src, wts.at[z, lane, x, :, pl.ds(part * cols, cols)], local_sem.at[1 + part]
        )
        copy.start()
        own_w.append(copy)

    barrier = pltpu.get_barrier_semaphore()
    for step in range(1, planes):
        pl.semaphore_signal(
            barrier, inc=1, device_id=at((z + step) % planes, lane), device_id_type=MESH
        )
    for peer in (x_peer, core_peer, y_peer, diag_peer):
        pl.semaphore_signal(barrier, inc=1, device_id=peer, device_id_type=MESH)
    pl.semaphore_wait(barrier, planes - 1 + 4)

    def weight_copy(step, part):
        plane = (z + step) % planes
        return remote(
            weight_parts(plane)[part],
            wts.at[z, lane, x, :, pl.ds(part * cols, cols)],
            w_send.at[step - 1, part], w_recv.at[step - 1, part], at(plane, lane),
        )

    def weight_landed(step, part):
        plane = (z + planes - step) % planes
        here = wts.at[plane, lane, x, :, pl.ds(part * cols, cols)]
        return remote(here, here, w_send.at[step - 1, part], w_recv.at[step - 1, part], at(plane, lane))

    for step in range(1, planes):
        for part in range(3):
            weight_copy(step, part).start()

    own_tok.wait()
    spot = lax.broadcasted_iota(jnp.int32, (extra, ntok), 0) == me
    event = lax.broadcasted_iota(jnp.int32, (extra, ntok), 1) == off_ref[0]
    pick = jnp.where(spot & event, 1.0, 0.0).astype(jnp.bfloat16)
    tok[z, pl.ds(ntok, extra), :] = jnp.dot(
        pick, tok[z, pl.ds(0, ntok), :], preferred_element_type=jnp.float32
    ).astype(jnp.bfloat16)

    def tok_up(source):
        return remote(tok.at[source], tok.at[source], t_send.at[0, source], t_recv.at[source], at(z + 1, lane))

    def tok_down(source):
        return remote(tok.at[source], tok.at[source], t_send.at[1, source], t_recv.at[source], at(z - 1, lane))

    can_up, can_down = z + 1 < planes, z >= 1

    @pl.when(can_up)
    def _():
        tok_up(z).start()

    @pl.when(can_down)
    def _():
        tok_down(z).start()

    def pass_on(dist):
        @pl.when(z >= dist)
        def _():
            tok_up_or_recv(z - dist)

            @pl.when(can_up)
            def _():
                tok_up(z - dist).start()

        @pl.when(z + dist < planes)
        def _():
            tok_up_or_recv(z + dist)

            @pl.when(can_down)
            def _():
                tok_down(z + dist).start()

    def tok_up_or_recv(source):
        remote(tok.at[source], tok.at[source], t_send.at[0, source], t_recv.at[source], core_peer).wait_recv()

    for copy in own_w:
        copy.wait()
    for step in range(1, planes):
        for part in range(3):
            weight_landed(step, part).wait_recv()
    x_out = remote(wts.at[:, lane, x], wts.at[:, lane, x], wx_send, wx_recv, x_peer)
    x_out.start()
    x_in = remote(wts.at[:, lane, 1 - x], wts.at[:, lane, 1 - x], wx_send, wx_recv, x_peer)
    x_in.wait_recv()

    def lane_copy(which, index, peer):
        return remote(wts.at[:, which], wts.at[:, which], wl_send.at[index], wl_recv.at[index], peer)

    lane_copy(lane, 0, y_peer).start()
    lane_copy(lane, 1, core_peer).start()
    if planes > 1:
        pass_on(1)
    lane_copy(y_lane, 0, y_peer).wait_recv()
    lane_copy(y_lane, 2, core_peer).start()
    lane_copy(core_lane, 1, core_peer).wait_recv()
    lane_copy(diag_lane, 2, core_peer).wait_recv()

    def order_of(plane):
        return sorted(range(planes), key=lambda p: (abs(p - plane), p))

    def nth(index):
        value = jnp.int32(order_of(0)[index])
        for plane in range(1, planes):
            value = jnp.where(z == plane, order_of(plane)[index], value)
        return value

    order = [nth(i) for i in range(planes)]

    def kv_rows(plane, where):
        return kv.at[pl.ds((plane * LANES + where) * nblk, nblk)]

    def kv_copy(index, which, where, peer):
        ref = kv_rows(order[index], where)
        return remote(ref, ref, k_send.at[which, index], k_recv.at[which, index], peer)

    def project(index):
        p = order[index]
        weights = wts[...].reshape(-1, 3 * cols)
        res = jnp.dot(tok[p], weights, preferred_element_type=jnp.float32)
        res = res.astype(jnp.bfloat16)
        qry[p] = res[:ntok, :cols]
        kv_rows(p, lane)[...] = res[:ntok, cols:].reshape(nblk, BLOCK, 2 * cols)
        events[lane, p] = res[ntok:, cols:]
        kv_copy(index, 0, lane, y_peer).start()
        kv_copy(index, 1, lane, core_peer).start()

    def kv_forward(index):
        kv_copy(index, 0, y_lane, y_peer).wait_recv()
        kv_copy(index, 2, y_lane, core_peer).start()

    project(0)
    for index in range(1, planes):
        if index > 1:
            pass_on(index)
        project(index)
        kv_forward(index - 1)

    def event_copy(index, where, peer):
        return remote(events.at[where], events.at[where], e_send.at[index], e_recv.at[index], peer)

    partners = ((y_lane, y_peer), (core_lane, core_peer), (diag_lane, diag_peer))
    for index, (where, peer) in enumerate(partners):
        event_copy(index, lane, peer).start()
    kv_forward(planes - 1)
    for index in range(planes):
        kv_copy(index, 1, core_lane, core_peer).wait_recv()
        kv_copy(index, 2, diag_lane, core_peer).wait_recv()

    for index, (where, peer) in enumerate(partners):
        event_copy(index, where, peer).wait_recv()
    glob = events[...].reshape(LANES * planes, extra, 2 * cols).astype(jnp.float32)
    glob = jnp.sum(glob, axis=0)[: planes * LANES].astype(jnp.bfloat16)
    total_blocks = planes * LANES * nblk
    scale = HD ** (-0.5)
    keys = (3 + R) * BLOCK + glob.shape[0]
    column = lax.broadcasted_iota(jnp.int32, (BLOCK, keys), 1)

    def ctx_copy(plane, index):
        return remote(
            ctx.at[plane],
            out_ref.at[:, pl.ds(pl.multiple_of(z * cols, cols), cols)],
            c_send.at[index], c_recv.at[z], at(plane, lane),
        )

    def attend(plane):
        def body(sub, carry):
            block = (plane * LANES + lane) * nblk + sub
            starts = [
                jnp.maximum(block - 1, 0),
                block,
                jnp.minimum(block + 1, total_blocks - 1),
            ]
            hidden = ((column < BLOCK) & (block == 0)) | (
                (column >= 2 * BLOCK) & (column < 3 * BLOCK) & (block == total_blocks - 1)
            )
            q_rows = pl.ds(pl.multiple_of(sub * BLOCK, BLOCK), BLOCK)
            for h in range(heads):
                base = (block * H + z * heads + h) * R
                where = starts + [blocks_ref[base + j] for j in range(R)]
                k_cols = slice(h * HD, (h + 1) * HD)
                v_cols = slice(cols + h * HD, cols + (h + 1) * HD)
                key = jnp.concatenate(
                    [kv[w, :, k_cols] for w in where] + [glob[:, k_cols]], axis=0
                )
                val = jnp.concatenate(
                    [kv[w, :, v_cols] for w in where] + [glob[:, v_cols]], axis=0
                )
                score = lax.dot_general(
                    qry[plane, q_rows, k_cols], key, (((1,), (1,)), ((), ())),
                    preferred_element_type=jnp.float32,
                ) * scale
                score = jnp.where(hidden, -jnp.inf, score)
                expo = jnp.exp(score - jnp.max(score, axis=1, keepdims=True))
                soft = (expo / jnp.sum(expo, axis=1, keepdims=True)).astype(jnp.bfloat16)
                ctx[plane, q_rows, k_cols] = jnp.dot(
                    soft, val, preferred_element_type=jnp.float32
                ).astype(jnp.bfloat16)
            return carry

        lax.fori_loop(0, nblk, body, 0)

    for index in range(planes - 1, 0, -1):
        attend(order[index])
        ctx_copy(order[index], index).start()
    attend(z)
    own = pltpu.make_async_copy(
        ctx.at[z], out_ref.at[:, pl.ds(pl.multiple_of(z * cols, cols), cols)], local_sem.at[0]
    )
    own.start()
    own.wait()

    for index in range(1, planes):
        ctx_copy(order[index], index).wait_send()
        plane = order[index]
        there = out_ref.at[:, pl.ds(pl.multiple_of(plane * cols, cols), cols)]
        remote(ctx.at[plane], there, c_send.at[index], c_recv.at[plane], core_peer).wait_recv()
    for step in range(1, planes):
        for part in range(3):
            weight_copy(step, part).wait_send()
    x_out.wait_send()
    lane_copy(lane, 0, y_peer).wait_send()
    lane_copy(lane, 1, core_peer).wait_send()
    lane_copy(y_lane, 2, core_peer).wait_send()
    for index in range(planes):
        kv_copy(index, 0, lane, y_peer).wait_send()
        kv_copy(index, 1, lane, core_peer).wait_send()
        kv_copy(index, 2, y_lane, core_peer).wait_send()
    for index, (where, peer) in enumerate(partners):
        event_copy(index, lane, peer).wait_send()
    for source in range(planes):
        @pl.when(can_up & (z >= source))
        def _():
            tok_up(source).wait_send()

        @pl.when(can_down & (z <= source))
        def _():
            tok_down(source).wait_send()


def fused(tokens, w_query, w_keyval, global_off, rand_dev, rand_sub):
    nseq = lax.axis_size("seq")
    ntok, width = tokens.shape
    planes = nseq // LANES
    extra = -(-nseq // 16) * 16
    slot_rows = ntok + extra
    cols = H // planes * HD
    half = w_query.shape[0] // 2
    rows = (rand_dev * (ntok // BLOCK) + rand_sub).reshape(-1)
    dma = pltpu.SemaphoreType.DMA
    steps = max(planes - 1, 1)
    return pl.pallas_call(
        functools.partial(fused_kernel, planes),
        out_shape=jax.ShapeDtypeStruct((ntok, H * HD), jnp.bfloat16),
        in_specs=[pl.BlockSpec(memory_space=pl.ANY)] * 3
        + [pl.BlockSpec(memory_space=pltpu.SMEM)] * 2,
        out_specs=pl.BlockSpec(memory_space=pl.ANY),
        scratch_shapes=[
            pltpu.VMEM((planes, slot_rows, width), jnp.bfloat16),
            pltpu.VMEM((planes, LANES, 2, half, 3 * cols), jnp.bfloat16),
            pltpu.VMEM((planes, ntok, cols), jnp.bfloat16),
            pltpu.VMEM((nseq * ntok // BLOCK, BLOCK, 2 * cols), jnp.bfloat16),
            pltpu.VMEM((LANES, planes, extra, 2 * cols), jnp.bfloat16),
            pltpu.VMEM((planes, ntok, cols), jnp.bfloat16),
            dma((4,)),
            dma((steps, 3)),
            dma((steps, 3)),
            dma,
            dma,
            dma((3,)),
            dma((3,)),
            dma((2, planes)),
            dma((planes,)),
            dma((3, planes)),
            dma((3, planes)),
            dma((3,)),
            dma((3,)),
            dma((planes,)),
            dma((planes,)),
        ],
        compiler_params=pltpu.CompilerParams(
            collective_id=0, has_side_effects=True, vmem_limit_bytes=48 * 1024 * 1024
        ),
        cost_estimate=pl.CostEstimate(
            flops=2 * planes * slot_rows * width * 3 * cols,
            bytes_accessed=2 * planes * slot_rows * width,
            transcendentals=ntok * H * 400,
        ),
    )(tokens, w_query, w_keyval, global_off, rows)


def solution(mesh):
    in_specs = (
        P(("groups", "seq"), None),
        P("seq", None),
        P("seq", None),
        P(("groups", "seq")),
        P("groups", None, None),
        P("groups", None, None),
    )
    out_specs = P(("groups", "seq"), None)
    nseq, groups = mesh.shape["seq"], mesh.shape["groups"]
    planes = nseq // LANES
    whole_heads = groups == 2 and planes * LANES == nseq and H % planes == 0
    body = fused if whole_heads else local
    return jax.shard_map(body, mesh=mesh, in_specs=in_specs, out_specs=out_specs, check_vma=False)
```

```python
import functools

import jax
import jax.numpy as jnp
from jax import lax
from jax.experimental import pallas as pl
from jax.experimental.pallas import tpu as pltpu
from jax.sharding import PartitionSpec as P

H = 8
HD = 128
BLOCK = 64
R = 3
BLK_DEV = 4
LANES = 4
MESH = pl.DeviceIdType.MESH


def padded_2(block, sides, width):
    for axis, dim in sides:
        count = lax.axis_size(axis)
        forward = [(i, i + 1) for i in range(count - 1)]
        backward = [(target, source) for source, target in forward]
        low = lax.ppermute(
            lax.slice_in_dim(block, block.shape[dim] - width, None, axis=dim), axis, forward
        )
        high = lax.ppermute(lax.slice_in_dim(block, 0, width, axis=dim), axis, backward)
        block = jnp.concatenate([low, block, high], axis=dim)
    return block


def fold_rows(left, piece):
    return jnp.dot(left, piece, preferred_element_type=jnp.float32)


def local(tokens, w_query, w_keyval, global_off, rand_dev, rand_sub):
    ntok = tokens.shape[0]
    nseq = lax.axis_size("seq")
    me_index = lax.axis_index("seq")
    nblk = ntok // BLOCK
    inner = H * HD
    glob_rows = lax.all_gather(jnp.take(tokens, global_off, axis=0), "seq", axis=0, tiled=True)
    left_kv = jnp.concatenate([tokens, glob_rows], axis=0)
    query = fold_rows(tokens, lax.all_gather(w_query, "seq", axis=0, tiled=True))
    keyval = fold_rows(left_kv, lax.all_gather(w_keyval, "seq", axis=0, tiled=True))
    query = query.astype(jnp.bfloat16)
    keyval = keyval.astype(jnp.bfloat16)
    glob_kv = keyval[ntok:]
    keyval = keyval[:ntok]
    glob_kv = glob_kv.reshape(glob_kv.shape[0], 2, H, HD)
    padded = padded_2(keyval, (("seq", 0),), BLOCK)
    window = jnp.concatenate(
        [padded[j * BLOCK : j * BLOCK + ntok].reshape(nblk, BLOCK, 2, H, HD) for j in range(3)],
        axis=1,
    )
    capacity = max(2, 3 * BLK_DEV * H * R // (2 * nseq))
    nreq = nblk * H * R
    dev_all = rand_dev.reshape(nseq, nreq)
    sub_all = rand_sub.reshape(nseq, nreq)
    match = (dev_all == me_index).astype(jnp.int32)
    slot_all = jnp.cumsum(match, axis=1) - 1
    head_of = jnp.arange(nreq, dtype=jnp.int32) // R % H
    code_all = head_of[None, :] * nblk + sub_all
    picked = (match[:, None, :] == 1) & (
        slot_all[:, None, :] == jnp.arange(capacity, dtype=jnp.int32)[None, :, None]
    )
    source = jnp.sum(jnp.where(picked, code_all[:, None, :], 0), axis=2)
    tiles = (
        keyval.reshape(nblk, BLOCK, 2, H, HD)
        .transpose(3, 0, 1, 2, 4)
        .reshape(H * nblk, BLOCK, 2 * HD)
    )
    outgoing = jnp.take(tiles, source, axis=0)
    incoming = lax.all_to_all(outgoing, "seq", split_axis=0, concat_axis=0, tiled=True)
    my_dev = lax.dynamic_slice_in_dim(rand_dev, me_index * nblk, nblk, 0).reshape(nreq)
    onehot = (my_dev[:, None] == jnp.arange(nseq, dtype=jnp.int32)[None, :]).astype(jnp.int32)
    my_slot = jnp.sum(onehot * (jnp.cumsum(onehot, axis=0) - 1), axis=1)
    flat_index = my_dev * capacity + my_slot
    fetched = jnp.take(incoming.reshape(nseq * capacity, BLOCK, 2 * HD), flat_index, axis=0)
    fetched = fetched.reshape(nblk, H, R, BLOCK, 2, HD)
    scale = HD ** (-0.5)
    qry = query.reshape(nblk, BLOCK, H, HD)
    s_win = (
        jnp.einsum("bqhd,bkhd->bhqk", qry, window[:, :, 0], preferred_element_type=jnp.float32)
        * scale
    )
    s_rnd = (
        jnp.einsum(
            "bqhd,bhrkd->bhqrk", qry, fetched[:, :, :, :, 0], preferred_element_type=jnp.float32
        ).reshape(nblk, H, BLOCK, R * BLOCK)
        * scale
    )
    s_glb = (
        jnp.einsum("bqhd,ghd->bhqg", qry, glob_kv[:, 0], preferred_element_type=jnp.float32) * scale
    )
    blk_ids = me_index * nblk + jnp.arange(nblk, dtype=jnp.int32)
    left_ok = jnp.repeat((blk_ids > 0)[:, None], BLOCK, axis=1)
    right_ok = jnp.repeat((blk_ids < nseq * nblk - 1)[:, None], BLOCK, axis=1)
    middle_ok = jnp.ones((nblk, BLOCK), dtype=bool)
    window_ok = jnp.concatenate([left_ok, middle_ok, right_ok], axis=1)
    s_win = jnp.where(window_ok[:, None, None, :], s_win, -jnp.inf)
    scores = jnp.concatenate([s_win, s_rnd, s_glb], axis=3)
    highest = jnp.max(scores, axis=3, keepdims=True)
    expo = jnp.exp(scores - highest)
    weights = (expo / jnp.sum(expo, axis=3, keepdims=True)).astype(jnp.bfloat16)
    w_win = weights[..., : 3 * BLOCK]
    w_rnd = weights[..., 3 * BLOCK : 3 * BLOCK + R * BLOCK].reshape(nblk, H, BLOCK, R, BLOCK)
    w_glb = weights[..., 3 * BLOCK + R * BLOCK :]
    ctx = jnp.einsum("bhqk,bkhd->bqhd", w_win, window[:, :, 1], preferred_element_type=jnp.float32)
    ctx = ctx + jnp.einsum(
        "bhqrk,bhrkd->bqhd", w_rnd, fetched[:, :, :, :, 1], preferred_element_type=jnp.float32
    )
    ctx = ctx + jnp.einsum(
        "bhqg,ghd->bqhd", w_glb, glob_kv[:, 1], preferred_element_type=jnp.float32
    )
    return ctx.reshape(ntok, inner).astype(jnp.bfloat16)


def fused_kernel(
    planes, tok_hbm, wq_hbm, wkv_hbm, pick_hbm, blocks_hbm, out_ref,
    tok, wts, qry, kv, far_q, far_kv, picks, ctx, blocks_ref,
    local_sem, w_send, w_recv, g_send, g_recv, t_send, t_recv, f_send, f_recv,
    k_send, k_recv, p_send, p_recv, o_send, o_recv, c_send, c_recv,
):
    ntok = tok_hbm.shape[0]
    nblk = ntok // BLOCK
    heads = H // planes
    cols = heads * HD
    half = wts.shape[4]
    x = lax.axis_index("groups")
    me = lax.axis_index("seq")
    z = me // LANES
    lane = me % LANES
    core_lane = lane + 1 - 2 * (lane % 2)
    y_lane = (lane + 2) % LANES
    diag_lane = (core_lane + 2) % LANES
    mid = planes // 2
    workers, ends = (mid - 1, mid), (0, planes - 1)
    lower = z < mid
    own_worker = jnp.where(lower, workers[0], workers[1])
    own_end = jnp.where(lower, ends[0], ends[1])
    far_worker = jnp.where(lower, workers[1], workers[0])
    far_end = jnp.where(lower, ends[1], ends[0])
    mate = jnp.where(z == own_worker, own_end, own_worker)
    order = [own_worker, own_end, far_worker, far_end]

    def at(plane, where):
        return {"seq": plane * LANES + where}

    x_peer = {"groups": 1 - x}
    core_peer = at(z, core_lane)
    y_peer = at(z, y_lane)
    diag_peer = at(z, diag_lane)
    partners = ((y_lane, y_peer), (core_lane, core_peer), (diag_lane, diag_peer))

    def remote(src, dst, send, recv, peer):
        return pltpu.make_async_remote_copy(
            src_ref=src, dst_ref=dst, send_sem=send, recv_sem=recv, device_id=peer,
            device_id_type=MESH,
        )

    blocks_in = pltpu.make_async_copy(blocks_hbm, blocks_ref, local_sem.at[0])
    blocks_in.start()
    pick_in = pltpu.make_async_copy(pick_hbm, picks.at[lane, z], local_sem.at[1])
    pick_in.start()
    tok_in = pltpu.make_async_copy(tok_hbm, tok.at[z], local_sem.at[2])
    tok_in.start()

    barrier = pltpu.get_barrier_semaphore()
    for step in range(1, planes):
        pl.semaphore_signal(
            barrier, inc=1, device_id=at((z + step) % planes, lane), device_id_type=MESH
        )
    for peer in (x_peer, core_peer, y_peer, diag_peer):
        pl.semaphore_signal(barrier, inc=1, device_id=peer, device_id_type=MESH)
    pl.semaphore_wait(barrier, planes - 1 + 4)

    def weight_refs(index, kind, part):
        plane = (ends, workers)[kind][index]
        rows = pl.ds(pl.multiple_of(x * half, half), half)
        first = (0, 0, H * HD)[part] + plane * cols
        src = (wq_hbm, wkv_hbm, wkv_hbm)[part].at[rows, pl.ds(first, cols)]
        return src, wts.at[kind, z, lane, x, :, pl.ds(part * cols, cols)]

    def weight_remote(index, kind, part):
        src, dst = weight_refs(index, kind, part)
        return remote(
            src, dst, w_send.at[index, kind, part], w_recv.at[z, kind, part],
            at(workers[index], lane),
        )

    def weights_out(kind):
        for index in range(2):
            for part in range(3):
                @pl.when(z != workers[index])
                def _():
                    weight_remote(index, kind, part).start()

                @pl.when(z == workers[index])
                def _():
                    src, dst = weight_refs(index, kind, part)
                    pltpu.make_async_copy(src, dst, w_recv.at[z, kind, part]).start()

    def weights_in(kind):
        for plane in range(planes):
            for part in range(3):
                here = wts.at[kind, plane, lane, x, :, pl.ds(part * cols, cols)]
                remote(here, here, w_send.at[0, kind, part], w_recv.at[plane, kind, part], core_peer).wait_recv()

    towards = jnp.where(lower, z + 1, z - 1)
    own_out = remote(tok_hbm, tok.at[z], t_send.at[0], t_recv.at[z], at(towards, lane))
    pass_out = remote(
        tok.at[own_end], tok.at[own_end], t_send.at[1], t_recv.at[own_end], at(towards, lane)
    )

    def tok_wait(plane):
        remote(tok.at[plane], tok.at[plane], t_send.at[0], t_recv.at[plane], core_peer).wait_recv()

    weights_out(0)
    own_out.start()
    weights_out(1)
    pick_in.wait()

    def pick_copy(step):
        ref = picks.at[lane, z]
        return remote(ref, ref, p_send.at[step - 1], p_recv.at[z], at((z + step) % planes, lane))

    for step in range(1, planes):
        pick_copy(step).start()

    width = 3 * cols
    every, left, right = pl.ds(0, width), pl.ds(0, width // 2), pl.ds(width // 2, width // 2)
    moves = (
        (x, lane, every, x_peer, 1 - x, lane),
        (x, lane, every, y_peer, x, y_lane),
        (x, lane, every, core_peer, x, core_lane),
        (1 - x, lane, left, y_peer, 1 - x, y_lane),
        (1 - x, lane, every, core_peer, 1 - x, core_lane),
        (x, y_lane, right, x_peer, 1 - x, y_lane),
        (x, y_lane, every, core_peer, x, diag_lane),
        (1 - x, y_lane, left, core_peer, 1 - x, diag_lane),
        (1 - x, y_lane, right, core_peer, 1 - x, diag_lane),
    )

    def gather_out(kind, index):
        group, where, part, peer = moves[index][:4]
        ref = wts.at[kind, :, where, group, :, part]
        return remote(ref, ref, g_send.at[kind, index], g_recv.at[kind, index], peer)

    def gather_wait(kind, index):
        part, peer, group, where = moves[index][2:]
        ref = wts.at[kind, :, where, group, :, part]
        remote(ref, ref, g_send.at[kind, index], g_recv.at[kind, index], peer).wait_recv()

    def gather_first(kind):
        weights_in(kind)
        for index in range(3):
            gather_out(kind, index).start()

    def gather_second(kind):
        gather_wait(kind, 0)
        gather_out(kind, 3).start()
        gather_out(kind, 4).start()
        gather_wait(kind, 1)
        gather_out(kind, 5).start()
        gather_out(kind, 6).start()

    def gather_last(kind):
        gather_wait(kind, 3)
        gather_out(kind, 7).start()
        gather_wait(kind, 5)
        gather_out(kind, 8).start()
        for index in (2, 4, 6, 7, 8):
            gather_wait(kind, index)

    def kv_rows(ref, plane, where):
        return ref.at[pl.ds((plane * LANES + where) * nblk, nblk)]

    def kv_copy(index, which, where, peer):
        ref = kv_rows(kv, order[index], where)
        return remote(ref, ref, k_send.at[which, index], k_recv.at[which, index], peer)

    def kv_out(index):
        kv_copy(index, 0, lane, y_peer).start()
        kv_copy(index, 1, lane, core_peer).start()

    def kv_forward(index):
        kv_copy(index, 0, y_lane, y_peer).wait_recv()
        kv_copy(index, 2, y_lane, core_peer).start()

    def project(index, kind):
        weights = wts[kind].reshape(-1, width)
        res = jnp.dot(tok[order[index]], weights, preferred_element_type=jnp.float32)
        return res.astype(jnp.bfloat16)

    def far_copies(index):
        p = order[index]
        return (
            remote(far_q.at[index], qry.at[p], f_send.at[0, index], f_recv.at[0, index], at(mate, lane)),
            remote(
                far_kv.at[index], kv_rows(kv, p, lane), f_send.at[1, index], f_recv.at[1, index],
                at(mate, lane),
            ),
        )

    def project_far(index):
        res = project(index, 0)
        far_q[index] = res[:, :cols]
        far_kv[index] = res[:, cols:].reshape(nblk, BLOCK, 2 * cols)
        for copy in far_copies(index):
            copy.start()

    def project_own(index):
        res = project(index, 1)
        qry[order[index]] = res[:, :cols]
        kv_rows(kv, order[index], lane)[...] = res[:, cols:].reshape(nblk, BLOCK, 2 * cols)
        kv_out(index)

    @pl.when(z == own_worker)
    def _():
        gather_first(0)
        tok_in.wait()
        tok_wait(own_end)
        pass_out.start()
        gather_second(0)
        gather_first(1)
        gather_last(0)
        project_far(0)
        project_far(1)
        gather_second(1)
        tok_wait(far_worker)
        project_far(2)
        gather_last(1)
        project_own(0)
        project_own(1)
        kv_forward(0)
        project_own(2)
        kv_forward(1)
        tok_wait(far_end)
        project_far(3)
        project_own(3)
        kv_forward(2)
        kv_forward(3)

    @pl.when(z != own_worker)
    def _():
        tok_in.wait()
        for index in range(planes):
            here_q, here_kv = qry.at[order[index]], kv_rows(kv, order[index], lane)
            remote(here_kv, here_kv, f_send.at[1, index], f_recv.at[1, index], core_peer).wait_recv()
            kv_out(index)
            remote(here_q, here_q, f_send.at[0, index], f_recv.at[0, index], core_peer).wait_recv()
            if index:
                kv_forward(index - 1)
        kv_forward(planes - 1)

    for step in range(1, planes):
        source = (z + step) % planes
        ref = picks.at[lane, source]
        remote(ref, ref, p_send.at[0], p_recv.at[source], core_peer).wait_recv()

    def pick_lane(index, where, peer):
        return remote(picks.at[where], picks.at[where], o_send.at[index], o_recv.at[index], peer)

    for index, (where, peer) in enumerate(partners):
        pick_lane(index, lane, peer).start()
    for index, (where, peer) in enumerate(partners):
        pick_lane(index, where, peer).wait_recv()
    glob = jnp.zeros((picks.shape[2], 2 * cols), jnp.float32)
    for index in range(planes):
        kv_copy(index, 1, core_lane, core_peer).wait_recv()
        kv_copy(index, 2, diag_lane, core_peer).wait_recv()
    for plane in range(planes):
        for where in range(LANES):
            rows = kv_rows(kv, plane, where)[...].reshape(ntok, 2 * cols)
            glob = glob + jnp.dot(picks[where, plane], rows, preferred_element_type=jnp.float32)
    glob = glob[: planes * LANES].astype(jnp.bfloat16)
    blocks_in.wait()
    total_blocks = planes * LANES * nblk
    scale = HD ** (-0.5)
    keys = (3 + R) * BLOCK + glob.shape[0]
    column = lax.broadcasted_iota(jnp.int32, (BLOCK, keys), 1)

    def ctx_copy(plane, index):
        return remote(
            ctx.at[plane],
            out_ref.at[:, pl.ds(pl.multiple_of(z * cols, cols), cols)],
            c_send.at[index], c_recv.at[z], at(plane, lane),
        )

    def attend(plane):
        for sub in range(nblk):
            block = (plane * LANES + lane) * nblk + sub
            starts = [
                jnp.maximum(block - 1, 0),
                block,
                jnp.minimum(block + 1, total_blocks - 1),
            ]
            hidden = ((column < BLOCK) & (block == 0)) | (
                (column >= 2 * BLOCK) & (column < 3 * BLOCK) & (block == total_blocks - 1)
            )
            q_rows = slice(sub * BLOCK, (sub + 1) * BLOCK)
            for h in range(heads):
                base = (block * H + z * heads + h) * R
                where = starts + [blocks_ref[base + j] for j in range(R)]
                k_cols = slice(h * HD, (h + 1) * HD)
                v_cols = slice(cols + h * HD, cols + (h + 1) * HD)
                key = jnp.concatenate(
                    [kv[w, :, k_cols] for w in where] + [glob[:, k_cols]], axis=0
                )
                val = jnp.concatenate(
                    [kv[w, :, v_cols] for w in where] + [glob[:, v_cols]], axis=0
                )
                score = lax.dot_general(
                    qry[plane, q_rows, k_cols], key, (((1,), (1,)), ((), ())),
                    preferred_element_type=jnp.float32,
                ) * scale
                score = jnp.where(hidden, -jnp.inf, score)
                expo = jnp.exp(score - jnp.max(score, axis=1, keepdims=True))
                soft = (expo / jnp.sum(expo, axis=1, keepdims=True)).astype(jnp.bfloat16)
                ctx[plane, q_rows, k_cols] = jnp.dot(
                    soft, val, preferred_element_type=jnp.float32
                ).astype(jnp.bfloat16)

    others = (far_end, far_worker, mate)
    for index, plane in enumerate(others):
        attend(plane)
        ctx_copy(plane, index).start()
    attend(z)
    own = pltpu.make_async_copy(
        ctx.at[z], out_ref.at[:, pl.ds(pl.multiple_of(z * cols, cols), cols)], local_sem.at[0]
    )
    own.start()
    own.wait()

    for index, plane in enumerate(others):
        ctx_copy(plane, index).wait_send()
        there = out_ref.at[:, pl.ds(pl.multiple_of(plane * cols, cols), cols)]
        remote(ctx.at[plane], there, c_send.at[index], c_recv.at[plane], core_peer).wait_recv()
    for index in range(2):
        @pl.when(z != workers[index])
        def _():
            for kind in range(2):
                for part in range(3):
                    weight_remote(index, kind, part).wait_send()
    own_out.wait_send()

    @pl.when(z == own_worker)
    def _():
        pass_out.wait_send()
        for kind in range(2):
            for index in range(len(moves)):
                gather_out(kind, index).wait_send()
        for index in range(planes):
            for copy in far_copies(index):
                copy.wait_send()

    for index in range(planes):
        kv_copy(index, 0, lane, y_peer).wait_send()
        kv_copy(index, 1, lane, core_peer).wait_send()
        kv_copy(index, 2, y_lane, core_peer).wait_send()
    for step in range(1, planes):
        pick_copy(step).wait_send()
    for index, (where, peer) in enumerate(partners):
        pick_lane(index, lane, peer).wait_send()


def fused(tokens, w_query, w_keyval, global_off, rand_dev, rand_sub):
    nseq = lax.axis_size("seq")
    ntok, width = tokens.shape
    planes = nseq // LANES
    nblk = ntok // BLOCK
    picked = -(-nseq // 16) * 16
    cols = H // planes * HD
    half = w_query.shape[0] // 2
    blocks = (rand_dev * nblk + rand_sub).reshape(-1)
    shape = (picked, ntok)
    at_row = lax.broadcasted_iota(jnp.int32, shape, 0) == lax.axis_index("seq")
    at_event = lax.broadcasted_iota(jnp.int32, shape, 1) == global_off[0]
    pick = jnp.where(at_row & at_event, 1.0, 0.0).astype(jnp.bfloat16)
    dma = pltpu.SemaphoreType.DMA
    return pl.pallas_call(
        functools.partial(fused_kernel, planes),
        out_shape=jax.ShapeDtypeStruct((ntok, H * HD), jnp.bfloat16),
        in_specs=[pl.BlockSpec(memory_space=pl.ANY)] * 5,
        out_specs=pl.BlockSpec(memory_space=pl.ANY),
        scratch_shapes=[
            pltpu.VMEM((planes, ntok, width), jnp.bfloat16),
            pltpu.VMEM((2, planes, LANES, 2, half, 3 * cols), jnp.bfloat16),
            pltpu.VMEM((planes, ntok, cols), jnp.bfloat16),
            pltpu.VMEM((nseq * nblk, BLOCK, 2 * cols), jnp.bfloat16),
            pltpu.VMEM((planes, ntok, cols), jnp.bfloat16),
            pltpu.VMEM((planes, nblk, BLOCK, 2 * cols), jnp.bfloat16),
            pltpu.VMEM((LANES, planes, picked, ntok), jnp.bfloat16),
            pltpu.VMEM((planes, ntok, cols), jnp.bfloat16),
            pltpu.SMEM(blocks.shape, jnp.int32),
            dma((3,)),
            dma((2, 2, 3)),
            dma((planes, 2, 3)),
            dma((2, 9)),
            dma((2, 9)),
            dma((2,)),
            dma((planes,)),
            dma((2, planes)),
            dma((2, planes)),
            dma((3, planes)),
            dma((3, planes)),
            dma((planes - 1,)),
            dma((planes,)),
            dma((3,)),
            dma((3,)),
            dma((planes - 1,)),
            dma((planes,)),
        ],
        compiler_params=pltpu.CompilerParams(
            collective_id=0, has_side_effects=True, vmem_limit_bytes=48 * 1024 * 1024
        ),
        cost_estimate=pl.CostEstimate(
            flops=2 * planes * ntok * width * 3 * cols,
            bytes_accessed=2 * planes * ntok * width,
            transcendentals=ntok * H * 400,
        ),
    )(tokens, w_query, w_keyval, pick, blocks)


def solution(mesh):
    in_specs = (
        P(("groups", "seq"), None),
        P("seq", None),
        P("seq", None),
        P(("groups", "seq")),
        P("groups", None, None),
        P("groups", None, None),
    )
    out_specs = P(("groups", "seq"), None)
    nseq, groups = mesh.shape["seq"], mesh.shape["groups"]
    planes = nseq // LANES
    paired = groups == 2 and planes * LANES == nseq and planes == 4
    body = fused if paired else local
    return jax.shard_map(body, mesh=mesh, in_specs=in_specs, out_specs=out_specs, check_vma=False)
```

```python
import functools

import jax
import jax.numpy as jnp
from jax import lax
from jax.experimental import pallas as pl
from jax.experimental.pallas import tpu as pltpu
from jax.sharding import PartitionSpec as P

H = 8
HD = 128
BLOCK = 64
R = 3
BLK_DEV = 4
LANES = 4
MESH = pl.DeviceIdType.MESH


def padded_2(block, sides, width):
    for axis, dim in sides:
        count = lax.axis_size(axis)
        forward = [(i, i + 1) for i in range(count - 1)]
        backward = [(target, source) for source, target in forward]
        low = lax.ppermute(
            lax.slice_in_dim(block, block.shape[dim] - width, None, axis=dim), axis, forward
        )
        high = lax.ppermute(lax.slice_in_dim(block, 0, width, axis=dim), axis, backward)
        block = jnp.concatenate([low, block, high], axis=dim)
    return block


def fold_rows(left, piece):
    return jnp.dot(left, piece, preferred_element_type=jnp.float32)


def local(tokens, w_query, w_keyval, global_off, rand_dev, rand_sub):
    ntok = tokens.shape[0]
    nseq = lax.axis_size("seq")
    me_index = lax.axis_index("seq")
    nblk = ntok // BLOCK
    inner = H * HD
    glob_rows = lax.all_gather(jnp.take(tokens, global_off, axis=0), "seq", axis=0, tiled=True)
    left_kv = jnp.concatenate([tokens, glob_rows], axis=0)
    query = fold_rows(tokens, lax.all_gather(w_query, "seq", axis=0, tiled=True))
    keyval = fold_rows(left_kv, lax.all_gather(w_keyval, "seq", axis=0, tiled=True))
    query = query.astype(jnp.bfloat16)
    keyval = keyval.astype(jnp.bfloat16)
    glob_kv = keyval[ntok:]
    keyval = keyval[:ntok]
    glob_kv = glob_kv.reshape(glob_kv.shape[0], 2, H, HD)
    padded = padded_2(keyval, (("seq", 0),), BLOCK)
    window = jnp.concatenate(
        [padded[j * BLOCK : j * BLOCK + ntok].reshape(nblk, BLOCK, 2, H, HD) for j in range(3)],
        axis=1,
    )
    capacity = max(2, 3 * BLK_DEV * H * R // (2 * nseq))
    nreq = nblk * H * R
    dev_all = rand_dev.reshape(nseq, nreq)
    sub_all = rand_sub.reshape(nseq, nreq)
    match = (dev_all == me_index).astype(jnp.int32)
    slot_all = jnp.cumsum(match, axis=1) - 1
    head_of = jnp.arange(nreq, dtype=jnp.int32) // R % H
    code_all = head_of[None, :] * nblk + sub_all
    picked = (match[:, None, :] == 1) & (
        slot_all[:, None, :] == jnp.arange(capacity, dtype=jnp.int32)[None, :, None]
    )
    source = jnp.sum(jnp.where(picked, code_all[:, None, :], 0), axis=2)
    tiles = (
        keyval.reshape(nblk, BLOCK, 2, H, HD)
        .transpose(3, 0, 1, 2, 4)
        .reshape(H * nblk, BLOCK, 2 * HD)
    )
    outgoing = jnp.take(tiles, source, axis=0)
    incoming = lax.all_to_all(outgoing, "seq", split_axis=0, concat_axis=0, tiled=True)
    my_dev = lax.dynamic_slice_in_dim(rand_dev, me_index * nblk, nblk, 0).reshape(nreq)
    onehot = (my_dev[:, None] == jnp.arange(nseq, dtype=jnp.int32)[None, :]).astype(jnp.int32)
    my_slot = jnp.sum(onehot * (jnp.cumsum(onehot, axis=0) - 1), axis=1)
    flat_index = my_dev * capacity + my_slot
    fetched = jnp.take(incoming.reshape(nseq * capacity, BLOCK, 2 * HD), flat_index, axis=0)
    fetched = fetched.reshape(nblk, H, R, BLOCK, 2, HD)
    scale = HD ** (-0.5)
    qry = query.reshape(nblk, BLOCK, H, HD)
    s_win = (
        jnp.einsum("bqhd,bkhd->bhqk", qry, window[:, :, 0], preferred_element_type=jnp.float32)
        * scale
    )
    s_rnd = (
        jnp.einsum(
            "bqhd,bhrkd->bhqrk", qry, fetched[:, :, :, :, 0], preferred_element_type=jnp.float32
        ).reshape(nblk, H, BLOCK, R * BLOCK)
        * scale
    )
    s_glb = (
        jnp.einsum("bqhd,ghd->bhqg", qry, glob_kv[:, 0], preferred_element_type=jnp.float32) * scale
    )
    blk_ids = me_index * nblk + jnp.arange(nblk, dtype=jnp.int32)
    left_ok = jnp.repeat((blk_ids > 0)[:, None], BLOCK, axis=1)
    right_ok = jnp.repeat((blk_ids < nseq * nblk - 1)[:, None], BLOCK, axis=1)
    middle_ok = jnp.ones((nblk, BLOCK), dtype=bool)
    window_ok = jnp.concatenate([left_ok, middle_ok, right_ok], axis=1)
    s_win = jnp.where(window_ok[:, None, None, :], s_win, -jnp.inf)
    scores = jnp.concatenate([s_win, s_rnd, s_glb], axis=3)
    highest = jnp.max(scores, axis=3, keepdims=True)
    expo = jnp.exp(scores - highest)
    weights = (expo / jnp.sum(expo, axis=3, keepdims=True)).astype(jnp.bfloat16)
    w_win = weights[..., : 3 * BLOCK]
    w_rnd = weights[..., 3 * BLOCK : 3 * BLOCK + R * BLOCK].reshape(nblk, H, BLOCK, R, BLOCK)
    w_glb = weights[..., 3 * BLOCK + R * BLOCK :]
    ctx = jnp.einsum("bhqk,bkhd->bqhd", w_win, window[:, :, 1], preferred_element_type=jnp.float32)
    ctx = ctx + jnp.einsum(
        "bhqrk,bhrkd->bqhd", w_rnd, fetched[:, :, :, :, 1], preferred_element_type=jnp.float32
    )
    ctx = ctx + jnp.einsum(
        "bhqg,ghd->bqhd", w_glb, glob_kv[:, 1], preferred_element_type=jnp.float32
    )
    return ctx.reshape(ntok, inner).astype(jnp.bfloat16)


def fused_kernel(
    planes, tok_hbm, wq_hbm, wkv_hbm, pick_hbm, dev_hbm, sub_hbm, out_ref,
    tok, wts, qry, kv, far_q, far_kv, picks, ctx, dev_ref, sub_ref,
    local_sem, w_send, w_recv, g_send, g_recv, t_send, t_recv, f_send, f_recv,
    k_send, k_recv, p_send, p_recv, o_send, o_recv, c_send, c_recv,
):
    ntok = tok_hbm.shape[0]
    nblk = ntok // BLOCK
    heads = H // planes
    cols = heads * HD
    half = wts.shape[4]
    x = lax.axis_index("groups")
    me = lax.axis_index("seq")
    z = me // LANES
    lane = me % LANES
    core_lane = lane + 1 - 2 * (lane % 2)
    y_lane = (lane + 2) % LANES
    diag_lane = (core_lane + 2) % LANES
    mid = planes // 2
    workers, ends = (mid - 1, mid), (0, planes - 1)
    lower = z < mid
    own_worker = jnp.where(lower, workers[0], workers[1])
    own_end = jnp.where(lower, ends[0], ends[1])
    far_worker = jnp.where(lower, workers[1], workers[0])
    far_end = jnp.where(lower, ends[1], ends[0])
    mate = jnp.where(z == own_worker, own_end, own_worker)
    order = [own_worker, own_end, far_worker, far_end]

    def at(plane, where):
        return {"seq": plane * LANES + where}

    x_peer = {"groups": 1 - x}
    core_peer = at(z, core_lane)
    y_peer = at(z, y_lane)
    diag_peer = at(z, diag_lane)
    partners = ((y_lane, y_peer), (core_lane, core_peer), (diag_lane, diag_peer))

    def remote(src, dst, send, recv, peer):
        return pltpu.make_async_remote_copy(
            src_ref=src, dst_ref=dst, send_sem=send, recv_sem=recv, device_id=peer,
            device_id_type=MESH,
        )

    dev_in = pltpu.make_async_copy(dev_hbm, dev_ref, local_sem.at[0])
    dev_in.start()
    sub_in = pltpu.make_async_copy(sub_hbm, sub_ref, local_sem.at[3])
    sub_in.start()
    pick_in = pltpu.make_async_copy(pick_hbm, picks.at[lane, z], local_sem.at[1])
    pick_in.start()
    tok_in = pltpu.make_async_copy(tok_hbm, tok.at[z], local_sem.at[2])
    tok_in.start()

    barrier = pltpu.get_barrier_semaphore()
    for step in range(1, planes):
        pl.semaphore_signal(
            barrier, inc=1, device_id=at((z + step) % planes, lane), device_id_type=MESH
        )
    for peer in (x_peer, core_peer, y_peer, diag_peer):
        pl.semaphore_signal(barrier, inc=1, device_id=peer, device_id_type=MESH)
    pl.semaphore_wait(barrier, planes - 1 + 4)

    def weight_refs(index, kind, part):
        plane = (ends, workers)[kind][index]
        rows = pl.ds(pl.multiple_of(x * half, half), half)
        first = (0, 0, H * HD)[part] + plane * cols
        src = (wq_hbm, wkv_hbm, wkv_hbm)[part].at[rows, pl.ds(first, cols)]
        return src, wts.at[kind, z, lane, x, :, pl.ds(part * cols, cols)]

    def weight_remote(index, kind, part):
        src, dst = weight_refs(index, kind, part)
        return remote(
            src, dst, w_send.at[index, kind, part], w_recv.at[z, kind, part],
            at(workers[index], lane),
        )

    def weights_out(kind):
        for index in range(2):
            for part in range(3):
                @pl.when(z != workers[index])
                def _():
                    weight_remote(index, kind, part).start()

                @pl.when(z == workers[index])
                def _():
                    src, dst = weight_refs(index, kind, part)
                    pltpu.make_async_copy(src, dst, w_recv.at[z, kind, part]).start()

    def weights_in(kind):
        for plane in range(planes):
            for part in range(3):
                here = wts.at[kind, plane, lane, x, :, pl.ds(part * cols, cols)]
                remote(here, here, w_send.at[0, kind, part], w_recv.at[plane, kind, part], core_peer).wait_recv()

    towards = jnp.where(lower, z + 1, z - 1)
    chunk = ntok // 2
    chunks = (pl.ds(0, chunk), pl.ds(chunk, chunk))

    def own_out(c):
        return remote(
            tok_hbm.at[chunks[c]], tok.at[z, chunks[c]], t_send.at[0, c], t_recv.at[z, c],
            at(towards, lane),
        )

    def pass_out(c):
        ref = tok.at[own_end, chunks[c]]
        return remote(ref, ref, t_send.at[1, c], t_recv.at[own_end, c], at(towards, lane))

    def tok_wait(plane, c):
        ref = tok.at[plane, chunks[c]]
        remote(ref, ref, t_send.at[0, c], t_recv.at[plane, c], core_peer).wait_recv()

    weights_out(0)
    weights_out(1)
    own_out(0).start()
    own_out(1).start()
    pick_in.wait()

    def pick_copy(step):
        ref = picks.at[lane, z]
        return remote(ref, ref, p_send.at[step - 1], p_recv.at[z], at((z + step) % planes, lane))

    for step in range(1, planes):
        pick_copy(step).start()

    width = 3 * cols
    every, left, right = pl.ds(0, width), pl.ds(0, width // 2), pl.ds(width // 2, width // 2)
    moves = (
        (x, lane, every, x_peer, 1 - x, lane),
        (x, lane, every, y_peer, x, y_lane),
        (x, lane, every, core_peer, x, core_lane),
        (1 - x, lane, left, y_peer, 1 - x, y_lane),
        (1 - x, lane, every, core_peer, 1 - x, core_lane),
        (x, y_lane, right, x_peer, 1 - x, y_lane),
        (x, y_lane, every, core_peer, x, diag_lane),
        (1 - x, y_lane, left, core_peer, 1 - x, diag_lane),
        (1 - x, y_lane, right, core_peer, 1 - x, diag_lane),
    )

    def gather_out(kind, index):
        group, where, part, peer = moves[index][:4]
        ref = wts.at[kind, :, where, group, :, part]
        return remote(ref, ref, g_send.at[kind, index], g_recv.at[kind, index], peer)

    def gather_wait(kind, index):
        part, peer, group, where = moves[index][2:]
        ref = wts.at[kind, :, where, group, :, part]
        remote(ref, ref, g_send.at[kind, index], g_recv.at[kind, index], peer).wait_recv()

    def gather_first(kind):
        weights_in(kind)
        for index in range(3):
            gather_out(kind, index).start()

    def gather_second(kind):
        gather_wait(kind, 0)
        gather_out(kind, 3).start()
        gather_out(kind, 4).start()
        gather_wait(kind, 1)
        gather_out(kind, 5).start()
        gather_out(kind, 6).start()

    def gather_last(kind):
        gather_wait(kind, 3)
        gather_out(kind, 7).start()
        gather_wait(kind, 5)
        gather_out(kind, 8).start()
        for index in (2, 4, 6, 7, 8):
            gather_wait(kind, index)

    def kv_rows(ref, plane, where, first=0, count=nblk):
        return ref.at[pl.ds((plane * LANES + where) * nblk + first, count)]

    units = [(i, 0, ntok) for i in range(planes - 1)]
    units += [(planes - 1, 0, chunk), (planes - 1, chunk, chunk)]

    def unit_kv(unit, where):
        index, first, count = units[unit]
        return kv_rows(kv, order[index], where, first // BLOCK, count // BLOCK)

    def unit_q(unit):
        index, first, count = units[unit]
        return qry.at[order[index], pl.ds(first, count)]

    def kv_copy(unit, which, where, peer):
        ref = unit_kv(unit, where)
        return remote(ref, ref, k_send.at[which, unit], k_recv.at[which, unit], peer)

    def kv_out(unit):
        kv_copy(unit, 0, lane, y_peer).start()
        kv_copy(unit, 1, lane, core_peer).start()

    def kv_forward(unit):
        kv_copy(unit, 0, y_lane, y_peer).wait_recv()
        kv_copy(unit, 2, y_lane, core_peer).start()

    def project(unit, kind):
        index, first, count = units[unit]
        weights = wts[kind].reshape(-1, width)
        rows = tok[order[index], pl.ds(first, count)]
        res = jnp.dot(rows, weights, preferred_element_type=jnp.float32).astype(jnp.bfloat16)
        return res[:, :cols], res[:, cols:].reshape(count // BLOCK, BLOCK, 2 * cols)

    def far_refs(unit):
        index, first, count = units[unit]
        blocks = pl.ds(index * nblk + first // BLOCK, count // BLOCK)
        return far_q.at[index, pl.ds(first, count)], far_kv.at[blocks]

    def far_copies(unit):
        from_q, from_kv = far_refs(unit)
        return (
            remote(from_kv, unit_kv(unit, lane), f_send.at[1, unit], f_recv.at[1, unit], at(mate, lane)),
            remote(from_q, unit_q(unit), f_send.at[0, unit], f_recv.at[0, unit], at(mate, lane)),
        )

    def project_far(unit):
        from_q, from_kv = far_refs(unit)
        from_q[...], from_kv[...] = project(unit, 0)
        for copy in far_copies(unit):
            copy.start()

    def project_own(unit):
        unit_q(unit)[...], unit_kv(unit, lane)[...] = project(unit, 1)
        kv_out(unit)

    @pl.when(z == own_worker)
    def _():
        gather_first(0)
        gather_second(0)
        tok_in.wait()
        tok_wait(own_end, 0)
        pass_out(0).start()
        gather_first(1)
        gather_last(0)
        project_far(0)
        tok_wait(own_end, 1)
        pass_out(1).start()
        project_far(1)
        gather_second(1)
        tok_wait(far_worker, 0)
        tok_wait(far_worker, 1)
        project_far(2)
        gather_last(1)
        project_own(0)
        project_own(1)
        kv_forward(0)
        project_own(2)
        kv_forward(1)
        tok_wait(far_end, 0)
        project_far(3)
        project_own(3)
        kv_forward(2)
        tok_wait(far_end, 1)
        project_far(4)
        project_own(4)
        kv_forward(3)
        kv_forward(4)

    @pl.when(z != own_worker)
    def _():
        tok_in.wait()
        for unit in range(len(units)):
            here = unit_kv(unit, lane)
            remote(here, here, f_send.at[1, unit], f_recv.at[1, unit], core_peer).wait_recv()
            kv_out(unit)
            if unit:
                kv_forward(unit - 1)
        kv_forward(len(units) - 1)
        for unit in range(len(units)):
            here = unit_q(unit)
            remote(here, here, f_send.at[0, unit], f_recv.at[0, unit], core_peer).wait_recv()

    for step in range(1, planes):
        source = (z + step) % planes
        ref = picks.at[lane, source]
        remote(ref, ref, p_send.at[0], p_recv.at[source], core_peer).wait_recv()

    def pick_lane(index, where, peer):
        return remote(picks.at[where], picks.at[where], o_send.at[index], o_recv.at[index], peer)

    for index, (where, peer) in enumerate(partners):
        pick_lane(index, lane, peer).start()
    for index, (where, peer) in enumerate(partners):
        pick_lane(index, where, peer).wait_recv()
    glob = jnp.zeros((picks.shape[2], 2 * cols), jnp.float32)
    for unit in range(len(units)):
        kv_copy(unit, 1, core_lane, core_peer).wait_recv()
        kv_copy(unit, 2, diag_lane, core_peer).wait_recv()
    for plane in range(planes):
        for where in range(LANES):
            rows = kv_rows(kv, plane, where)[...].reshape(ntok, 2 * cols)
            glob = glob + jnp.dot(picks[where, plane], rows, preferred_element_type=jnp.float32)
    glob = glob[: planes * LANES].astype(jnp.bfloat16)
    dev_in.wait()
    sub_in.wait()
    total_blocks = planes * LANES * nblk
    scale = HD ** (-0.5)
    keys = (3 + R) * BLOCK + glob.shape[0]
    column = lax.broadcasted_iota(jnp.int32, (BLOCK, keys), 1)

    def ctx_copy(plane, index):
        return remote(
            ctx.at[plane],
            out_ref.at[:, pl.ds(pl.multiple_of(z * cols, cols), cols)],
            c_send.at[index], c_recv.at[z], at(plane, lane),
        )

    def attend(plane):
        for sub in range(nblk):
            block = (plane * LANES + lane) * nblk + sub
            starts = [
                jnp.maximum(block - 1, 0),
                block,
                jnp.minimum(block + 1, total_blocks - 1),
            ]
            q_rows = slice(sub * BLOCK, (sub + 1) * BLOCK)
            for h in range(heads):
                head = z * heads + h
                where = starts + [
                    dev_ref[j, head, block] * nblk + sub_ref[j, head, block] for j in range(R)
                ]
                k_cols = slice(h * HD, (h + 1) * HD)
                v_cols = slice(cols + h * HD, cols + (h + 1) * HD)
                key = jnp.concatenate(
                    [kv[w, :, k_cols] for w in where] + [glob[:, k_cols]], axis=0
                )
                val = jnp.concatenate(
                    [kv[w, :, v_cols] for w in where] + [glob[:, v_cols]], axis=0
                )
                score = lax.dot_general(
                    qry[plane, q_rows, k_cols], key, (((1,), (1,)), ((), ())),
                    preferred_element_type=jnp.float32,
                ) * scale
                if sub == 0:
                    score = jnp.where((column < BLOCK) & (block == 0), -jnp.inf, score)
                if sub == nblk - 1:
                    after = (column >= 2 * BLOCK) & (column < 3 * BLOCK)
                    score = jnp.where(after & (block == total_blocks - 1), -jnp.inf, score)
                expo = jnp.exp(score - jnp.max(score, axis=1, keepdims=True))
                soft = (expo * (1.0 / jnp.sum(expo, axis=1, keepdims=True))).astype(jnp.bfloat16)
                ctx[plane, q_rows, k_cols] = jnp.dot(
                    soft, val, preferred_element_type=jnp.float32
                ).astype(jnp.bfloat16)

    others = (far_end, far_worker, mate)
    for index, plane in enumerate(others):
        attend(plane)
        ctx_copy(plane, index).start()
    attend(z)
    own = pltpu.make_async_copy(
        ctx.at[z], out_ref.at[:, pl.ds(pl.multiple_of(z * cols, cols), cols)], local_sem.at[0]
    )
    own.start()
    own.wait()

    for index, plane in enumerate(others):
        ctx_copy(plane, index).wait_send()
        there = out_ref.at[:, pl.ds(pl.multiple_of(plane * cols, cols), cols)]
        remote(ctx.at[plane], there, c_send.at[index], c_recv.at[plane], core_peer).wait_recv()
    for index in range(2):
        @pl.when(z != workers[index])
        def _():
            for kind in range(2):
                for part in range(3):
                    weight_remote(index, kind, part).wait_send()
    for c in range(2):
        own_out(c).wait_send()

    @pl.when(z == own_worker)
    def _():
        for c in range(2):
            pass_out(c).wait_send()
        for kind in range(2):
            for index in range(len(moves)):
                gather_out(kind, index).wait_send()
        for unit in range(len(units)):
            for copy in far_copies(unit):
                copy.wait_send()

    for unit in range(len(units)):
        kv_copy(unit, 0, lane, y_peer).wait_send()
        kv_copy(unit, 1, lane, core_peer).wait_send()
        kv_copy(unit, 2, y_lane, core_peer).wait_send()
    for step in range(1, planes):
        pick_copy(step).wait_send()
    for index, (where, peer) in enumerate(partners):
        pick_lane(index, lane, peer).wait_send()


def fused(tokens, w_query, w_keyval, global_off, rand_dev, rand_sub):
    nseq = lax.axis_size("seq")
    ntok, width = tokens.shape
    planes = nseq // LANES
    nblk = ntok // BLOCK
    picked = -(-nseq // 16) * 16
    cols = H // planes * HD
    half = w_query.shape[0] // 2
    dev, sub = rand_dev.transpose(2, 1, 0), rand_sub.transpose(2, 1, 0)
    shape = (picked, ntok)
    at_row = lax.broadcasted_iota(jnp.int32, shape, 0) == lax.axis_index("seq")
    at_event = lax.broadcasted_iota(jnp.int32, shape, 1) == global_off[0]
    pick = jnp.where(at_row & at_event, 1.0, 0.0).astype(jnp.bfloat16)
    dma = pltpu.SemaphoreType.DMA
    return pl.pallas_call(
        functools.partial(fused_kernel, planes),
        out_shape=jax.ShapeDtypeStruct((ntok, H * HD), jnp.bfloat16),
        in_specs=[pl.BlockSpec(memory_space=pl.ANY)] * 6,
        out_specs=pl.BlockSpec(memory_space=pl.ANY),
        scratch_shapes=[
            pltpu.VMEM((planes, ntok, width), jnp.bfloat16),
            pltpu.VMEM((2, planes, LANES, 2, half, 3 * cols), jnp.bfloat16),
            pltpu.VMEM((planes, ntok, cols), jnp.bfloat16),
            pltpu.VMEM((nseq * nblk, BLOCK, 2 * cols), jnp.bfloat16),
            pltpu.VMEM((planes, ntok, cols), jnp.bfloat16),
            pltpu.VMEM((planes * nblk, BLOCK, 2 * cols), jnp.bfloat16),
            pltpu.VMEM((LANES, planes, picked, ntok), jnp.bfloat16),
            pltpu.VMEM((planes, ntok, cols), jnp.bfloat16),
            pltpu.SMEM(dev.shape, jnp.int32),
            pltpu.SMEM(sub.shape, jnp.int32),
            dma((4,)),
            dma((2, 2, 3)),
            dma((planes, 2, 3)),
            dma((2, 9)),
            dma((2, 9)),
            dma((2, 2)),
            dma((planes, 2)),
            dma((2, planes + 1)),
            dma((2, planes + 1)),
            dma((3, planes + 1)),
            dma((3, planes + 1)),
            dma((planes - 1,)),
            dma((planes,)),
            dma((3,)),
            dma((3,)),
            dma((planes - 1,)),
            dma((planes,)),
        ],
        compiler_params=pltpu.CompilerParams(
            collective_id=0, has_side_effects=True, vmem_limit_bytes=60 * 1024 * 1024
        ),
        cost_estimate=pl.CostEstimate(
            flops=2 * planes * ntok * width * 3 * cols,
            bytes_accessed=2 * planes * ntok * width,
            transcendentals=ntok * H * 400,
        ),
    )(tokens, w_query, w_keyval, pick, dev, sub)


def solution(mesh):
    in_specs = (
        P(("groups", "seq"), None),
        P("seq", None),
        P("seq", None),
        P(("groups", "seq")),
        P("groups", None, None),
        P("groups", None, None),
    )
    out_specs = P(("groups", "seq"), None)
    nseq, groups = mesh.shape["seq"], mesh.shape["groups"]
    planes = nseq // LANES
    paired = groups == 2 and planes * LANES == nseq and planes == 4
    body = fused if paired else local
    return jax.shard_map(body, mesh=mesh, in_specs=in_specs, out_specs=out_specs, check_vma=False)
```

```python
import functools

import jax
import jax.numpy as jnp
from jax import lax
from jax.experimental import pallas as pl
from jax.experimental.pallas import tpu as pltpu
from jax.sharding import PartitionSpec as P

H = 8
HD = 128
BLOCK = 64
R = 3
BLK_DEV = 4
LANES = 4
MESH = pl.DeviceIdType.MESH


def padded_2(block, sides, width):
    for axis, dim in sides:
        count = lax.axis_size(axis)
        forward = [(i, i + 1) for i in range(count - 1)]
        backward = [(target, source) for source, target in forward]
        low = lax.ppermute(
            lax.slice_in_dim(block, block.shape[dim] - width, None, axis=dim), axis, forward
        )
        high = lax.ppermute(lax.slice_in_dim(block, 0, width, axis=dim), axis, backward)
        block = jnp.concatenate([low, block, high], axis=dim)
    return block


def fold_rows(left, piece):
    return jnp.dot(left, piece, preferred_element_type=jnp.float32)


def local(tokens, w_query, w_keyval, global_off, rand_dev, rand_sub):
    ntok = tokens.shape[0]
    nseq = lax.axis_size("seq")
    me_index = lax.axis_index("seq")
    nblk = ntok // BLOCK
    inner = H * HD
    glob_rows = lax.all_gather(jnp.take(tokens, global_off, axis=0), "seq", axis=0, tiled=True)
    left_kv = jnp.concatenate([tokens, glob_rows], axis=0)
    query = fold_rows(tokens, lax.all_gather(w_query, "seq", axis=0, tiled=True))
    keyval = fold_rows(left_kv, lax.all_gather(w_keyval, "seq", axis=0, tiled=True))
    query = query.astype(jnp.bfloat16)
    keyval = keyval.astype(jnp.bfloat16)
    glob_kv = keyval[ntok:]
    keyval = keyval[:ntok]
    glob_kv = glob_kv.reshape(glob_kv.shape[0], 2, H, HD)
    padded = padded_2(keyval, (("seq", 0),), BLOCK)
    window = jnp.concatenate(
        [padded[j * BLOCK : j * BLOCK + ntok].reshape(nblk, BLOCK, 2, H, HD) for j in range(3)],
        axis=1,
    )
    capacity = max(2, 3 * BLK_DEV * H * R // (2 * nseq))
    nreq = nblk * H * R
    dev_all = rand_dev.reshape(nseq, nreq)
    sub_all = rand_sub.reshape(nseq, nreq)
    match = (dev_all == me_index).astype(jnp.int32)
    slot_all = jnp.cumsum(match, axis=1) - 1
    head_of = jnp.arange(nreq, dtype=jnp.int32) // R % H
    code_all = head_of[None, :] * nblk + sub_all
    picked = (match[:, None, :] == 1) & (
        slot_all[:, None, :] == jnp.arange(capacity, dtype=jnp.int32)[None, :, None]
    )
    source = jnp.sum(jnp.where(picked, code_all[:, None, :], 0), axis=2)
    tiles = (
        keyval.reshape(nblk, BLOCK, 2, H, HD)
        .transpose(3, 0, 1, 2, 4)
        .reshape(H * nblk, BLOCK, 2 * HD)
    )
    outgoing = jnp.take(tiles, source, axis=0)
    incoming = lax.all_to_all(outgoing, "seq", split_axis=0, concat_axis=0, tiled=True)
    my_dev = lax.dynamic_slice_in_dim(rand_dev, me_index * nblk, nblk, 0).reshape(nreq)
    onehot = (my_dev[:, None] == jnp.arange(nseq, dtype=jnp.int32)[None, :]).astype(jnp.int32)
    my_slot = jnp.sum(onehot * (jnp.cumsum(onehot, axis=0) - 1), axis=1)
    flat_index = my_dev * capacity + my_slot
    fetched = jnp.take(incoming.reshape(nseq * capacity, BLOCK, 2 * HD), flat_index, axis=0)
    fetched = fetched.reshape(nblk, H, R, BLOCK, 2, HD)
    scale = HD ** (-0.5)
    qry = query.reshape(nblk, BLOCK, H, HD)
    s_win = (
        jnp.einsum("bqhd,bkhd->bhqk", qry, window[:, :, 0], preferred_element_type=jnp.float32)
        * scale
    )
    s_rnd = (
        jnp.einsum(
            "bqhd,bhrkd->bhqrk", qry, fetched[:, :, :, :, 0], preferred_element_type=jnp.float32
        ).reshape(nblk, H, BLOCK, R * BLOCK)
        * scale
    )
    s_glb = (
        jnp.einsum("bqhd,ghd->bhqg", qry, glob_kv[:, 0], preferred_element_type=jnp.float32) * scale
    )
    blk_ids = me_index * nblk + jnp.arange(nblk, dtype=jnp.int32)
    left_ok = jnp.repeat((blk_ids > 0)[:, None], BLOCK, axis=1)
    right_ok = jnp.repeat((blk_ids < nseq * nblk - 1)[:, None], BLOCK, axis=1)
    middle_ok = jnp.ones((nblk, BLOCK), dtype=bool)
    window_ok = jnp.concatenate([left_ok, middle_ok, right_ok], axis=1)
    s_win = jnp.where(window_ok[:, None, None, :], s_win, -jnp.inf)
    scores = jnp.concatenate([s_win, s_rnd, s_glb], axis=3)
    highest = jnp.max(scores, axis=3, keepdims=True)
    expo = jnp.exp(scores - highest)
    weights = (expo / jnp.sum(expo, axis=3, keepdims=True)).astype(jnp.bfloat16)
    w_win = weights[..., : 3 * BLOCK]
    w_rnd = weights[..., 3 * BLOCK : 3 * BLOCK + R * BLOCK].reshape(nblk, H, BLOCK, R, BLOCK)
    w_glb = weights[..., 3 * BLOCK + R * BLOCK :]
    ctx = jnp.einsum("bhqk,bkhd->bqhd", w_win, window[:, :, 1], preferred_element_type=jnp.float32)
    ctx = ctx + jnp.einsum(
        "bhqrk,bhrkd->bqhd", w_rnd, fetched[:, :, :, :, 1], preferred_element_type=jnp.float32
    )
    ctx = ctx + jnp.einsum(
        "bhqg,ghd->bqhd", w_glb, glob_kv[:, 1], preferred_element_type=jnp.float32
    )
    return ctx.reshape(ntok, inner).astype(jnp.bfloat16)


def chunks_of(ntok):
    half, quarter = ntok // 2, ntok // 4
    return ((0, half), (half, quarter), (half + quarter, quarter))


def fused_kernel(
    planes, tok_hbm, wq_hbm, wkv_hbm, pick_hbm, dev_hbm, sub_hbm, out_ref,
    tok, wts, qry, kv, far_q, far_kv, picks, ctx, glob_sum, dev_ref, sub_ref,
    local_sem, w_send, w_recv, g_send, g_recv, t_send, t_recv, f_send, f_recv,
    k_send, k_recv, p_send, p_recv, o_send, o_recv, c_send, c_recv,
):
    ntok = tok_hbm.shape[0]
    nblk = ntok // BLOCK
    heads = H // planes
    cols = heads * HD
    half = wts.shape[4]
    x = lax.axis_index("groups")
    me = lax.axis_index("seq")
    z = me // LANES
    lane = me % LANES
    core_lane = lane + 1 - 2 * (lane % 2)
    y_lane = (lane + 2) % LANES
    diag_lane = (core_lane + 2) % LANES
    mid = planes // 2
    workers, ends = (mid - 1, mid), (0, planes - 1)
    lower = z < mid
    own_worker = jnp.where(lower, workers[0], workers[1])
    own_end = jnp.where(lower, ends[0], ends[1])
    far_worker = jnp.where(lower, workers[1], workers[0])
    far_end = jnp.where(lower, ends[1], ends[0])
    mate = jnp.where(z == own_worker, own_end, own_worker)
    order = [own_worker, own_end, far_worker, far_end]

    def at(plane, where):
        return {"seq": plane * LANES + where}

    x_peer = {"groups": 1 - x}
    core_peer = at(z, core_lane)
    y_peer = at(z, y_lane)
    diag_peer = at(z, diag_lane)
    partners = ((y_lane, y_peer), (core_lane, core_peer), (diag_lane, diag_peer))

    def remote(src, dst, send, recv, peer):
        return pltpu.make_async_remote_copy(
            src_ref=src, dst_ref=dst, send_sem=send, recv_sem=recv, device_id=peer,
            device_id_type=MESH,
        )

    dev_in = pltpu.make_async_copy(dev_hbm, dev_ref, local_sem.at[0])
    dev_in.start()
    sub_in = pltpu.make_async_copy(sub_hbm, sub_ref, local_sem.at[3])
    sub_in.start()
    pick_in = pltpu.make_async_copy(pick_hbm, picks.at[lane, z], local_sem.at[1])
    pick_in.start()
    tok_in = pltpu.make_async_copy(tok_hbm, tok.at[z], local_sem.at[2])
    tok_in.start()

    barrier = pltpu.get_barrier_semaphore()
    for step in range(1, planes):
        pl.semaphore_signal(
            barrier, inc=1, device_id=at((z + step) % planes, lane), device_id_type=MESH
        )
    for peer in (x_peer, core_peer, y_peer, diag_peer):
        pl.semaphore_signal(barrier, inc=1, device_id=peer, device_id_type=MESH)
    pl.semaphore_wait(barrier, planes - 1 + 4)

    def weight_refs(index, kind, part):
        plane = (ends, workers)[kind][index]
        rows = pl.ds(pl.multiple_of(x * half, half), half)
        first = (0, 0, H * HD)[part] + plane * cols
        src = (wq_hbm, wkv_hbm, wkv_hbm)[part].at[rows, pl.ds(first, cols)]
        return src, wts.at[kind, z, lane, x, :, pl.ds(part * cols, cols)]

    def weight_remote(index, kind, part):
        src, dst = weight_refs(index, kind, part)
        return remote(
            src, dst, w_send.at[index, kind, part], w_recv.at[z, kind, part],
            at(workers[index], lane),
        )

    def weights_out(kind):
        for index in range(2):
            for part in range(3):
                @pl.when(z != workers[index])
                def _():
                    weight_remote(index, kind, part).start()

                @pl.when(z == workers[index])
                def _():
                    src, dst = weight_refs(index, kind, part)
                    pltpu.make_async_copy(src, dst, w_recv.at[z, kind, part]).start()

    def weights_in(kind):
        for plane in range(planes):
            for part in range(3):
                here = wts.at[kind, plane, lane, x, :, pl.ds(part * cols, cols)]
                remote(here, here, w_send.at[0, kind, part], w_recv.at[plane, kind, part], core_peer).wait_recv()

    towards = jnp.where(lower, z + 1, z - 1)
    cuts = chunks_of(ntok)
    chunks = [pl.ds(first, count) for first, count in cuts]

    def own_out(c):
        return remote(
            tok_hbm.at[chunks[c]], tok.at[z, chunks[c]], t_send.at[0, c], t_recv.at[z, c],
            at(towards, lane),
        )

    def pass_out(c):
        ref = tok.at[own_end, chunks[c]]
        return remote(ref, ref, t_send.at[1, c], t_recv.at[own_end, c], at(towards, lane))

    def tok_wait(plane, c):
        ref = tok.at[plane, chunks[c]]
        remote(ref, ref, t_send.at[0, c], t_recv.at[plane, c], core_peer).wait_recv()

    weights_out(0)
    weights_out(1)
    for c in range(len(cuts)):
        own_out(c).start()

    def pick_copy(step):
        return remote(pick_hbm, picks.at[lane, z], p_send.at[step - 1], p_recv.at[z], at((z + step) % planes, lane))

    for step in range(1, planes):
        pick_copy(step).start()

    width = 3 * cols
    every, left, right = pl.ds(0, width), pl.ds(0, width // 2), pl.ds(width // 2, width // 2)
    moves = (
        (x, lane, every, x_peer, 1 - x, lane),
        (x, lane, every, y_peer, x, y_lane),
        (x, lane, every, core_peer, x, core_lane),
        (1 - x, lane, left, y_peer, 1 - x, y_lane),
        (1 - x, lane, every, core_peer, 1 - x, core_lane),
        (x, y_lane, right, x_peer, 1 - x, y_lane),
        (x, y_lane, every, core_peer, x, diag_lane),
        (1 - x, y_lane, left, core_peer, 1 - x, diag_lane),
        (1 - x, y_lane, right, core_peer, 1 - x, diag_lane),
    )

    def gather_out(kind, index):
        group, where, part, peer = moves[index][:4]
        ref = wts.at[kind, :, where, group, :, part]
        return remote(ref, ref, g_send.at[kind, index], g_recv.at[kind, index], peer)

    def gather_wait(kind, index):
        part, peer, group, where = moves[index][2:]
        ref = wts.at[kind, :, where, group, :, part]
        remote(ref, ref, g_send.at[kind, index], g_recv.at[kind, index], peer).wait_recv()

    def gather_first(kind):
        weights_in(kind)
        for index in range(3):
            gather_out(kind, index).start()

    def gather_second(kind):
        gather_wait(kind, 0)
        gather_out(kind, 3).start()
        gather_out(kind, 4).start()
        gather_wait(kind, 1)
        gather_out(kind, 5).start()
        gather_out(kind, 6).start()

    def gather_last(kind):
        gather_wait(kind, 3)
        gather_out(kind, 7).start()
        gather_wait(kind, 5)
        gather_out(kind, 8).start()
        for index in (2, 4, 6, 7, 8):
            gather_wait(kind, index)

    def kv_rows(ref, plane, where, first=0, count=nblk):
        return ref.at[pl.ds((plane * LANES + where) * nblk + first, count)]

    units = [(i, 0, ntok) for i in range(planes - 1)]
    units += [(planes - 1, first, count) for first, count in cuts]

    def unit_kv(unit, where):
        index, first, count = units[unit]
        return kv_rows(kv, order[index], where, first // BLOCK, count // BLOCK)

    def unit_q(unit):
        index, first, count = units[unit]
        return qry.at[order[index], pl.ds(first, count)]

    def kv_copy(unit, which, where, peer):
        ref = unit_kv(unit, where)
        return remote(ref, ref, k_send.at[which, unit], k_recv.at[which, unit], peer)

    def kv_out(unit):
        kv_copy(unit, 0, lane, y_peer).start()
        kv_copy(unit, 1, lane, core_peer).start()

    def kv_forward(unit):
        kv_copy(unit, 0, y_lane, y_peer).wait_recv()
        kv_copy(unit, 2, y_lane, core_peer).start()

    def project(unit, kind):
        index, first, count = units[unit]
        weights = wts[kind].reshape(-1, width)
        rows = tok[order[index], pl.ds(first, count)]
        res = jnp.dot(rows, weights, preferred_element_type=jnp.float32).astype(jnp.bfloat16)
        return res[:, :cols], res[:, cols:].reshape(count // BLOCK, BLOCK, 2 * cols)

    def far_refs(unit):
        index, first, count = units[unit]
        blocks = pl.ds(index * nblk + first // BLOCK, count // BLOCK)
        return far_q.at[index, pl.ds(first, count)], far_kv.at[blocks]

    def far_copies(unit):
        from_q, from_kv = far_refs(unit)
        return (
            remote(from_kv, unit_kv(unit, lane), f_send.at[1, unit], f_recv.at[1, unit], at(mate, lane)),
            remote(from_q, unit_q(unit), f_send.at[0, unit], f_recv.at[0, unit], at(mate, lane)),
        )

    def project_far(unit):
        from_q, from_kv = far_refs(unit)
        from_q[...], from_kv[...] = project(unit, 0)
        for copy in far_copies(unit):
            copy.start()

    def project_own(unit):
        unit_q(unit)[...], unit_kv(unit, lane)[...] = project(unit, 1)
        kv_out(unit)

    def pick_lane(index, where, peer):
        return remote(picks.at[where], picks.at[where], o_send.at[index], o_recv.at[index], peer)

    def picks_first():
        pick_in.wait()
        for step in range(1, planes):
            source = (z + step) % planes
            ref = picks.at[lane, source]
            remote(ref, ref, p_send.at[0], p_recv.at[source], core_peer).wait_recv()
        for index, (where, peer) in enumerate(partners):
            pick_lane(index, lane, peer).start()

    def picks_last():
        for index, (where, peer) in enumerate(partners):
            pick_lane(index, where, peer).wait_recv()

    def glob_add(index):
        for unit in [u for u in range(len(units)) if units[u][0] == index]:
            kv_copy(unit, 1, core_lane, core_peer).wait_recv()
            kv_copy(unit, 2, diag_lane, core_peer).wait_recv()
        total = jnp.zeros(glob_sum.shape, jnp.float32) if index == 0 else glob_sum[...]
        for where in range(LANES):
            rows = kv_rows(kv, order[index], where)[...].reshape(ntok, 2 * cols)
            total = total + jnp.dot(
                picks[where, order[index]], rows, preferred_element_type=jnp.float32
            )
        glob_sum[...] = total

    last = len(units) - 1

    @pl.when(z == own_worker)
    def _():
        gather_first(0)
        gather_second(0)
        tok_in.wait()
        tok_wait(own_end, 0)
        pass_out(0).start()
        gather_first(1)
        gather_last(0)
        project_far(0)
        for c in range(1, len(cuts)):
            tok_wait(own_end, c)
            pass_out(c).start()
        project_far(1)
        gather_second(1)
        picks_first()
        for c in range(len(cuts)):
            tok_wait(far_worker, c)
        project_far(2)
        gather_last(1)
        project_own(0)
        project_own(1)
        kv_forward(0)
        project_own(2)
        kv_forward(1)
        picks_last()
        for unit in range(planes - 1, len(units)):
            tok_wait(far_end, unit - planes + 1)
            project_far(unit)
            project_own(unit)
            kv_forward(unit - 1)
            if unit < last:
                glob_add(unit - planes + 1)
        glob_add(planes - 2)
        kv_forward(last)

    @pl.when(z != own_worker)
    def _():
        tok_in.wait()
        picks_first()
        picks_last()
        for unit in range(len(units)):
            here = unit_kv(unit, lane)
            remote(here, here, f_send.at[1, unit], f_recv.at[1, unit], core_peer).wait_recv()
            kv_out(unit)
            if unit:
                kv_forward(unit - 1)
            if planes - 1 <= unit < last:
                glob_add(unit - planes + 1)
        glob_add(planes - 2)
        kv_forward(last)
        for unit in range(len(units)):
            here = unit_q(unit)
            remote(here, here, f_send.at[0, unit], f_recv.at[0, unit], core_peer).wait_recv()

    glob_add(planes - 1)
    glob = glob_sum[: planes * LANES].astype(jnp.bfloat16)
    dev_in.wait()
    sub_in.wait()
    total_blocks = planes * LANES * nblk
    scale = HD ** (-0.5)
    keys = (3 + R) * BLOCK + glob.shape[0]
    column = lax.broadcasted_iota(jnp.int32, (BLOCK, keys), 1)

    def ctx_copy(plane, index):
        return remote(
            ctx.at[plane],
            out_ref.at[:, pl.ds(pl.multiple_of(z * cols, cols), cols)],
            c_send.at[index], c_recv.at[z], at(plane, lane),
        )

    def attend(plane):
        for sub in range(nblk):
            block = (plane * LANES + lane) * nblk + sub
            starts = [
                jnp.maximum(block - 1, 0),
                block,
                jnp.minimum(block + 1, total_blocks - 1),
            ]
            q_rows = slice(sub * BLOCK, (sub + 1) * BLOCK)
            for h in range(heads):
                head = z * heads + h
                where = starts + [
                    dev_ref[j, head, block] * nblk + sub_ref[j, head, block] for j in range(R)
                ]
                k_cols = slice(h * HD, (h + 1) * HD)
                v_cols = slice(cols + h * HD, cols + (h + 1) * HD)
                key = jnp.concatenate(
                    [kv[w, :, k_cols] for w in where] + [glob[:, k_cols]], axis=0
                )
                val = jnp.concatenate(
                    [kv[w, :, v_cols] for w in where] + [glob[:, v_cols]], axis=0
                )
                score = lax.dot_general(
                    qry[plane, q_rows, k_cols], key, (((1,), (1,)), ((), ())),
                    preferred_element_type=jnp.float32,
                ) * scale
                if sub == 0:
                    score = jnp.where((column < BLOCK) & (block == 0), -jnp.inf, score)
                if sub == nblk - 1:
                    after = (column >= 2 * BLOCK) & (column < 3 * BLOCK)
                    score = jnp.where(after & (block == total_blocks - 1), -jnp.inf, score)
                expo = jnp.exp(score - jnp.max(score, axis=1, keepdims=True))
                soft = (expo * (1.0 / jnp.sum(expo, axis=1, keepdims=True))).astype(jnp.bfloat16)
                ctx[plane, q_rows, k_cols] = jnp.dot(
                    soft, val, preferred_element_type=jnp.float32
                ).astype(jnp.bfloat16)

    others = (far_end, far_worker, mate)
    for index, plane in enumerate(others):
        attend(plane)
        ctx_copy(plane, index).start()
    attend(z)
    own = pltpu.make_async_copy(
        ctx.at[z], out_ref.at[:, pl.ds(pl.multiple_of(z * cols, cols), cols)], local_sem.at[0]
    )
    own.start()
    own.wait()

    for index, plane in enumerate(others):
        ctx_copy(plane, index).wait_send()
        there = out_ref.at[:, pl.ds(pl.multiple_of(plane * cols, cols), cols)]
        remote(ctx.at[plane], there, c_send.at[index], c_recv.at[plane], core_peer).wait_recv()
    for index in range(2):
        @pl.when(z != workers[index])
        def _():
            for kind in range(2):
                for part in range(3):
                    weight_remote(index, kind, part).wait_send()
    for c in range(len(cuts)):
        own_out(c).wait_send()

    @pl.when(z == own_worker)
    def _():
        for c in range(len(cuts)):
            pass_out(c).wait_send()
        for kind in range(2):
            for index in range(len(moves)):
                gather_out(kind, index).wait_send()
        for unit in range(len(units)):
            for copy in far_copies(unit):
                copy.wait_send()

    for unit in range(len(units)):
        kv_copy(unit, 0, lane, y_peer).wait_send()
        kv_copy(unit, 1, lane, core_peer).wait_send()
        kv_copy(unit, 2, y_lane, core_peer).wait_send()
    for step in range(1, planes):
        pick_copy(step).wait_send()
    for index, (where, peer) in enumerate(partners):
        pick_lane(index, lane, peer).wait_send()


def fused(tokens, w_query, w_keyval, global_off, rand_dev, rand_sub):
    nseq = lax.axis_size("seq")
    ntok, width = tokens.shape
    planes = nseq // LANES
    nblk = ntok // BLOCK
    picked = -(-nseq // 16) * 16
    cols = H // planes * HD
    half = w_query.shape[0] // 2
    dev, sub = rand_dev.transpose(2, 1, 0), rand_sub.transpose(2, 1, 0)
    shape = (picked, ntok)
    at_row = lax.broadcasted_iota(jnp.int32, shape, 0) == lax.axis_index("seq")
    at_event = lax.broadcasted_iota(jnp.int32, shape, 1) == global_off[0]
    pick = jnp.where(at_row & at_event, 1.0, 0.0).astype(jnp.bfloat16)
    dma = pltpu.SemaphoreType.DMA
    cuts = chunks_of(ntok)
    units = planes - 1 + len(cuts)
    return pl.pallas_call(
        functools.partial(fused_kernel, planes),
        out_shape=jax.ShapeDtypeStruct((ntok, H * HD), jnp.bfloat16),
        in_specs=[pl.BlockSpec(memory_space=pl.ANY)] * 6,
        out_specs=pl.BlockSpec(memory_space=pl.ANY),
        scratch_shapes=[
            pltpu.VMEM((planes, ntok, width), jnp.bfloat16),
            pltpu.VMEM((2, planes, LANES, 2, half, 3 * cols), jnp.bfloat16),
            pltpu.VMEM((planes, ntok, cols), jnp.bfloat16),
            pltpu.VMEM((nseq * nblk, BLOCK, 2 * cols), jnp.bfloat16),
            pltpu.VMEM((planes, ntok, cols), jnp.bfloat16),
            pltpu.VMEM((planes * nblk, BLOCK, 2 * cols), jnp.bfloat16),
            pltpu.VMEM((LANES, planes, picked, ntok), jnp.bfloat16),
            pltpu.VMEM((planes, ntok, cols), jnp.bfloat16),
            pltpu.VMEM((picked, 2 * cols), jnp.float32),
            pltpu.SMEM(dev.shape, jnp.int32),
            pltpu.SMEM(sub.shape, jnp.int32),
            dma((4,)),
            dma((2, 2, 3)),
            dma((planes, 2, 3)),
            dma((2, 9)),
            dma((2, 9)),
            dma((2, len(cuts))),
            dma((planes, len(cuts))),
            dma((2, units)),
            dma((2, units)),
            dma((3, units)),
            dma((3, units)),
            dma((planes - 1,)),
            dma((planes,)),
            dma((3,)),
            dma((3,)),
            dma((planes - 1,)),
            dma((planes,)),
        ],
        compiler_params=pltpu.CompilerParams(
            collective_id=0, has_side_effects=True, vmem_limit_bytes=60 * 1024 * 1024
        ),
        cost_estimate=pl.CostEstimate(
            flops=2 * planes * ntok * width * 3 * cols,
            bytes_accessed=2 * planes * ntok * width,
            transcendentals=ntok * H * 400,
        ),
    )(tokens, w_query, w_keyval, pick, dev, sub)


def solution(mesh):
    in_specs = (
        P(("groups", "seq"), None),
        P("seq", None),
        P("seq", None),
        P(("groups", "seq")),
        P("groups", None, None),
        P("groups", None, None),
    )
    out_specs = P(("groups", "seq"), None)
    nseq, groups = mesh.shape["seq"], mesh.shape["groups"]
    planes = nseq // LANES
    paired = groups == 2 and planes * LANES == nseq and planes == 4
    body = fused if paired else local
    return jax.shard_map(body, mesh=mesh, in_specs=in_specs, out_specs=out_specs, check_vma=False)
```

```python
import functools
import math

import jax
import jax.numpy as jnp
from jax import lax
from jax.experimental import pallas as pl
from jax.experimental.pallas import tpu as pltpu
from jax.sharding import PartitionSpec as P

H = 8
HD = 128
BLOCK = 64
R = 3
BLK_DEV = 4
LANES = 4
MESH = pl.DeviceIdType.MESH


def padded_2(block, sides, width):
    for axis, dim in sides:
        count = lax.axis_size(axis)
        forward = [(i, i + 1) for i in range(count - 1)]
        backward = [(target, source) for source, target in forward]
        low = lax.ppermute(
            lax.slice_in_dim(block, block.shape[dim] - width, None, axis=dim), axis, forward
        )
        high = lax.ppermute(lax.slice_in_dim(block, 0, width, axis=dim), axis, backward)
        block = jnp.concatenate([low, block, high], axis=dim)
    return block


def fold_rows(left, piece):
    return jnp.dot(left, piece, preferred_element_type=jnp.float32)


def local(tokens, w_query, w_keyval, global_off, rand_dev, rand_sub):
    ntok = tokens.shape[0]
    nseq = lax.axis_size("seq")
    me_index = lax.axis_index("seq")
    nblk = ntok // BLOCK
    inner = H * HD
    glob_rows = lax.all_gather(jnp.take(tokens, global_off, axis=0), "seq", axis=0, tiled=True)
    left_kv = jnp.concatenate([tokens, glob_rows], axis=0)
    query = fold_rows(tokens, lax.all_gather(w_query, "seq", axis=0, tiled=True))
    keyval = fold_rows(left_kv, lax.all_gather(w_keyval, "seq", axis=0, tiled=True))
    query = query.astype(jnp.bfloat16)
    keyval = keyval.astype(jnp.bfloat16)
    glob_kv = keyval[ntok:]
    keyval = keyval[:ntok]
    glob_kv = glob_kv.reshape(glob_kv.shape[0], 2, H, HD)
    padded = padded_2(keyval, (("seq", 0),), BLOCK)
    window = jnp.concatenate(
        [padded[j * BLOCK : j * BLOCK + ntok].reshape(nblk, BLOCK, 2, H, HD) for j in range(3)],
        axis=1,
    )
    capacity = max(2, 3 * BLK_DEV * H * R // (2 * nseq))
    nreq = nblk * H * R
    dev_all = rand_dev.reshape(nseq, nreq)
    sub_all = rand_sub.reshape(nseq, nreq)
    match = (dev_all == me_index).astype(jnp.int32)
    slot_all = jnp.cumsum(match, axis=1) - 1
    head_of = jnp.arange(nreq, dtype=jnp.int32) // R % H
    code_all = head_of[None, :] * nblk + sub_all
    picked = (match[:, None, :] == 1) & (
        slot_all[:, None, :] == jnp.arange(capacity, dtype=jnp.int32)[None, :, None]
    )
    source = jnp.sum(jnp.where(picked, code_all[:, None, :], 0), axis=2)
    tiles = (
        keyval.reshape(nblk, BLOCK, 2, H, HD)
        .transpose(3, 0, 1, 2, 4)
        .reshape(H * nblk, BLOCK, 2 * HD)
    )
    outgoing = jnp.take(tiles, source, axis=0)
    incoming = lax.all_to_all(outgoing, "seq", split_axis=0, concat_axis=0, tiled=True)
    my_dev = lax.dynamic_slice_in_dim(rand_dev, me_index * nblk, nblk, 0).reshape(nreq)
    onehot = (my_dev[:, None] == jnp.arange(nseq, dtype=jnp.int32)[None, :]).astype(jnp.int32)
    my_slot = jnp.sum(onehot * (jnp.cumsum(onehot, axis=0) - 1), axis=1)
    flat_index = my_dev * capacity + my_slot
    fetched = jnp.take(incoming.reshape(nseq * capacity, BLOCK, 2 * HD), flat_index, axis=0)
    fetched = fetched.reshape(nblk, H, R, BLOCK, 2, HD)
    scale = HD ** (-0.5)
    qry = query.reshape(nblk, BLOCK, H, HD)
    s_win = (
        jnp.einsum("bqhd,bkhd->bhqk", qry, window[:, :, 0], preferred_element_type=jnp.float32)
        * scale
    )
    s_rnd = (
        jnp.einsum(
            "bqhd,bhrkd->bhqrk", qry, fetched[:, :, :, :, 0], preferred_element_type=jnp.float32
        ).reshape(nblk, H, BLOCK, R * BLOCK)
        * scale
    )
    s_glb = (
        jnp.einsum("bqhd,ghd->bhqg", qry, glob_kv[:, 0], preferred_element_type=jnp.float32) * scale
    )
    blk_ids = me_index * nblk + jnp.arange(nblk, dtype=jnp.int32)
    left_ok = jnp.repeat((blk_ids > 0)[:, None], BLOCK, axis=1)
    right_ok = jnp.repeat((blk_ids < nseq * nblk - 1)[:, None], BLOCK, axis=1)
    middle_ok = jnp.ones((nblk, BLOCK), dtype=bool)
    window_ok = jnp.concatenate([left_ok, middle_ok, right_ok], axis=1)
    s_win = jnp.where(window_ok[:, None, None, :], s_win, -jnp.inf)
    scores = jnp.concatenate([s_win, s_rnd, s_glb], axis=3)
    highest = jnp.max(scores, axis=3, keepdims=True)
    expo = jnp.exp(scores - highest)
    weights = (expo / jnp.sum(expo, axis=3, keepdims=True)).astype(jnp.bfloat16)
    w_win = weights[..., : 3 * BLOCK]
    w_rnd = weights[..., 3 * BLOCK : 3 * BLOCK + R * BLOCK].reshape(nblk, H, BLOCK, R, BLOCK)
    w_glb = weights[..., 3 * BLOCK + R * BLOCK :]
    ctx = jnp.einsum("bhqk,bkhd->bqhd", w_win, window[:, :, 1], preferred_element_type=jnp.float32)
    ctx = ctx + jnp.einsum(
        "bhqrk,bhrkd->bqhd", w_rnd, fetched[:, :, :, :, 1], preferred_element_type=jnp.float32
    )
    ctx = ctx + jnp.einsum(
        "bhqg,ghd->bqhd", w_glb, glob_kv[:, 1], preferred_element_type=jnp.float32
    )
    return ctx.reshape(ntok, inner).astype(jnp.bfloat16)


def chunks_of(ntok):
    half, quarter = ntok // 2, ntok // 4
    return ((0, half), (half, quarter), (half + quarter, quarter))


def fused_kernel(
    planes, tok_hbm, wq_hbm, wkv_hbm, off_ref, dev_hbm, sub_hbm, out_ref,
    tok, wts, qry, kv, far_q, far_kv, picks, ctx, glob_sum, dev_ref, sub_ref,
    local_sem, w_send, w_recv, g_send, g_recv, t_send, t_recv, f_send, f_recv,
    k_send, k_recv, p_send, p_recv, o_send, o_recv, c_send, c_recv,
):
    ntok = tok_hbm.shape[0]
    nblk = ntok // BLOCK
    heads = H // planes
    cols = heads * HD
    half = wts.shape[4]
    x = lax.axis_index("groups")
    me = lax.axis_index("seq")
    z = me // LANES
    lane = me % LANES
    core_lane = lane + 1 - 2 * (lane % 2)
    y_lane = (lane + 2) % LANES
    diag_lane = (core_lane + 2) % LANES
    mid = planes // 2
    workers, ends = (mid - 1, mid), (0, planes - 1)
    lower = z < mid
    own_worker = jnp.where(lower, workers[0], workers[1])
    own_end = jnp.where(lower, ends[0], ends[1])
    far_worker = jnp.where(lower, workers[1], workers[0])
    far_end = jnp.where(lower, ends[1], ends[0])
    mate = jnp.where(z == own_worker, own_end, own_worker)
    order = [own_worker, own_end, far_worker, far_end]

    def at(plane, where):
        return {"seq": plane * LANES + where}

    x_peer = {"groups": 1 - x}
    core_peer = at(z, core_lane)
    y_peer = at(z, y_lane)
    diag_peer = at(z, diag_lane)
    partners = ((y_lane, y_peer), (core_lane, core_peer), (diag_lane, diag_peer))

    def remote(src, dst, send, recv, peer):
        return pltpu.make_async_remote_copy(
            src_ref=src, dst_ref=dst, send_sem=send, recv_sem=recv, device_id=peer,
            device_id_type=MESH,
        )

    dev_in = pltpu.make_async_copy(dev_hbm, dev_ref, local_sem.at[0])
    dev_in.start()
    sub_in = pltpu.make_async_copy(sub_hbm, sub_ref, local_sem.at[1])
    sub_in.start()
    tok_in = pltpu.make_async_copy(tok_hbm, tok.at[z], local_sem.at[2])
    tok_in.start()

    barrier = pltpu.get_barrier_semaphore()
    for step in range(1, planes):
        pl.semaphore_signal(
            barrier, inc=1, device_id=at((z + step) % planes, lane), device_id_type=MESH
        )
    for peer in (x_peer, core_peer, y_peer, diag_peer):
        pl.semaphore_signal(barrier, inc=1, device_id=peer, device_id_type=MESH)
    pl.semaphore_wait(barrier, planes - 1 + 4)

    def weight_refs(index, kind, part):
        plane = (ends, workers)[kind][index]
        rows = pl.ds(pl.multiple_of(x * half, half), half)
        first = (0, 0, H * HD)[part] + plane * cols
        src = (wq_hbm, wkv_hbm, wkv_hbm)[part].at[rows, pl.ds(first, cols)]
        return src, wts.at[kind, z, lane, x, :, pl.ds(part * cols, cols)]

    def weight_remote(index, kind, part):
        src, dst = weight_refs(index, kind, part)
        return remote(
            src, dst, w_send.at[index, kind, part], w_recv.at[z, kind, part],
            at(workers[index], lane),
        )

    def weights_out(kind):
        for index in range(2):
            for part in range(3):
                @pl.when(z != workers[index])
                def _():
                    weight_remote(index, kind, part).start()

                @pl.when(z == workers[index])
                def _():
                    src, dst = weight_refs(index, kind, part)
                    pltpu.make_async_copy(src, dst, w_recv.at[z, kind, part]).start()

    def weights_in(kind):
        for plane in range(planes):
            for part in range(3):
                here = wts.at[kind, plane, lane, x, :, pl.ds(part * cols, cols)]
                remote(here, here, w_send.at[0, kind, part], w_recv.at[plane, kind, part], core_peer).wait_recv()

    towards = jnp.where(lower, z + 1, z - 1)
    cuts = chunks_of(ntok)
    chunks = [pl.ds(first, count) for first, count in cuts]

    def own_out(c):
        return remote(
            tok_hbm.at[chunks[c]], tok.at[z, chunks[c]], t_send.at[0, c], t_recv.at[z, c],
            at(towards, lane),
        )

    def pass_out(c):
        ref = tok.at[own_end, chunks[c]]
        return remote(ref, ref, t_send.at[1, c], t_recv.at[own_end, c], at(towards, lane))

    def tok_wait(plane, c):
        ref = tok.at[plane, chunks[c]]
        remote(ref, ref, t_send.at[0, c], t_recv.at[plane, c], core_peer).wait_recv()

    weights_out(0)
    weights_out(1)
    own_out(0).start()

    at_row = lax.broadcasted_iota(jnp.int32, picks.shape[2:], 0) == me
    at_event = lax.broadcasted_iota(jnp.int32, picks.shape[2:], 1) == off_ref[0]
    picks[lane, z] = jnp.where(at_row & at_event, 1.0, 0.0).astype(jnp.bfloat16)

    def pick_copy(step):
        return remote(picks.at[lane, z], picks.at[lane, z], p_send.at[step - 1], p_recv.at[z], at((z + step) % planes, lane))

    for step in range(1, planes):
        pick_copy(step).start()

    width = 3 * cols
    every, left, right = pl.ds(0, width), pl.ds(0, width // 2), pl.ds(width // 2, width // 2)
    moves = (
        (x, lane, every, x_peer, 1 - x, lane),
        (x, lane, every, y_peer, x, y_lane),
        (x, lane, every, core_peer, x, core_lane),
        (1 - x, lane, left, y_peer, 1 - x, y_lane),
        (1 - x, lane, every, core_peer, 1 - x, core_lane),
        (x, y_lane, right, x_peer, 1 - x, y_lane),
        (x, y_lane, every, core_peer, x, diag_lane),
        (1 - x, y_lane, left, core_peer, 1 - x, diag_lane),
        (1 - x, y_lane, right, core_peer, 1 - x, diag_lane),
    )

    def gather_out(kind, index):
        group, where, part, peer = moves[index][:4]
        ref = wts.at[kind, :, where, group, :, part]
        return remote(ref, ref, g_send.at[kind, index], g_recv.at[kind, index], peer)

    def gather_wait(kind, index):
        part, peer, group, where = moves[index][2:]
        ref = wts.at[kind, :, where, group, :, part]
        remote(ref, ref, g_send.at[kind, index], g_recv.at[kind, index], peer).wait_recv()

    def gather_first(kind):
        weights_in(kind)
        for index in range(3):
            gather_out(kind, index).start()

    def gather_second(kind):
        gather_wait(kind, 0)
        gather_out(kind, 3).start()
        gather_out(kind, 4).start()
        gather_wait(kind, 1)
        gather_out(kind, 5).start()
        gather_out(kind, 6).start()

    def gather_last(kind):
        gather_wait(kind, 3)
        gather_out(kind, 7).start()
        gather_wait(kind, 5)
        gather_out(kind, 8).start()
        for index in (2, 4, 6, 7, 8):
            gather_wait(kind, index)

    def kv_rows(ref, plane, where, first=0, count=nblk):
        return ref.at[pl.ds((plane * LANES + where) * nblk + first, count)]

    units = [(i, 0, ntok) for i in range(planes - 1)]
    units += [(planes - 1, first, count) for first, count in cuts]

    def unit_kv(unit, where):
        index, first, count = units[unit]
        return kv_rows(kv, order[index], where, first // BLOCK, count // BLOCK)

    def unit_q(unit):
        index, first, count = units[unit]
        return qry.at[order[index], pl.ds(first, count)]

    def kv_copy(unit, which, where, peer):
        ref = unit_kv(unit, where)
        return remote(ref, ref, k_send.at[which, unit], k_recv.at[which, unit], peer)

    def kv_out(unit):
        kv_copy(unit, 0, lane, y_peer).start()
        kv_copy(unit, 1, lane, core_peer).start()

    def kv_forward(unit):
        kv_copy(unit, 0, y_lane, y_peer).wait_recv()
        kv_copy(unit, 2, y_lane, core_peer).start()

    def project(unit, kind):
        index, first, count = units[unit]
        weights = wts[kind].reshape(-1, width)
        rows = tok[order[index], pl.ds(first, count)]
        res = jnp.dot(rows, weights, preferred_element_type=jnp.float32).astype(jnp.bfloat16)
        return res[:, :cols], res[:, cols:].reshape(count // BLOCK, BLOCK, 2 * cols)

    def far_refs(unit):
        index, first, count = units[unit]
        blocks = pl.ds(index * nblk + first // BLOCK, count // BLOCK)
        return far_q.at[index, pl.ds(first, count)], far_kv.at[blocks]

    def far_copies(unit):
        from_q, from_kv = far_refs(unit)
        return (
            remote(from_kv, unit_kv(unit, lane), f_send.at[1, unit], f_recv.at[1, unit], at(mate, lane)),
            remote(from_q, unit_q(unit), f_send.at[0, unit], f_recv.at[0, unit], at(mate, lane)),
        )

    def project_far(unit):
        from_q, from_kv = far_refs(unit)
        from_q[...], from_kv[...] = project(unit, 0)
        for copy in far_copies(unit):
            copy.start()

    def project_own(unit):
        unit_q(unit)[...], unit_kv(unit, lane)[...] = project(unit, 1)
        kv_out(unit)

    def pick_lane(index, where, peer):
        return remote(picks.at[where], picks.at[where], o_send.at[index], o_recv.at[index], peer)

    def picks_first():
        for step in range(1, planes):
            source = (z + step) % planes
            ref = picks.at[lane, source]
            remote(ref, ref, p_send.at[0], p_recv.at[source], core_peer).wait_recv()
        for index, (where, peer) in enumerate(partners):
            pick_lane(index, lane, peer).start()

    def picks_last():
        for index, (where, peer) in enumerate(partners):
            pick_lane(index, where, peer).wait_recv()

    def glob_add(index):
        for unit in [u for u in range(len(units)) if units[u][0] == index]:
            kv_copy(unit, 1, core_lane, core_peer).wait_recv()
            kv_copy(unit, 2, diag_lane, core_peer).wait_recv()
        total = jnp.zeros(glob_sum.shape, jnp.float32) if index == 0 else glob_sum[...]
        for where in range(LANES):
            rows = kv_rows(kv, order[index], where)[...].reshape(ntok, 2 * cols)
            total = total + jnp.dot(
                picks[where, order[index]], rows, preferred_element_type=jnp.float32
            )
        glob_sum[...] = total

    last = len(units) - 1

    @pl.when(z == own_worker)
    def _():
        gather_first(0)
        own_out(1).start()
        gather_second(0)
        own_out(2).start()
        tok_in.wait()
        tok_wait(own_end, 0)
        pass_out(0).start()
        gather_first(1)
        gather_last(0)
        project_far(0)
        for c in range(1, len(cuts)):
            tok_wait(own_end, c)
            pass_out(c).start()
        project_far(1)
        gather_second(1)
        picks_first()
        for c in range(len(cuts)):
            tok_wait(far_worker, c)
        project_far(2)
        gather_last(1)
        project_own(0)
        project_own(1)
        kv_forward(0)
        project_own(2)
        kv_forward(1)
        picks_last()
        for unit in range(planes - 1, len(units)):
            tok_wait(far_end, unit - planes + 1)
            project_far(unit)
            project_own(unit)
            kv_forward(unit - 1)
            if unit < last:
                glob_add(unit - planes + 1)
        glob_add(planes - 2)
        kv_forward(last)

    @pl.when(z != own_worker)
    def _():
        own_out(1).start()
        own_out(2).start()
        tok_in.wait()
        picks_first()
        picks_last()
        for unit in range(len(units)):
            here = unit_kv(unit, lane)
            remote(here, here, f_send.at[1, unit], f_recv.at[1, unit], core_peer).wait_recv()
            kv_out(unit)
            if unit:
                kv_forward(unit - 1)
            if planes - 1 <= unit < last:
                glob_add(unit - planes + 1)
        glob_add(planes - 2)
        kv_forward(last)
        for unit in range(len(units)):
            here = unit_q(unit)
            remote(here, here, f_send.at[0, unit], f_recv.at[0, unit], core_peer).wait_recv()

    glob_add(planes - 1)
    glob = glob_sum[: planes * LANES].astype(jnp.bfloat16)
    dev_in.wait()
    sub_in.wait()
    total_blocks = planes * LANES * nblk
    scale = HD ** (-0.5) * math.log2(math.e)
    keys = (3 + R) * BLOCK + glob.shape[0]
    column = lax.broadcasted_iota(jnp.int32, (BLOCK, keys), 1)

    def ctx_copy(plane, index):
        return remote(
            ctx.at[plane],
            out_ref.at[:, pl.ds(pl.multiple_of(z * cols, cols), cols)],
            c_send.at[index], c_recv.at[z], at(plane, lane),
        )

    def attend(plane):
        for sub in range(nblk):
            block = (plane * LANES + lane) * nblk + sub
            starts = [
                jnp.maximum(block - 1, 0),
                block,
                jnp.minimum(block + 1, total_blocks - 1),
            ]
            q_rows = slice(sub * BLOCK, (sub + 1) * BLOCK)
            for h in range(heads):
                head = z * heads + h
                where = starts + [
                    dev_ref[j, head, block] * nblk + sub_ref[j, head, block] for j in range(R)
                ]
                k_cols = slice(h * HD, (h + 1) * HD)
                v_cols = slice(cols + h * HD, cols + (h + 1) * HD)
                key = jnp.concatenate(
                    [kv[w, :, k_cols] for w in where] + [glob[:, k_cols]], axis=0
                )
                val = jnp.concatenate(
                    [kv[w, :, v_cols] for w in where] + [glob[:, v_cols]], axis=0
                )
                score = lax.dot_general(
                    qry[plane, q_rows, k_cols], key, (((1,), (1,)), ((), ())),
                    preferred_element_type=jnp.float32,
                )
                if sub == 0:
                    score = jnp.where((column < BLOCK) & (block == 0), -jnp.inf, score)
                if sub == nblk - 1:
                    after = (column >= 2 * BLOCK) & (column < 3 * BLOCK)
                    score = jnp.where(after & (block == total_blocks - 1), -jnp.inf, score)
                expo = jnp.exp2((score - jnp.max(score, axis=1, keepdims=True)) * scale)
                soft = (expo * (1.0 / jnp.sum(expo, axis=1, keepdims=True))).astype(jnp.bfloat16)
                ctx[plane, q_rows, k_cols] = jnp.dot(
                    soft, val, preferred_element_type=jnp.float32
                ).astype(jnp.bfloat16)

    others = (far_end, far_worker, mate)
    for index, plane in enumerate(others):
        attend(plane)
        ctx_copy(plane, index).start()
    attend(z)
    own = pltpu.make_async_copy(
        ctx.at[z], out_ref.at[:, pl.ds(pl.multiple_of(z * cols, cols), cols)], local_sem.at[0]
    )
    own.start()
    own.wait()

    for index, plane in enumerate(others):
        ctx_copy(plane, index).wait_send()
        there = out_ref.at[:, pl.ds(pl.multiple_of(plane * cols, cols), cols)]
        remote(ctx.at[plane], there, c_send.at[index], c_recv.at[plane], core_peer).wait_recv()
    for index in range(2):
        @pl.when(z != workers[index])
        def _():
            for kind in range(2):
                for part in range(3):
                    weight_remote(index, kind, part).wait_send()
    for c in range(len(cuts)):
        own_out(c).wait_send()

    @pl.when(z == own_worker)
    def _():
        for c in range(len(cuts)):
            pass_out(c).wait_send()
        for kind in range(2):
            for index in range(len(moves)):
                gather_out(kind, index).wait_send()
        for unit in range(len(units)):
            for copy in far_copies(unit):
                copy.wait_send()

    for unit in range(len(units)):
        kv_copy(unit, 0, lane, y_peer).wait_send()
        kv_copy(unit, 1, lane, core_peer).wait_send()
        kv_copy(unit, 2, y_lane, core_peer).wait_send()
    for step in range(1, planes):
        pick_copy(step).wait_send()
    for index, (where, peer) in enumerate(partners):
        pick_lane(index, lane, peer).wait_send()


def fused(tokens, w_query, w_keyval, global_off, rand_dev, rand_sub):
    nseq = lax.axis_size("seq")
    ntok, width = tokens.shape
    planes = nseq // LANES
    nblk = ntok // BLOCK
    picked = -(-nseq // 16) * 16
    cols = H // planes * HD
    half = w_query.shape[0] // 2
    dev, sub = rand_dev.transpose(2, 1, 0), rand_sub.transpose(2, 1, 0)
    dma = pltpu.SemaphoreType.DMA
    cuts = chunks_of(ntok)
    units = planes - 1 + len(cuts)
    return pl.pallas_call(
        functools.partial(fused_kernel, planes),
        out_shape=jax.ShapeDtypeStruct((ntok, H * HD), jnp.bfloat16),
        in_specs=[pl.BlockSpec(memory_space=pl.ANY)] * 3
        + [pl.BlockSpec(memory_space=pltpu.SMEM)]
        + [pl.BlockSpec(memory_space=pl.ANY)] * 2,
        out_specs=pl.BlockSpec(memory_space=pl.ANY),
        scratch_shapes=[
            pltpu.VMEM((planes, ntok, width), jnp.bfloat16),
            pltpu.VMEM((2, planes, LANES, 2, half, 3 * cols), jnp.bfloat16),
            pltpu.VMEM((planes, ntok, cols), jnp.bfloat16),
            pltpu.VMEM((nseq * nblk, BLOCK, 2 * cols), jnp.bfloat16),
            pltpu.VMEM((planes, ntok, cols), jnp.bfloat16),
            pltpu.VMEM((planes * nblk, BLOCK, 2 * cols), jnp.bfloat16),
            pltpu.VMEM((LANES, planes, picked, ntok), jnp.bfloat16),
            pltpu.VMEM((planes, ntok, cols), jnp.bfloat16),
            pltpu.VMEM((picked, 2 * cols), jnp.float32),
            pltpu.SMEM(dev.shape, jnp.int32),
            pltpu.SMEM(sub.shape, jnp.int32),
            dma((3,)),
            dma((2, 2, 3)),
            dma((planes, 2, 3)),
            dma((2, 9)),
            dma((2, 9)),
            dma((2, len(cuts))),
            dma((planes, len(cuts))),
            dma((2, units)),
            dma((2, units)),
            dma((3, units)),
            dma((3, units)),
            dma((planes - 1,)),
            dma((planes,)),
            dma((3,)),
            dma((3,)),
            dma((planes - 1,)),
            dma((planes,)),
        ],
        compiler_params=pltpu.CompilerParams(
            collective_id=0, has_side_effects=True, vmem_limit_bytes=60 * 1024 * 1024
        ),
        cost_estimate=pl.CostEstimate(
            flops=2 * planes * ntok * width * 3 * cols,
            bytes_accessed=2 * planes * ntok * width,
            transcendentals=ntok * H * 400,
        ),
    )(tokens, w_query, w_keyval, global_off, dev, sub)


def solution(mesh):
    in_specs = (
        P(("groups", "seq"), None),
        P("seq", None),
        P("seq", None),
        P(("groups", "seq")),
        P("groups", None, None),
        P("groups", None, None),
    )
    out_specs = P(("groups", "seq"), None)
    nseq, groups = mesh.shape["seq"], mesh.shape["groups"]
    planes = nseq // LANES
    paired = groups == 2 and planes * LANES == nseq and planes == 4
    body = fused if paired else local
    return jax.shard_map(body, mesh=mesh, in_specs=in_specs, out_specs=out_specs, check_vma=False)
```

```python
import functools
import math

import jax
import jax.numpy as jnp
from jax import lax
from jax.experimental import pallas as pl
from jax.experimental.pallas import tpu as pltpu
from jax.sharding import PartitionSpec as P

H = 8
HD = 128
BLOCK = 64
R = 3
BLK_DEV = 4
LANES = 4
MESH = pl.DeviceIdType.MESH


def padded_2(block, sides, width):
    for axis, dim in sides:
        count = lax.axis_size(axis)
        forward = [(i, i + 1) for i in range(count - 1)]
        backward = [(target, source) for source, target in forward]
        low = lax.ppermute(
            lax.slice_in_dim(block, block.shape[dim] - width, None, axis=dim), axis, forward
        )
        high = lax.ppermute(lax.slice_in_dim(block, 0, width, axis=dim), axis, backward)
        block = jnp.concatenate([low, block, high], axis=dim)
    return block


def fold_rows(left, piece):
    return jnp.dot(left, piece, preferred_element_type=jnp.float32)


def local(tokens, w_query, w_keyval, global_off, rand_dev, rand_sub):
    ntok = tokens.shape[0]
    nseq = lax.axis_size("seq")
    me_index = lax.axis_index("seq")
    nblk = ntok // BLOCK
    inner = H * HD
    glob_rows = lax.all_gather(jnp.take(tokens, global_off, axis=0), "seq", axis=0, tiled=True)
    left_kv = jnp.concatenate([tokens, glob_rows], axis=0)
    query = fold_rows(tokens, lax.all_gather(w_query, "seq", axis=0, tiled=True))
    keyval = fold_rows(left_kv, lax.all_gather(w_keyval, "seq", axis=0, tiled=True))
    query = query.astype(jnp.bfloat16)
    keyval = keyval.astype(jnp.bfloat16)
    glob_kv = keyval[ntok:]
    keyval = keyval[:ntok]
    glob_kv = glob_kv.reshape(glob_kv.shape[0], 2, H, HD)
    padded = padded_2(keyval, (("seq", 0),), BLOCK)
    window = jnp.concatenate(
        [padded[j * BLOCK : j * BLOCK + ntok].reshape(nblk, BLOCK, 2, H, HD) for j in range(3)],
        axis=1,
    )
    capacity = max(2, 3 * BLK_DEV * H * R // (2 * nseq))
    nreq = nblk * H * R
    dev_all = rand_dev.reshape(nseq, nreq)
    sub_all = rand_sub.reshape(nseq, nreq)
    match = (dev_all == me_index).astype(jnp.int32)
    slot_all = jnp.cumsum(match, axis=1) - 1
    head_of = jnp.arange(nreq, dtype=jnp.int32) // R % H
    code_all = head_of[None, :] * nblk + sub_all
    picked = (match[:, None, :] == 1) & (
        slot_all[:, None, :] == jnp.arange(capacity, dtype=jnp.int32)[None, :, None]
    )
    source = jnp.sum(jnp.where(picked, code_all[:, None, :], 0), axis=2)
    tiles = (
        keyval.reshape(nblk, BLOCK, 2, H, HD)
        .transpose(3, 0, 1, 2, 4)
        .reshape(H * nblk, BLOCK, 2 * HD)
    )
    outgoing = jnp.take(tiles, source, axis=0)
    incoming = lax.all_to_all(outgoing, "seq", split_axis=0, concat_axis=0, tiled=True)
    my_dev = lax.dynamic_slice_in_dim(rand_dev, me_index * nblk, nblk, 0).reshape(nreq)
    onehot = (my_dev[:, None] == jnp.arange(nseq, dtype=jnp.int32)[None, :]).astype(jnp.int32)
    my_slot = jnp.sum(onehot * (jnp.cumsum(onehot, axis=0) - 1), axis=1)
    flat_index = my_dev * capacity + my_slot
    fetched = jnp.take(incoming.reshape(nseq * capacity, BLOCK, 2 * HD), flat_index, axis=0)
    fetched = fetched.reshape(nblk, H, R, BLOCK, 2, HD)
    scale = HD ** (-0.5)
    qry = query.reshape(nblk, BLOCK, H, HD)
    s_win = (
        jnp.einsum("bqhd,bkhd->bhqk", qry, window[:, :, 0], preferred_element_type=jnp.float32)
        * scale
    )
    s_rnd = (
        jnp.einsum(
            "bqhd,bhrkd->bhqrk", qry, fetched[:, :, :, :, 0], preferred_element_type=jnp.float32
        ).reshape(nblk, H, BLOCK, R * BLOCK)
        * scale
    )
    s_glb = (
        jnp.einsum("bqhd,ghd->bhqg", qry, glob_kv[:, 0], preferred_element_type=jnp.float32) * scale
    )
    blk_ids = me_index * nblk + jnp.arange(nblk, dtype=jnp.int32)
    left_ok = jnp.repeat((blk_ids > 0)[:, None], BLOCK, axis=1)
    right_ok = jnp.repeat((blk_ids < nseq * nblk - 1)[:, None], BLOCK, axis=1)
    middle_ok = jnp.ones((nblk, BLOCK), dtype=bool)
    window_ok = jnp.concatenate([left_ok, middle_ok, right_ok], axis=1)
    s_win = jnp.where(window_ok[:, None, None, :], s_win, -jnp.inf)
    scores = jnp.concatenate([s_win, s_rnd, s_glb], axis=3)
    highest = jnp.max(scores, axis=3, keepdims=True)
    expo = jnp.exp(scores - highest)
    weights = (expo / jnp.sum(expo, axis=3, keepdims=True)).astype(jnp.bfloat16)
    w_win = weights[..., : 3 * BLOCK]
    w_rnd = weights[..., 3 * BLOCK : 3 * BLOCK + R * BLOCK].reshape(nblk, H, BLOCK, R, BLOCK)
    w_glb = weights[..., 3 * BLOCK + R * BLOCK :]
    ctx = jnp.einsum("bhqk,bkhd->bqhd", w_win, window[:, :, 1], preferred_element_type=jnp.float32)
    ctx = ctx + jnp.einsum(
        "bhqrk,bhrkd->bqhd", w_rnd, fetched[:, :, :, :, 1], preferred_element_type=jnp.float32
    )
    ctx = ctx + jnp.einsum(
        "bhqg,ghd->bqhd", w_glb, glob_kv[:, 1], preferred_element_type=jnp.float32
    )
    return ctx.reshape(ntok, inner).astype(jnp.bfloat16)


def chunks_of(ntok):
    half, quarter = ntok // 2, ntok // 4
    return ((0, half), (half, quarter), (half + quarter, quarter))


def fused_kernel(
    planes, tok_hbm, wq_hbm, wkv_hbm, off_ref, dev_hbm, sub_hbm, out_ref,
    tok, wts, qry, kv, far_q, far_kv, picks, ctx, glob_sum, dev_ref, sub_ref,
    local_sem, w_send, w_recv, g_send, g_recv, t_send, t_recv, f_send, f_recv,
    k_send, k_recv, p_send, p_recv, o_send, o_recv, c_send, c_recv,
):
    ntok = tok_hbm.shape[0]
    nblk = ntok // BLOCK
    heads = H // planes
    cols = heads * HD
    half = wts.shape[4]
    x = lax.axis_index("groups")
    me = lax.axis_index("seq")
    z = me // LANES
    lane = me % LANES
    core_lane = lane + 1 - 2 * (lane % 2)
    y_lane = (lane + 2) % LANES
    diag_lane = (core_lane + 2) % LANES
    mid = planes // 2
    workers, ends = (mid - 1, mid), (0, planes - 1)
    lower = z < mid
    own_worker = jnp.where(lower, workers[0], workers[1])
    own_end = jnp.where(lower, ends[0], ends[1])
    far_worker = jnp.where(lower, workers[1], workers[0])
    far_end = jnp.where(lower, ends[1], ends[0])
    mate = jnp.where(z == own_worker, own_end, own_worker)
    order = [own_worker, own_end, far_worker, far_end]

    def at(plane, where):
        return {"seq": plane * LANES + where}

    x_peer = {"groups": 1 - x}
    core_peer = at(z, core_lane)
    y_peer = at(z, y_lane)
    diag_peer = at(z, diag_lane)
    partners = ((y_lane, y_peer), (core_lane, core_peer), (diag_lane, diag_peer))

    def remote(src, dst, send, recv, peer):
        return pltpu.make_async_remote_copy(
            src_ref=src, dst_ref=dst, send_sem=send, recv_sem=recv, device_id=peer,
            device_id_type=MESH,
        )

    dev_in = pltpu.make_async_copy(dev_hbm, dev_ref, local_sem.at[0])
    dev_in.start()
    sub_in = pltpu.make_async_copy(sub_hbm, sub_ref, local_sem.at[1])
    sub_in.start()
    tok_in = pltpu.make_async_copy(tok_hbm, tok.at[z], local_sem.at[2])
    tok_in.start()

    barrier = pltpu.get_barrier_semaphore()
    for step in range(1, planes):
        pl.semaphore_signal(
            barrier, inc=1, device_id=at((z + step) % planes, lane), device_id_type=MESH
        )
    for peer in (x_peer, core_peer, y_peer, diag_peer):
        pl.semaphore_signal(barrier, inc=1, device_id=peer, device_id_type=MESH)
    pl.semaphore_wait(barrier, planes - 1 + 4)

    def weight_refs(index, kind, part):
        plane = (ends, workers)[kind][index]
        rows = pl.ds(pl.multiple_of(x * half, half), half)
        first = (0, 0, H * HD)[part] + plane * cols
        src = (wq_hbm, wkv_hbm, wkv_hbm)[part].at[rows, pl.ds(first, cols)]
        return src, wts.at[kind, z, lane, x, :, pl.ds(part * cols, cols)]

    def weight_remote(index, kind, part):
        src, dst = weight_refs(index, kind, part)
        return remote(
            src, dst, w_send.at[index, kind, part], w_recv.at[z, kind, part],
            at(workers[index], lane),
        )

    def weights_out(kind):
        for index in range(2):
            for part in range(3):
                @pl.when(z != workers[index])
                def _():
                    weight_remote(index, kind, part).start()

                @pl.when(z == workers[index])
                def _():
                    src, dst = weight_refs(index, kind, part)
                    pltpu.make_async_copy(src, dst, w_recv.at[z, kind, part]).start()

    def weights_in(kind):
        for plane in range(planes):
            for part in range(3):
                here = wts.at[kind, plane, lane, x, :, pl.ds(part * cols, cols)]
                remote(here, here, w_send.at[0, kind, part], w_recv.at[plane, kind, part], core_peer).wait_recv()

    towards = jnp.where(lower, z + 1, z - 1)
    cuts = chunks_of(ntok)
    chunks = [pl.ds(first, count) for first, count in cuts]

    def own_out(c):
        return remote(
            tok_hbm.at[chunks[c]], tok.at[z, chunks[c]], t_send.at[0, c], t_recv.at[z, c],
            at(towards, lane),
        )

    def pass_out(c):
        ref = tok.at[own_end, chunks[c]]
        return remote(ref, ref, t_send.at[1, c], t_recv.at[own_end, c], at(towards, lane))

    def tok_wait(plane, c):
        ref = tok.at[plane, chunks[c]]
        remote(ref, ref, t_send.at[0, c], t_recv.at[plane, c], core_peer).wait_recv()

    weights_out(0)
    weights_out(1)
    own_out(0).start()

    at_row = lax.broadcasted_iota(jnp.int32, picks.shape[2:], 0) == me
    at_event = lax.broadcasted_iota(jnp.int32, picks.shape[2:], 1) == off_ref[0]
    picks[lane, z] = jnp.where(at_row & at_event, 1.0, 0.0).astype(jnp.bfloat16)

    def pick_copy(step):
        return remote(picks.at[lane, z], picks.at[lane, z], p_send.at[step - 1], p_recv.at[z], at((z + step) % planes, lane))

    for step in range(1, planes):
        pick_copy(step).start()

    width = 3 * cols
    every, left, right = pl.ds(0, width), pl.ds(0, width // 2), pl.ds(width // 2, width // 2)
    moves = (
        (x, lane, every, x_peer, 1 - x, lane),
        (x, lane, every, y_peer, x, y_lane),
        (x, lane, every, core_peer, x, core_lane),
        (1 - x, lane, left, y_peer, 1 - x, y_lane),
        (1 - x, lane, every, core_peer, 1 - x, core_lane),
        (x, y_lane, right, x_peer, 1 - x, y_lane),
        (x, y_lane, every, core_peer, x, diag_lane),
        (1 - x, y_lane, left, core_peer, 1 - x, diag_lane),
        (1 - x, y_lane, right, core_peer, 1 - x, diag_lane),
    )

    def gather_out(kind, index):
        group, where, part, peer = moves[index][:4]
        ref = wts.at[kind, :, where, group, :, part]
        return remote(ref, ref, g_send.at[kind, index], g_recv.at[kind, index], peer)

    def gather_wait(kind, index):
        part, peer, group, where = moves[index][2:]
        ref = wts.at[kind, :, where, group, :, part]
        remote(ref, ref, g_send.at[kind, index], g_recv.at[kind, index], peer).wait_recv()

    def gather_first(kind):
        weights_in(kind)
        for index in range(3):
            gather_out(kind, index).start()

    def gather_second(kind):
        gather_wait(kind, 0)
        gather_out(kind, 3).start()
        gather_out(kind, 4).start()
        gather_wait(kind, 1)
        gather_out(kind, 5).start()
        gather_out(kind, 6).start()

    def gather_last(kind):
        gather_wait(kind, 3)
        gather_out(kind, 7).start()
        gather_wait(kind, 5)
        gather_out(kind, 8).start()
        for index in (2, 4, 6, 7, 8):
            gather_wait(kind, index)

    def kv_rows(ref, plane, where, first=0, count=nblk):
        return ref.at[pl.ds((plane * LANES + where) * nblk + first, count)]

    units = [(i, 0, ntok) for i in range(planes - 1)]
    units += [(planes - 1, first, count) for first, count in cuts]

    def unit_kv(unit, where):
        index, first, count = units[unit]
        return kv_rows(kv, order[index], where, first // BLOCK, count // BLOCK)

    def unit_q(unit):
        index, first, count = units[unit]
        return qry.at[order[index], pl.ds(first, count)]

    def kv_copy(unit, which, where, peer):
        ref = unit_kv(unit, where)
        return remote(ref, ref, k_send.at[which, unit], k_recv.at[which, unit], peer)

    def kv_out(unit):
        kv_copy(unit, 0, lane, y_peer).start()
        kv_copy(unit, 1, lane, core_peer).start()

    def kv_forward(unit):
        kv_copy(unit, 0, y_lane, y_peer).wait_recv()
        kv_copy(unit, 2, y_lane, core_peer).start()

    def project(unit, kind):
        index, first, count = units[unit]
        weights = wts[kind].reshape(-1, width)
        rows = tok[order[index], pl.ds(first, count)]
        res = jnp.dot(rows, weights, preferred_element_type=jnp.float32).astype(jnp.bfloat16)
        return res[:, :cols], res[:, cols:].reshape(count // BLOCK, BLOCK, 2 * cols)

    def far_refs(unit):
        index, first, count = units[unit]
        blocks = pl.ds(index * nblk + first // BLOCK, count // BLOCK)
        return far_q.at[index, pl.ds(first, count)], far_kv.at[blocks]

    def far_copies(unit):
        from_q, from_kv = far_refs(unit)
        return (
            remote(from_kv, unit_kv(unit, lane), f_send.at[1, unit], f_recv.at[1, unit], at(mate, lane)),
            remote(from_q, unit_q(unit), f_send.at[0, unit], f_recv.at[0, unit], at(mate, lane)),
        )

    def project_far(unit):
        from_q, from_kv = far_refs(unit)
        from_q[...], from_kv[...] = project(unit, 0)
        for copy in far_copies(unit):
            copy.start()

    def project_own(unit):
        unit_q(unit)[...], unit_kv(unit, lane)[...] = project(unit, 1)
        kv_out(unit)

    def pick_lane(index, where, peer):
        return remote(picks.at[where], picks.at[where], o_send.at[index], o_recv.at[index], peer)

    def picks_first():
        for step in range(1, planes):
            source = (z + step) % planes
            ref = picks.at[lane, source]
            remote(ref, ref, p_send.at[0], p_recv.at[source], core_peer).wait_recv()
        for index, (where, peer) in enumerate(partners):
            pick_lane(index, lane, peer).start()

    def picks_last():
        for index, (where, peer) in enumerate(partners):
            pick_lane(index, where, peer).wait_recv()

    def glob_add(index):
        for unit in [u for u in range(len(units)) if units[u][0] == index]:
            kv_copy(unit, 1, core_lane, core_peer).wait_recv()
            kv_copy(unit, 2, diag_lane, core_peer).wait_recv()
        total = jnp.zeros(glob_sum.shape, jnp.float32) if index == 0 else glob_sum[...]
        for where in range(LANES):
            rows = kv_rows(kv, order[index], where)[...].reshape(ntok, 2 * cols)
            total = total + jnp.dot(
                picks[where, order[index]], rows, preferred_element_type=jnp.float32
            )
        glob_sum[...] = total

    last = len(units) - 1

    @pl.when(z == own_worker)
    def _():
        gather_first(0)
        own_out(1).start()
        gather_second(0)
        own_out(2).start()
        tok_in.wait()
        tok_wait(own_end, 0)
        pass_out(0).start()
        gather_first(1)
        gather_last(0)
        project_far(0)
        for c in range(1, len(cuts)):
            tok_wait(own_end, c)
            pass_out(c).start()
        project_far(1)
        gather_second(1)
        picks_first()
        for c in range(len(cuts)):
            tok_wait(far_worker, c)
        project_far(2)
        gather_last(1)
        project_own(0)
        project_own(1)
        kv_forward(0)
        project_own(2)
        kv_forward(1)
        picks_last()
        for unit in range(planes - 1, len(units)):
            tok_wait(far_end, unit - planes + 1)
            project_far(unit)
            project_own(unit)
            kv_forward(unit - 1)
            if unit < last:
                glob_add(unit - planes + 1)
        glob_add(planes - 2)
        kv_forward(last)

    @pl.when(z != own_worker)
    def _():
        own_out(1).start()
        own_out(2).start()
        tok_in.wait()
        picks_first()
        picks_last()
        for unit in range(len(units)):
            here = unit_kv(unit, lane)
            remote(here, here, f_send.at[1, unit], f_recv.at[1, unit], core_peer).wait_recv()
            kv_out(unit)
            if unit:
                kv_forward(unit - 1)
            if planes - 1 <= unit < last:
                glob_add(unit - planes + 1)
        glob_add(planes - 2)
        kv_forward(last)
        for unit in range(len(units)):
            here = unit_q(unit)
            remote(here, here, f_send.at[0, unit], f_recv.at[0, unit], core_peer).wait_recv()

    glob_add(planes - 1)
    glob = glob_sum[: planes * LANES].astype(jnp.bfloat16)
    dev_in.wait()
    sub_in.wait()
    total_blocks = planes * LANES * nblk
    scale = HD ** (-0.5) * math.log2(math.e)
    keys = (3 + R) * BLOCK + glob.shape[0]
    key_row = lax.broadcasted_iota(jnp.int32, (keys, heads * BLOCK), 0)

    def ctx_copy(plane, index):
        return remote(
            ctx.at[plane],
            out_ref.at[:, pl.ds(pl.multiple_of(z * cols, cols), cols)],
            c_send.at[index], c_recv.at[z], at(plane, lane),
        )

    def attend(plane):
        for sub in range(nblk):
            block = (plane * LANES + lane) * nblk + sub
            starts = [
                jnp.maximum(block - 1, 0),
                block,
                jnp.minimum(block + 1, total_blocks - 1),
            ]
            q_rows = slice(sub * BLOCK, (sub + 1) * BLOCK)
            picked = []
            for j in range(R):
                picked.append([
                    dev_ref[j, z * heads + h, block] * nblk + sub_ref[j, z * heads + h, block]
                    for h in range(heads)
                ])

            def side_by_side(first):
                rows = [kv[w, :, first : first + cols] for w in starts]
                for choice in picked:
                    rows.append(jnp.concatenate(
                        [
                            kv[choice[h], :, first + h * HD : first + (h + 1) * HD]
                            for h in range(heads)
                        ],
                        axis=1,
                    ))
                rows.append(glob[:, first : first + cols])
                return jnp.concatenate(rows, axis=0)

            queries = jnp.concatenate(
                [
                    jnp.concatenate(
                        [
                            qry[plane, q_rows, k * HD : (k + 1) * HD]
                            if k == h
                            else jnp.zeros((BLOCK, HD), jnp.bfloat16)
                            for k in range(heads)
                        ],
                        axis=1,
                    )
                    for h in range(heads)
                ],
                axis=0,
            )
            score = lax.dot_general(
                side_by_side(0), queries, (((1,), (1,)), ((), ())),
                preferred_element_type=jnp.float32,
            )
            if sub == 0:
                score = jnp.where((key_row < BLOCK) & (block == 0), -jnp.inf, score)
            if sub == nblk - 1:
                after = (key_row >= 2 * BLOCK) & (key_row < 3 * BLOCK)
                score = jnp.where(after & (block == total_blocks - 1), -jnp.inf, score)
            expo = jnp.exp2((score - jnp.max(score, axis=0, keepdims=True)) * scale)
            soft = (expo * (1.0 / jnp.sum(expo, axis=0, keepdims=True))).astype(jnp.bfloat16)
            res = lax.dot_general(
                soft, side_by_side(cols), (((0,), (0,)), ((), ())),
                preferred_element_type=jnp.float32,
            ).astype(jnp.bfloat16)
            for h in range(heads):
                ctx[plane, q_rows, h * HD : (h + 1) * HD] = res[
                    h * BLOCK : (h + 1) * BLOCK, h * HD : (h + 1) * HD
                ]

    others = (far_end, far_worker, mate)
    for index, plane in enumerate(others):
        attend(plane)
        ctx_copy(plane, index).start()
    attend(z)
    own = pltpu.make_async_copy(
        ctx.at[z], out_ref.at[:, pl.ds(pl.multiple_of(z * cols, cols), cols)], local_sem.at[0]
    )
    own.start()
    own.wait()

    for index, plane in enumerate(others):
        ctx_copy(plane, index).wait_send()
        there = out_ref.at[:, pl.ds(pl.multiple_of(plane * cols, cols), cols)]
        remote(ctx.at[plane], there, c_send.at[index], c_recv.at[plane], core_peer).wait_recv()
    for index in range(2):
        @pl.when(z != workers[index])
        def _():
            for kind in range(2):
                for part in range(3):
                    weight_remote(index, kind, part).wait_send()
    for c in range(len(cuts)):
        own_out(c).wait_send()

    @pl.when(z == own_worker)
    def _():
        for c in range(len(cuts)):
            pass_out(c).wait_send()
        for kind in range(2):
            for index in range(len(moves)):
                gather_out(kind, index).wait_send()
        for unit in range(len(units)):
            for copy in far_copies(unit):
                copy.wait_send()

    for unit in range(len(units)):
        kv_copy(unit, 0, lane, y_peer).wait_send()
        kv_copy(unit, 1, lane, core_peer).wait_send()
        kv_copy(unit, 2, y_lane, core_peer).wait_send()
    for step in range(1, planes):
        pick_copy(step).wait_send()
    for index, (where, peer) in enumerate(partners):
        pick_lane(index, lane, peer).wait_send()


def fused(tokens, w_query, w_keyval, global_off, rand_dev, rand_sub):
    nseq = lax.axis_size("seq")
    ntok, width = tokens.shape
    planes = nseq // LANES
    nblk = ntok // BLOCK
    picked = -(-nseq // 16) * 16
    cols = H // planes * HD
    half = w_query.shape[0] // 2
    dev, sub = rand_dev.transpose(2, 1, 0), rand_sub.transpose(2, 1, 0)
    dma = pltpu.SemaphoreType.DMA
    cuts = chunks_of(ntok)
    units = planes - 1 + len(cuts)
    return pl.pallas_call(
        functools.partial(fused_kernel, planes),
        out_shape=jax.ShapeDtypeStruct((ntok, H * HD), jnp.bfloat16),
        in_specs=[pl.BlockSpec(memory_space=pl.ANY)] * 3
        + [pl.BlockSpec(memory_space=pltpu.SMEM)]
        + [pl.BlockSpec(memory_space=pl.ANY)] * 2,
        out_specs=pl.BlockSpec(memory_space=pl.ANY),
        scratch_shapes=[
            pltpu.VMEM((planes, ntok, width), jnp.bfloat16),
            pltpu.VMEM((2, planes, LANES, 2, half, 3 * cols), jnp.bfloat16),
            pltpu.VMEM((planes, ntok, cols), jnp.bfloat16),
            pltpu.VMEM((nseq * nblk, BLOCK, 2 * cols), jnp.bfloat16),
            pltpu.VMEM((planes, ntok, cols), jnp.bfloat16),
            pltpu.VMEM((planes * nblk, BLOCK, 2 * cols), jnp.bfloat16),
            pltpu.VMEM((LANES, planes, picked, ntok), jnp.bfloat16),
            pltpu.VMEM((planes, ntok, cols), jnp.bfloat16),
            pltpu.VMEM((picked, 2 * cols), jnp.float32),
            pltpu.SMEM(dev.shape, jnp.int32),
            pltpu.SMEM(sub.shape, jnp.int32),
            dma((3,)),
            dma((2, 2, 3)),
            dma((planes, 2, 3)),
            dma((2, 9)),
            dma((2, 9)),
            dma((2, len(cuts))),
            dma((planes, len(cuts))),
            dma((2, units)),
            dma((2, units)),
            dma((3, units)),
            dma((3, units)),
            dma((planes - 1,)),
            dma((planes,)),
            dma((3,)),
            dma((3,)),
            dma((planes - 1,)),
            dma((planes,)),
        ],
        compiler_params=pltpu.CompilerParams(
            collective_id=0, has_side_effects=True, vmem_limit_bytes=60 * 1024 * 1024
        ),
        cost_estimate=pl.CostEstimate(
            flops=2 * planes * ntok * width * 3 * cols,
            bytes_accessed=2 * planes * ntok * width,
            transcendentals=ntok * H * 400,
        ),
    )(tokens, w_query, w_keyval, global_off, dev, sub)


def solution(mesh):
    in_specs = (
        P(("groups", "seq"), None),
        P("seq", None),
        P("seq", None),
        P(("groups", "seq")),
        P("groups", None, None),
        P("groups", None, None),
    )
    out_specs = P(("groups", "seq"), None)
    nseq, groups = mesh.shape["seq"], mesh.shape["groups"]
    planes = nseq // LANES
    paired = groups == 2 and planes * LANES == nseq and planes == 4
    body = fused if paired else local
    return jax.shard_map(body, mesh=mesh, in_specs=in_specs, out_specs=out_specs, check_vma=False)
```

```python
import functools
import math

import jax
import jax.numpy as jnp
from jax import lax
from jax.experimental import pallas as pl
from jax.experimental.pallas import tpu as pltpu
from jax.sharding import PartitionSpec as P

H = 8
HD = 128
BLOCK = 64
R = 3
BLK_DEV = 4
LANES = 4
MESH = pl.DeviceIdType.MESH


def padded_2(block, sides, width):
    for axis, dim in sides:
        count = lax.axis_size(axis)
        forward = [(i, i + 1) for i in range(count - 1)]
        backward = [(target, source) for source, target in forward]
        low = lax.ppermute(
            lax.slice_in_dim(block, block.shape[dim] - width, None, axis=dim), axis, forward
        )
        high = lax.ppermute(lax.slice_in_dim(block, 0, width, axis=dim), axis, backward)
        block = jnp.concatenate([low, block, high], axis=dim)
    return block


def fold_rows(left, piece):
    return jnp.dot(left, piece, preferred_element_type=jnp.float32)


def local(tokens, w_query, w_keyval, global_off, rand_dev, rand_sub):
    ntok = tokens.shape[0]
    nseq = lax.axis_size("seq")
    me_index = lax.axis_index("seq")
    nblk = ntok // BLOCK
    inner = H * HD
    glob_rows = lax.all_gather(jnp.take(tokens, global_off, axis=0), "seq", axis=0, tiled=True)
    left_kv = jnp.concatenate([tokens, glob_rows], axis=0)
    query = fold_rows(tokens, lax.all_gather(w_query, "seq", axis=0, tiled=True))
    keyval = fold_rows(left_kv, lax.all_gather(w_keyval, "seq", axis=0, tiled=True))
    query = query.astype(jnp.bfloat16)
    keyval = keyval.astype(jnp.bfloat16)
    glob_kv = keyval[ntok:]
    keyval = keyval[:ntok]
    glob_kv = glob_kv.reshape(glob_kv.shape[0], 2, H, HD)
    padded = padded_2(keyval, (("seq", 0),), BLOCK)
    window = jnp.concatenate(
        [padded[j * BLOCK : j * BLOCK + ntok].reshape(nblk, BLOCK, 2, H, HD) for j in range(3)],
        axis=1,
    )
    capacity = max(2, 3 * BLK_DEV * H * R // (2 * nseq))
    nreq = nblk * H * R
    dev_all = rand_dev.reshape(nseq, nreq)
    sub_all = rand_sub.reshape(nseq, nreq)
    match = (dev_all == me_index).astype(jnp.int32)
    slot_all = jnp.cumsum(match, axis=1) - 1
    head_of = jnp.arange(nreq, dtype=jnp.int32) // R % H
    code_all = head_of[None, :] * nblk + sub_all
    picked = (match[:, None, :] == 1) & (
        slot_all[:, None, :] == jnp.arange(capacity, dtype=jnp.int32)[None, :, None]
    )
    source = jnp.sum(jnp.where(picked, code_all[:, None, :], 0), axis=2)
    tiles = (
        keyval.reshape(nblk, BLOCK, 2, H, HD)
        .transpose(3, 0, 1, 2, 4)
        .reshape(H * nblk, BLOCK, 2 * HD)
    )
    outgoing = jnp.take(tiles, source, axis=0)
    incoming = lax.all_to_all(outgoing, "seq", split_axis=0, concat_axis=0, tiled=True)
    my_dev = lax.dynamic_slice_in_dim(rand_dev, me_index * nblk, nblk, 0).reshape(nreq)
    onehot = (my_dev[:, None] == jnp.arange(nseq, dtype=jnp.int32)[None, :]).astype(jnp.int32)
    my_slot = jnp.sum(onehot * (jnp.cumsum(onehot, axis=0) - 1), axis=1)
    flat_index = my_dev * capacity + my_slot
    fetched = jnp.take(incoming.reshape(nseq * capacity, BLOCK, 2 * HD), flat_index, axis=0)
    fetched = fetched.reshape(nblk, H, R, BLOCK, 2, HD)
    scale = HD ** (-0.5)
    qry = query.reshape(nblk, BLOCK, H, HD)
    s_win = (
        jnp.einsum("bqhd,bkhd->bhqk", qry, window[:, :, 0], preferred_element_type=jnp.float32)
        * scale
    )
    s_rnd = (
        jnp.einsum(
            "bqhd,bhrkd->bhqrk", qry, fetched[:, :, :, :, 0], preferred_element_type=jnp.float32
        ).reshape(nblk, H, BLOCK, R * BLOCK)
        * scale
    )
    s_glb = (
        jnp.einsum("bqhd,ghd->bhqg", qry, glob_kv[:, 0], preferred_element_type=jnp.float32) * scale
    )
    blk_ids = me_index * nblk + jnp.arange(nblk, dtype=jnp.int32)
    left_ok = jnp.repeat((blk_ids > 0)[:, None], BLOCK, axis=1)
    right_ok = jnp.repeat((blk_ids < nseq * nblk - 1)[:, None], BLOCK, axis=1)
    middle_ok = jnp.ones((nblk, BLOCK), dtype=bool)
    window_ok = jnp.concatenate([left_ok, middle_ok, right_ok], axis=1)
    s_win = jnp.where(window_ok[:, None, None, :], s_win, -jnp.inf)
    scores = jnp.concatenate([s_win, s_rnd, s_glb], axis=3)
    highest = jnp.max(scores, axis=3, keepdims=True)
    expo = jnp.exp(scores - highest)
    weights = (expo / jnp.sum(expo, axis=3, keepdims=True)).astype(jnp.bfloat16)
    w_win = weights[..., : 3 * BLOCK]
    w_rnd = weights[..., 3 * BLOCK : 3 * BLOCK + R * BLOCK].reshape(nblk, H, BLOCK, R, BLOCK)
    w_glb = weights[..., 3 * BLOCK + R * BLOCK :]
    ctx = jnp.einsum("bhqk,bkhd->bqhd", w_win, window[:, :, 1], preferred_element_type=jnp.float32)
    ctx = ctx + jnp.einsum(
        "bhqrk,bhrkd->bqhd", w_rnd, fetched[:, :, :, :, 1], preferred_element_type=jnp.float32
    )
    ctx = ctx + jnp.einsum(
        "bhqg,ghd->bqhd", w_glb, glob_kv[:, 1], preferred_element_type=jnp.float32
    )
    return ctx.reshape(ntok, inner).astype(jnp.bfloat16)


def chunks_of(ntok):
    half, quarter = ntok // 2, ntok // 4
    return ((0, half), (half, quarter), (half + quarter, quarter))


def fused_kernel(
    planes, tok_hbm, wq_hbm, wkv_hbm, off_ref, dev_hbm, sub_hbm, out_ref,
    tok, wts, qry, kv, far_q, far_kv, picks, ctx, glob_sum, dev_ref, sub_ref,
    local_sem, w_send, w_recv, g_send, g_recv, t_send, t_recv, f_send, f_recv,
    k_send, k_recv, p_send, p_recv, o_send, o_recv, c_send, c_recv,
):
    ntok = tok_hbm.shape[0]
    nblk = ntok // BLOCK
    heads = H // planes
    cols = heads * HD
    half = wts.shape[4]
    x = lax.axis_index("groups")
    me = lax.axis_index("seq")
    z = me // LANES
    lane = me % LANES
    core_lane = lane + 1 - 2 * (lane % 2)
    y_lane = (lane + 2) % LANES
    diag_lane = (core_lane + 2) % LANES
    mid = planes // 2
    workers, ends = (mid - 1, mid), (0, planes - 1)
    lower = z < mid
    own_worker = jnp.where(lower, workers[0], workers[1])
    own_end = jnp.where(lower, ends[0], ends[1])
    far_worker = jnp.where(lower, workers[1], workers[0])
    far_end = jnp.where(lower, ends[1], ends[0])
    mate = jnp.where(z == own_worker, own_end, own_worker)
    order = [own_worker, own_end, far_worker, far_end]

    def at(plane, where):
        return {"seq": plane * LANES + where}

    x_peer = {"groups": 1 - x}
    core_peer = at(z, core_lane)
    y_peer = at(z, y_lane)
    diag_peer = at(z, diag_lane)
    partners = ((y_lane, y_peer), (core_lane, core_peer), (diag_lane, diag_peer))

    def remote(src, dst, send, recv, peer):
        return pltpu.make_async_remote_copy(
            src_ref=src, dst_ref=dst, send_sem=send, recv_sem=recv, device_id=peer,
            device_id_type=MESH,
        )

    dev_in = pltpu.make_async_copy(dev_hbm, dev_ref, local_sem.at[0])
    dev_in.start()
    sub_in = pltpu.make_async_copy(sub_hbm, sub_ref, local_sem.at[1])
    sub_in.start()
    tok_in = pltpu.make_async_copy(tok_hbm, tok.at[z], local_sem.at[2])
    tok_in.start()

    barrier = pltpu.get_barrier_semaphore()
    for step in range(1, planes):
        pl.semaphore_signal(
            barrier, inc=1, device_id=at((z + step) % planes, lane), device_id_type=MESH
        )
    for peer in (x_peer, core_peer, y_peer, diag_peer):
        pl.semaphore_signal(barrier, inc=1, device_id=peer, device_id_type=MESH)
    pl.semaphore_wait(barrier, planes - 1 + 4)

    def weight_refs(index, kind, part):
        plane = (ends, workers)[kind][index]
        rows = pl.ds(pl.multiple_of(x * half, half), half)
        first = (0, 0, H * HD)[part] + plane * cols
        src = (wq_hbm, wkv_hbm, wkv_hbm)[part].at[rows, pl.ds(first, cols)]
        return src, wts.at[kind, z, lane, x, :, pl.ds(part * cols, cols)]

    def weight_remote(index, kind, part):
        src, dst = weight_refs(index, kind, part)
        return remote(
            src, dst, w_send.at[index, kind, part], w_recv.at[z, kind, part],
            at(workers[index], lane),
        )

    def weights_out(kind):
        for index in range(2):
            for part in range(3):
                @pl.when(z != workers[index])
                def _():
                    weight_remote(index, kind, part).start()

                @pl.when(z == workers[index])
                def _():
                    src, dst = weight_refs(index, kind, part)
                    pltpu.make_async_copy(src, dst, w_recv.at[z, kind, part]).start()

    def weights_in(kind):
        for plane in range(planes):
            for part in range(3):
                here = wts.at[kind, plane, lane, x, :, pl.ds(part * cols, cols)]
                remote(here, here, w_send.at[0, kind, part], w_recv.at[plane, kind, part], core_peer).wait_recv()

    towards = jnp.where(lower, z + 1, z - 1)
    cuts = chunks_of(ntok)
    chunks = [pl.ds(first, count) for first, count in cuts]

    def own_out(c):
        return remote(
            tok_hbm.at[chunks[c]], tok.at[z, chunks[c]], t_send.at[0, c], t_recv.at[z, c],
            at(towards, lane),
        )

    def pass_out(c):
        ref = tok.at[own_end, chunks[c]]
        return remote(ref, ref, t_send.at[1, c], t_recv.at[own_end, c], at(towards, lane))

    def tok_wait(plane, c):
        ref = tok.at[plane, chunks[c]]
        remote(ref, ref, t_send.at[0, c], t_recv.at[plane, c], core_peer).wait_recv()

    weights_out(0)
    weights_out(1)
    own_out(0).start()

    at_row = lax.broadcasted_iota(jnp.int32, picks.shape[2:], 0) == me
    at_event = lax.broadcasted_iota(jnp.int32, picks.shape[2:], 1) == off_ref[0]
    picks[lane, z] = jnp.where(at_row & at_event, 1.0, 0.0).astype(jnp.bfloat16)

    def pick_copy(step):
        return remote(picks.at[lane, z], picks.at[lane, z], p_send.at[step - 1], p_recv.at[z], at((z + step) % planes, lane))

    for step in range(1, planes):
        pick_copy(step).start()

    width = 3 * cols
    every, left, right = pl.ds(0, width), pl.ds(0, width // 2), pl.ds(width // 2, width // 2)
    moves = (
        (x, lane, every, x_peer, 1 - x, lane),
        (x, lane, every, y_peer, x, y_lane),
        (x, lane, every, core_peer, x, core_lane),
        (1 - x, lane, left, y_peer, 1 - x, y_lane),
        (1 - x, lane, every, core_peer, 1 - x, core_lane),
        (x, y_lane, right, x_peer, 1 - x, y_lane),
        (x, y_lane, every, core_peer, x, diag_lane),
        (1 - x, y_lane, left, core_peer, 1 - x, diag_lane),
        (1 - x, y_lane, right, core_peer, 1 - x, diag_lane),
    )

    def gather_out(kind, index):
        group, where, part, peer = moves[index][:4]
        ref = wts.at[kind, :, where, group, :, part]
        return remote(ref, ref, g_send.at[kind, index], g_recv.at[kind, index], peer)

    def gather_wait(kind, index):
        part, peer, group, where = moves[index][2:]
        ref = wts.at[kind, :, where, group, :, part]
        remote(ref, ref, g_send.at[kind, index], g_recv.at[kind, index], peer).wait_recv()

    def gather_first(kind):
        weights_in(kind)
        for index in range(3):
            gather_out(kind, index).start()

    def gather_second(kind):
        gather_wait(kind, 0)
        gather_out(kind, 3).start()
        gather_out(kind, 4).start()
        gather_wait(kind, 1)
        gather_out(kind, 5).start()
        gather_out(kind, 6).start()

    def gather_last(kind):
        gather_wait(kind, 3)
        gather_out(kind, 7).start()
        gather_wait(kind, 5)
        gather_out(kind, 8).start()
        for index in (2, 4, 6, 7, 8):
            gather_wait(kind, index)

    def kv_rows(ref, plane, where, first=0, count=nblk):
        return ref.at[pl.ds((plane * LANES + where) * nblk + first, count)]

    units = [(i, 0, ntok) for i in range(planes - 1)]
    units += [(planes - 1, first, count) for first, count in cuts]

    def unit_kv(unit, where):
        index, first, count = units[unit]
        return kv_rows(kv, order[index], where, first // BLOCK, count // BLOCK)

    def unit_q(unit):
        index, first, count = units[unit]
        return qry.at[order[index], pl.ds(first, count)]

    def kv_copy(unit, which, where, peer):
        ref = unit_kv(unit, where)
        return remote(ref, ref, k_send.at[which, unit], k_recv.at[which, unit], peer)

    def kv_out(unit):
        kv_copy(unit, 0, lane, y_peer).start()
        kv_copy(unit, 1, lane, core_peer).start()

    def kv_forward(unit):
        kv_copy(unit, 0, y_lane, y_peer).wait_recv()
        kv_copy(unit, 2, y_lane, core_peer).start()

    def project(unit, kind):
        index, first, count = units[unit]
        weights = wts[kind].reshape(-1, width)
        rows = tok[order[index], pl.ds(first, count)]
        res = jnp.dot(rows, weights, preferred_element_type=jnp.float32).astype(jnp.bfloat16)
        return res[:, :cols], res[:, cols:].reshape(count // BLOCK, BLOCK, 2 * cols)

    def far_refs(unit):
        index, first, count = units[unit]
        blocks = pl.ds(index * nblk + first // BLOCK, count // BLOCK)
        return far_q.at[index, pl.ds(first, count)], far_kv.at[blocks]

    def far_copies(unit):
        from_q, from_kv = far_refs(unit)
        return (
            remote(from_kv, unit_kv(unit, lane), f_send.at[1, unit], f_recv.at[1, unit], at(mate, lane)),
            remote(from_q, unit_q(unit), f_send.at[0, unit], f_recv.at[0, unit], at(mate, lane)),
        )

    def project_far(unit):
        from_q, from_kv = far_refs(unit)
        from_q[...], from_kv[...] = project(unit, 0)
        far_copies(unit)[0].start()

    def project_own(unit):
        unit_q(unit)[...], unit_kv(unit, lane)[...] = project(unit, 1)
        kv_out(unit)

    def pick_lane(index, where, peer):
        return remote(picks.at[where], picks.at[where], o_send.at[index], o_recv.at[index], peer)

    def picks_first():
        for step in range(1, planes):
            source = (z + step) % planes
            ref = picks.at[lane, source]
            remote(ref, ref, p_send.at[0], p_recv.at[source], core_peer).wait_recv()
        for index, (where, peer) in enumerate(partners):
            pick_lane(index, lane, peer).start()

    def picks_last():
        for index, (where, peer) in enumerate(partners):
            pick_lane(index, where, peer).wait_recv()

    def glob_add(index):
        for unit in [u for u in range(len(units)) if units[u][0] == index]:
            kv_copy(unit, 1, core_lane, core_peer).wait_recv()
            kv_copy(unit, 2, diag_lane, core_peer).wait_recv()
        total = jnp.zeros(glob_sum.shape, jnp.float32) if index == 0 else glob_sum[...]
        for where in range(LANES):
            rows = kv_rows(kv, order[index], where)[...].reshape(ntok, 2 * cols)
            total = total + jnp.dot(
                picks[where, order[index]], rows, preferred_element_type=jnp.float32
            )
        glob_sum[...] = total

    last = len(units) - 1

    @pl.when(z == own_worker)
    def _():
        gather_first(0)
        own_out(1).start()
        gather_second(0)
        own_out(2).start()
        tok_in.wait()
        tok_wait(own_end, 0)
        pass_out(0).start()
        gather_first(1)
        tok_wait(own_end, 1)
        pass_out(1).start()
        gather_last(0)
        for c in range(2, len(cuts)):
            tok_wait(own_end, c)
            pass_out(c).start()
        project_far(0)
        project_far(1)
        gather_second(1)
        picks_first()
        for c in range(len(cuts)):
            tok_wait(far_worker, c)
        project_far(2)
        gather_last(1)
        project_own(0)
        project_own(1)
        kv_forward(0)
        project_own(2)
        kv_forward(1)
        picks_last()
        for unit in range(planes - 1, len(units)):
            tok_wait(far_end, unit - planes + 1)
            project_far(unit)
            for earlier in range(unit + 1 if unit == planes - 1 else 0):
                far_copies(earlier)[1].start()
            if unit >= planes:
                far_copies(unit)[1].start()
            project_own(unit)
            kv_forward(unit - 1)
            if unit < last:
                glob_add(unit - planes + 1)
        glob_add(planes - 2)
        kv_forward(last)

    @pl.when(z != own_worker)
    def _():
        own_out(1).start()
        own_out(2).start()
        tok_in.wait()
        picks_first()
        picks_last()
        for unit in range(len(units)):
            here = unit_kv(unit, lane)
            remote(here, here, f_send.at[1, unit], f_recv.at[1, unit], core_peer).wait_recv()
            kv_out(unit)
            if unit:
                kv_forward(unit - 1)
            if planes - 1 <= unit < last:
                glob_add(unit - planes + 1)
        glob_add(planes - 2)
        kv_forward(last)
        for unit in range(len(units)):
            here = unit_q(unit)
            remote(here, here, f_send.at[0, unit], f_recv.at[0, unit], core_peer).wait_recv()

    glob_add(planes - 1)
    glob = glob_sum[: planes * LANES].astype(jnp.bfloat16)
    dev_in.wait()
    sub_in.wait()
    total_blocks = planes * LANES * nblk
    scale = HD ** (-0.5) * math.log2(math.e)
    keys = (3 + R) * BLOCK + glob.shape[0]
    key_row = lax.broadcasted_iota(jnp.int32, (keys, heads * BLOCK), 0)

    def ctx_copy(plane, index):
        return remote(
            ctx.at[plane],
            out_ref.at[:, pl.ds(pl.multiple_of(z * cols, cols), cols)],
            c_send.at[index], c_recv.at[z], at(plane, lane),
        )

    def attend(plane):
        for sub in range(nblk):
            block = (plane * LANES + lane) * nblk + sub
            starts = [
                jnp.maximum(block - 1, 0),
                block,
                jnp.minimum(block + 1, total_blocks - 1),
            ]
            q_rows = slice(sub * BLOCK, (sub + 1) * BLOCK)
            picked = []
            for j in range(R):
                picked.append([
                    dev_ref[j, z * heads + h, block] * nblk + sub_ref[j, z * heads + h, block]
                    for h in range(heads)
                ])

            def side_by_side(first):
                rows = [kv[w, :, first : first + cols] for w in starts]
                for choice in picked:
                    rows.append(jnp.concatenate(
                        [
                            kv[choice[h], :, first + h * HD : first + (h + 1) * HD]
                            for h in range(heads)
                        ],
                        axis=1,
                    ))
                rows.append(glob[:, first : first + cols])
                return jnp.concatenate(rows, axis=0)

            queries = jnp.concatenate(
                [
                    jnp.concatenate(
                        [
                            qry[plane, q_rows, k * HD : (k + 1) * HD]
                            if k == h
                            else jnp.zeros((BLOCK, HD), jnp.bfloat16)
                            for k in range(heads)
                        ],
                        axis=1,
                    )
                    for h in range(heads)
                ],
                axis=0,
            )
            score = lax.dot_general(
                side_by_side(0), queries, (((1,), (1,)), ((), ())),
                preferred_element_type=jnp.float32,
            )
            if sub == 0:
                score = jnp.where((key_row < BLOCK) & (block == 0), -jnp.inf, score)
            if sub == nblk - 1:
                after = (key_row >= 2 * BLOCK) & (key_row < 3 * BLOCK)
                score = jnp.where(after & (block == total_blocks - 1), -jnp.inf, score)
            expo = jnp.exp2((score - jnp.max(score, axis=0, keepdims=True)) * scale)
            soft = (expo * (1.0 / jnp.sum(expo, axis=0, keepdims=True))).astype(jnp.bfloat16)
            res = lax.dot_general(
                soft, side_by_side(cols), (((0,), (0,)), ((), ())),
                preferred_element_type=jnp.float32,
            ).astype(jnp.bfloat16)
            for h in range(heads):
                ctx[plane, q_rows, h * HD : (h + 1) * HD] = res[
                    h * BLOCK : (h + 1) * BLOCK, h * HD : (h + 1) * HD
                ]

    others = (far_end, far_worker, mate)
    for index, plane in enumerate(others):
        attend(plane)
        ctx_copy(plane, index).start()
    attend(z)
    own = pltpu.make_async_copy(
        ctx.at[z], out_ref.at[:, pl.ds(pl.multiple_of(z * cols, cols), cols)], local_sem.at[0]
    )
    own.start()
    own.wait()

    for index, plane in enumerate(others):
        ctx_copy(plane, index).wait_send()
        there = out_ref.at[:, pl.ds(pl.multiple_of(plane * cols, cols), cols)]
        remote(ctx.at[plane], there, c_send.at[index], c_recv.at[plane], core_peer).wait_recv()
    for index in range(2):
        @pl.when(z != workers[index])
        def _():
            for kind in range(2):
                for part in range(3):
                    weight_remote(index, kind, part).wait_send()
    for c in range(len(cuts)):
        own_out(c).wait_send()

    @pl.when(z == own_worker)
    def _():
        for c in range(len(cuts)):
            pass_out(c).wait_send()
        for kind in range(2):
            for index in range(len(moves)):
                gather_out(kind, index).wait_send()
        for unit in range(len(units)):
            for copy in far_copies(unit):
                copy.wait_send()

    for unit in range(len(units)):
        kv_copy(unit, 0, lane, y_peer).wait_send()
        kv_copy(unit, 1, lane, core_peer).wait_send()
        kv_copy(unit, 2, y_lane, core_peer).wait_send()
    for step in range(1, planes):
        pick_copy(step).wait_send()
    for index, (where, peer) in enumerate(partners):
        pick_lane(index, lane, peer).wait_send()


def fused(tokens, w_query, w_keyval, global_off, rand_dev, rand_sub):
    nseq = lax.axis_size("seq")
    ntok, width = tokens.shape
    planes = nseq // LANES
    nblk = ntok // BLOCK
    picked = -(-nseq // 16) * 16
    cols = H // planes * HD
    half = w_query.shape[0] // 2
    dev, sub = rand_dev.transpose(2, 1, 0), rand_sub.transpose(2, 1, 0)
    dma = pltpu.SemaphoreType.DMA
    cuts = chunks_of(ntok)
    units = planes - 1 + len(cuts)
    return pl.pallas_call(
        functools.partial(fused_kernel, planes),
        out_shape=jax.ShapeDtypeStruct((ntok, H * HD), jnp.bfloat16),
        in_specs=[pl.BlockSpec(memory_space=pl.ANY)] * 3
        + [pl.BlockSpec(memory_space=pltpu.SMEM)]
        + [pl.BlockSpec(memory_space=pl.ANY)] * 2,
        out_specs=pl.BlockSpec(memory_space=pl.ANY),
        scratch_shapes=[
            pltpu.VMEM((planes, ntok, width), jnp.bfloat16),
            pltpu.VMEM((2, planes, LANES, 2, half, 3 * cols), jnp.bfloat16),
            pltpu.VMEM((planes, ntok, cols), jnp.bfloat16),
            pltpu.VMEM((nseq * nblk, BLOCK, 2 * cols), jnp.bfloat16),
            pltpu.VMEM((planes, ntok, cols), jnp.bfloat16),
            pltpu.VMEM((planes * nblk, BLOCK, 2 * cols), jnp.bfloat16),
            pltpu.VMEM((LANES, planes, picked, ntok), jnp.bfloat16),
            pltpu.VMEM((planes, ntok, cols), jnp.bfloat16),
            pltpu.VMEM((picked, 2 * cols), jnp.float32),
            pltpu.SMEM(dev.shape, jnp.int32),
            pltpu.SMEM(sub.shape, jnp.int32),
            dma((3,)),
            dma((2, 2, 3)),
            dma((planes, 2, 3)),
            dma((2, 9)),
            dma((2, 9)),
            dma((2, len(cuts))),
            dma((planes, len(cuts))),
            dma((2, units)),
            dma((2, units)),
            dma((3, units)),
            dma((3, units)),
            dma((planes - 1,)),
            dma((planes,)),
            dma((3,)),
            dma((3,)),
            dma((planes - 1,)),
            dma((planes,)),
        ],
        compiler_params=pltpu.CompilerParams(
            collective_id=0, has_side_effects=True, vmem_limit_bytes=60 * 1024 * 1024
        ),
        cost_estimate=pl.CostEstimate(
            flops=2 * planes * ntok * width * 3 * cols,
            bytes_accessed=2 * planes * ntok * width,
            transcendentals=ntok * H * 400,
        ),
    )(tokens, w_query, w_keyval, global_off, dev, sub)


def solution(mesh):
    in_specs = (
        P(("groups", "seq"), None),
        P("seq", None),
        P("seq", None),
        P(("groups", "seq")),
        P("groups", None, None),
        P("groups", None, None),
    )
    out_specs = P(("groups", "seq"), None)
    nseq, groups = mesh.shape["seq"], mesh.shape["groups"]
    planes = nseq // LANES
    paired = groups == 2 and planes * LANES == nseq and planes == 4
    body = fused if paired else local
    return jax.shard_map(body, mesh=mesh, in_specs=in_specs, out_specs=out_specs, check_vma=False)
```

```python
import functools
import math

import jax
import jax.numpy as jnp
from jax import lax
from jax.experimental import pallas as pl
from jax.experimental.pallas import tpu as pltpu
from jax.sharding import PartitionSpec as P

H = 8
HD = 128
BLOCK = 64
R = 3
BLK_DEV = 4
LANES = 4
MESH = pl.DeviceIdType.MESH


def padded_2(block, sides, width):
    for axis, dim in sides:
        count = lax.axis_size(axis)
        forward = [(i, i + 1) for i in range(count - 1)]
        backward = [(target, source) for source, target in forward]
        low = lax.ppermute(
            lax.slice_in_dim(block, block.shape[dim] - width, None, axis=dim), axis, forward
        )
        high = lax.ppermute(lax.slice_in_dim(block, 0, width, axis=dim), axis, backward)
        block = jnp.concatenate([low, block, high], axis=dim)
    return block


def fold_rows(left, piece):
    return jnp.dot(left, piece, preferred_element_type=jnp.float32)


def local(tokens, w_query, w_keyval, global_off, rand_dev, rand_sub):
    ntok = tokens.shape[0]
    nseq = lax.axis_size("seq")
    me_index = lax.axis_index("seq")
    nblk = ntok // BLOCK
    inner = H * HD
    glob_rows = lax.all_gather(jnp.take(tokens, global_off, axis=0), "seq", axis=0, tiled=True)
    left_kv = jnp.concatenate([tokens, glob_rows], axis=0)
    query = fold_rows(tokens, lax.all_gather(w_query, "seq", axis=0, tiled=True))
    keyval = fold_rows(left_kv, lax.all_gather(w_keyval, "seq", axis=0, tiled=True))
    query = query.astype(jnp.bfloat16)
    keyval = keyval.astype(jnp.bfloat16)
    glob_kv = keyval[ntok:]
    keyval = keyval[:ntok]
    glob_kv = glob_kv.reshape(glob_kv.shape[0], 2, H, HD)
    padded = padded_2(keyval, (("seq", 0),), BLOCK)
    window = jnp.concatenate(
        [padded[j * BLOCK : j * BLOCK + ntok].reshape(nblk, BLOCK, 2, H, HD) for j in range(3)],
        axis=1,
    )
    capacity = max(2, 3 * BLK_DEV * H * R // (2 * nseq))
    nreq = nblk * H * R
    dev_all = rand_dev.reshape(nseq, nreq)
    sub_all = rand_sub.reshape(nseq, nreq)
    match = (dev_all == me_index).astype(jnp.int32)
    slot_all = jnp.cumsum(match, axis=1) - 1
    head_of = jnp.arange(nreq, dtype=jnp.int32) // R % H
    code_all = head_of[None, :] * nblk + sub_all
    picked = (match[:, None, :] == 1) & (
        slot_all[:, None, :] == jnp.arange(capacity, dtype=jnp.int32)[None, :, None]
    )
    source = jnp.sum(jnp.where(picked, code_all[:, None, :], 0), axis=2)
    tiles = (
        keyval.reshape(nblk, BLOCK, 2, H, HD)
        .transpose(3, 0, 1, 2, 4)
        .reshape(H * nblk, BLOCK, 2 * HD)
    )
    outgoing = jnp.take(tiles, source, axis=0)
    incoming = lax.all_to_all(outgoing, "seq", split_axis=0, concat_axis=0, tiled=True)
    my_dev = lax.dynamic_slice_in_dim(rand_dev, me_index * nblk, nblk, 0).reshape(nreq)
    onehot = (my_dev[:, None] == jnp.arange(nseq, dtype=jnp.int32)[None, :]).astype(jnp.int32)
    my_slot = jnp.sum(onehot * (jnp.cumsum(onehot, axis=0) - 1), axis=1)
    flat_index = my_dev * capacity + my_slot
    fetched = jnp.take(incoming.reshape(nseq * capacity, BLOCK, 2 * HD), flat_index, axis=0)
    fetched = fetched.reshape(nblk, H, R, BLOCK, 2, HD)
    scale = HD ** (-0.5)
    qry = query.reshape(nblk, BLOCK, H, HD)
    s_win = (
        jnp.einsum("bqhd,bkhd->bhqk", qry, window[:, :, 0], preferred_element_type=jnp.float32)
        * scale
    )
    s_rnd = (
        jnp.einsum(
            "bqhd,bhrkd->bhqrk", qry, fetched[:, :, :, :, 0], preferred_element_type=jnp.float32
        ).reshape(nblk, H, BLOCK, R * BLOCK)
        * scale
    )
    s_glb = (
        jnp.einsum("bqhd,ghd->bhqg", qry, glob_kv[:, 0], preferred_element_type=jnp.float32) * scale
    )
    blk_ids = me_index * nblk + jnp.arange(nblk, dtype=jnp.int32)
    left_ok = jnp.repeat((blk_ids > 0)[:, None], BLOCK, axis=1)
    right_ok = jnp.repeat((blk_ids < nseq * nblk - 1)[:, None], BLOCK, axis=1)
    middle_ok = jnp.ones((nblk, BLOCK), dtype=bool)
    window_ok = jnp.concatenate([left_ok, middle_ok, right_ok], axis=1)
    s_win = jnp.where(window_ok[:, None, None, :], s_win, -jnp.inf)
    scores = jnp.concatenate([s_win, s_rnd, s_glb], axis=3)
    highest = jnp.max(scores, axis=3, keepdims=True)
    expo = jnp.exp(scores - highest)
    weights = (expo / jnp.sum(expo, axis=3, keepdims=True)).astype(jnp.bfloat16)
    w_win = weights[..., : 3 * BLOCK]
    w_rnd = weights[..., 3 * BLOCK : 3 * BLOCK + R * BLOCK].reshape(nblk, H, BLOCK, R, BLOCK)
    w_glb = weights[..., 3 * BLOCK + R * BLOCK :]
    ctx = jnp.einsum("bhqk,bkhd->bqhd", w_win, window[:, :, 1], preferred_element_type=jnp.float32)
    ctx = ctx + jnp.einsum(
        "bhqrk,bhrkd->bqhd", w_rnd, fetched[:, :, :, :, 1], preferred_element_type=jnp.float32
    )
    ctx = ctx + jnp.einsum(
        "bhqg,ghd->bqhd", w_glb, glob_kv[:, 1], preferred_element_type=jnp.float32
    )
    return ctx.reshape(ntok, inner).astype(jnp.bfloat16)


def chunks_of(ntok):
    half, quarter = ntok // 2, ntok // 4
    return ((0, half), (half, quarter), (half + quarter, quarter))


def fused_kernel(
    planes, tok_hbm, wq_hbm, wkv_hbm, off_ref, dev_hbm, sub_hbm, out_ref,
    tok, wts, qry, kv, far_q, far_kv, picks, ctx, glob_sum, dev_ref, sub_ref,
    local_sem, w_send, w_recv, g_send, g_recv, t_send, t_recv, f_send, f_recv,
    k_send, k_recv, p_send, p_recv, o_send, o_recv, c_send, c_recv,
):
    ntok = tok_hbm.shape[0]
    nblk = ntok // BLOCK
    heads = H // planes
    cols = heads * HD
    half = wts.shape[4]
    x = lax.axis_index("groups")
    me = lax.axis_index("seq")
    z = me // LANES
    lane = me % LANES
    core_lane = lane + 1 - 2 * (lane % 2)
    y_lane = (lane + 2) % LANES
    diag_lane = (core_lane + 2) % LANES
    mid = planes // 2
    workers, ends = (mid - 1, mid), (0, planes - 1)
    lower = z < mid
    own_worker = jnp.where(lower, workers[0], workers[1])
    own_end = jnp.where(lower, ends[0], ends[1])
    far_worker = jnp.where(lower, workers[1], workers[0])
    far_end = jnp.where(lower, ends[1], ends[0])
    mate = jnp.where(z == own_worker, own_end, own_worker)
    order = [own_worker, own_end, far_worker, far_end]

    def at(plane, where):
        return {"seq": plane * LANES + where}

    x_peer = {"groups": 1 - x}
    core_peer = at(z, core_lane)
    y_peer = at(z, y_lane)
    diag_peer = at(z, diag_lane)
    partners = ((y_lane, y_peer), (core_lane, core_peer), (diag_lane, diag_peer))

    def remote(src, dst, send, recv, peer):
        return pltpu.make_async_remote_copy(
            src_ref=src, dst_ref=dst, send_sem=send, recv_sem=recv, device_id=peer,
            device_id_type=MESH,
        )

    dev_in = pltpu.make_async_copy(dev_hbm, dev_ref, local_sem.at[0])
    dev_in.start()
    sub_in = pltpu.make_async_copy(sub_hbm, sub_ref, local_sem.at[1])
    sub_in.start()
    tok_in = pltpu.make_async_copy(tok_hbm, tok.at[z], local_sem.at[2])
    tok_in.start()

    barrier = pltpu.get_barrier_semaphore()
    for step in range(1, planes):
        pl.semaphore_signal(
            barrier, inc=1, device_id=at((z + step) % planes, lane), device_id_type=MESH
        )
    for peer in (x_peer, core_peer, y_peer, diag_peer):
        pl.semaphore_signal(barrier, inc=1, device_id=peer, device_id_type=MESH)
    pl.semaphore_wait(barrier, planes - 1 + 4)

    def weight_refs(index, kind, part):
        plane = (ends, workers)[kind][index]
        rows = pl.ds(pl.multiple_of(x * half, half), half)
        first = (0, 0, H * HD)[part] + plane * cols
        src = (wq_hbm, wkv_hbm, wkv_hbm)[part].at[rows, pl.ds(first, cols)]
        return src, wts.at[kind, z, lane, x, :, pl.ds(part * cols, cols)]

    def weight_remote(index, kind, part):
        src, dst = weight_refs(index, kind, part)
        return remote(
            src, dst, w_send.at[index, kind, part], w_recv.at[z, kind, part],
            at(workers[index], lane),
        )

    def weights_out(kind):
        for index in range(2):
            for part in range(3):
                @pl.when(z != workers[index])
                def _():
                    weight_remote(index, kind, part).start()

                @pl.when(z == workers[index])
                def _():
                    src, dst = weight_refs(index, kind, part)
                    pltpu.make_async_copy(src, dst, w_recv.at[z, kind, part]).start()

    def weights_in(kind):
        for plane in range(planes):
            for part in range(3):
                here = wts.at[kind, plane, lane, x, :, pl.ds(part * cols, cols)]
                remote(here, here, w_send.at[0, kind, part], w_recv.at[plane, kind, part], core_peer).wait_recv()

    towards = jnp.where(lower, z + 1, z - 1)
    cuts = chunks_of(ntok)
    chunks = [pl.ds(first, count) for first, count in cuts]

    def own_out(c):
        return remote(
            tok_hbm.at[chunks[c]], tok.at[z, chunks[c]], t_send.at[0, c], t_recv.at[z, c],
            at(towards, lane),
        )

    def pass_out(c):
        ref = tok.at[own_end, chunks[c]]
        return remote(ref, ref, t_send.at[1, c], t_recv.at[own_end, c], at(towards, lane))

    def tok_wait(plane, c):
        ref = tok.at[plane, chunks[c]]
        remote(ref, ref, t_send.at[0, c], t_recv.at[plane, c], core_peer).wait_recv()

    weights_out(0)
    weights_out(1)
    own_out(0).start()

    at_row = lax.broadcasted_iota(jnp.int32, picks.shape[2:], 0) == me
    at_event = lax.broadcasted_iota(jnp.int32, picks.shape[2:], 1) == off_ref[0]
    picks[lane, z] = jnp.where(at_row & at_event, 1.0, 0.0).astype(jnp.bfloat16)

    def pick_copy(step):
        return remote(picks.at[lane, z], picks.at[lane, z], p_send.at[step - 1], p_recv.at[z], at((z + step) % planes, lane))

    for step in range(1, planes):
        pick_copy(step).start()

    width = 3 * cols
    every, left, right = pl.ds(0, width), pl.ds(0, width // 2), pl.ds(width // 2, width // 2)
    moves = (
        (x, lane, every, x_peer, 1 - x, lane),
        (x, lane, every, y_peer, x, y_lane),
        (x, lane, every, core_peer, x, core_lane),
        (1 - x, lane, left, y_peer, 1 - x, y_lane),
        (1 - x, lane, every, core_peer, 1 - x, core_lane),
        (x, y_lane, right, x_peer, 1 - x, y_lane),
        (x, y_lane, every, core_peer, x, diag_lane),
        (1 - x, y_lane, left, core_peer, 1 - x, diag_lane),
        (1 - x, y_lane, right, core_peer, 1 - x, diag_lane),
    )

    def gather_out(kind, index):
        group, where, part, peer = moves[index][:4]
        ref = wts.at[kind, :, where, group, :, part]
        return remote(ref, ref, g_send.at[kind, index], g_recv.at[kind, index], peer)

    def gather_wait(kind, index):
        part, peer, group, where = moves[index][2:]
        ref = wts.at[kind, :, where, group, :, part]
        remote(ref, ref, g_send.at[kind, index], g_recv.at[kind, index], peer).wait_recv()

    def gather_first(kind):
        weights_in(kind)
        for index in range(3):
            gather_out(kind, index).start()

    def gather_second(kind):
        gather_wait(kind, 0)
        gather_out(kind, 3).start()
        gather_out(kind, 4).start()
        gather_wait(kind, 1)
        gather_out(kind, 5).start()
        gather_out(kind, 6).start()

    def gather_last(kind):
        gather_wait(kind, 3)
        gather_out(kind, 7).start()
        gather_wait(kind, 5)
        gather_out(kind, 8).start()
        for index in (2, 4, 6, 7, 8):
            gather_wait(kind, index)

    def kv_rows(ref, plane, where, first=0, count=nblk):
        return ref.at[pl.ds((plane * LANES + where) * nblk + first, count)]

    units = [(i, 0, ntok) for i in range(planes - 1)]
    units += [(planes - 1, first, count) for first, count in cuts]

    def unit_kv(unit, where):
        index, first, count = units[unit]
        return kv_rows(kv, order[index], where, first // BLOCK, count // BLOCK)

    def unit_q(unit):
        index, first, count = units[unit]
        return qry.at[order[index], pl.ds(first, count)]

    def kv_copy(unit, which, where, peer):
        ref = unit_kv(unit, where)
        return remote(ref, ref, k_send.at[which, unit], k_recv.at[which, unit], peer)

    def kv_out(unit):
        kv_copy(unit, 0, lane, y_peer).start()
        kv_copy(unit, 1, lane, core_peer).start()

    def kv_forward(unit):
        kv_copy(unit, 0, y_lane, y_peer).wait_recv()
        kv_copy(unit, 2, y_lane, core_peer).start()

    def project(unit, kind):
        index, first, count = units[unit]
        weights = wts[kind].reshape(-1, width)
        rows = tok[order[index], pl.ds(first, count)]
        res = jnp.dot(rows, weights, preferred_element_type=jnp.float32).astype(jnp.bfloat16)
        return res[:, :cols], res[:, cols:].reshape(count // BLOCK, BLOCK, 2 * cols)

    def far_refs(unit):
        index, first, count = units[unit]
        blocks = pl.ds(index * nblk + first // BLOCK, count // BLOCK)
        return far_q.at[index, pl.ds(first, count)], far_kv.at[blocks]

    def far_copies(unit):
        from_q, from_kv = far_refs(unit)
        return (
            remote(from_kv, unit_kv(unit, lane), f_send.at[1, unit], f_recv.at[1, unit], at(mate, lane)),
            remote(from_q, unit_q(unit), f_send.at[0, unit], f_recv.at[0, unit], at(mate, lane)),
        )

    def project_far(unit):
        from_q, from_kv = far_refs(unit)
        from_q[...], from_kv[...] = project(unit, 0)
        for copy in far_copies(unit):
            copy.start()

    def project_own(unit):
        unit_q(unit)[...], unit_kv(unit, lane)[...] = project(unit, 1)
        kv_out(unit)

    def pick_lane(index, where, peer):
        return remote(picks.at[where], picks.at[where], o_send.at[index], o_recv.at[index], peer)

    def picks_first():
        for step in range(1, planes):
            source = (z + step) % planes
            ref = picks.at[lane, source]
            remote(ref, ref, p_send.at[0], p_recv.at[source], core_peer).wait_recv()
        for index, (where, peer) in enumerate(partners):
            pick_lane(index, lane, peer).start()

    def picks_last():
        for index, (where, peer) in enumerate(partners):
            pick_lane(index, where, peer).wait_recv()

    def glob_add(index):
        for unit in [u for u in range(len(units)) if units[u][0] == index]:
            kv_copy(unit, 1, core_lane, core_peer).wait_recv()
            kv_copy(unit, 2, diag_lane, core_peer).wait_recv()
        total = jnp.zeros(glob_sum.shape, jnp.float32) if index == 0 else glob_sum[...]
        for where in range(LANES):
            rows = kv_rows(kv, order[index], where)[...].reshape(ntok, 2 * cols)
            total = total + jnp.dot(
                picks[where, order[index]], rows, preferred_element_type=jnp.float32
            )
        glob_sum[...] = total

    last = len(units) - 1

    @pl.when(z == own_worker)
    def _():
        gather_first(0)
        own_out(1).start()
        gather_second(0)
        own_out(2).start()
        tok_in.wait()
        tok_wait(own_end, 0)
        pass_out(0).start()
        gather_first(1)
        tok_wait(own_end, 1)
        pass_out(1).start()
        gather_last(0)
        project_far(0)
        for c in range(2, len(cuts)):
            tok_wait(own_end, c)
            pass_out(c).start()
        project_far(1)
        gather_second(1)
        picks_first()
        for c in range(len(cuts)):
            tok_wait(far_worker, c)
        project_far(2)
        gather_last(1)
        project_own(0)
        project_own(1)
        kv_forward(0)
        project_own(2)
        kv_forward(1)
        picks_last()
        for unit in range(planes - 1, len(units)):
            tok_wait(far_end, unit - planes + 1)
            project_far(unit)
            project_own(unit)
            kv_forward(unit - 1)
            if unit < last:
                glob_add(unit - planes + 1)
        glob_add(planes - 2)
        kv_forward(last)

    @pl.when(z != own_worker)
    def _():
        own_out(1).start()
        own_out(2).start()
        tok_in.wait()
        picks_first()
        picks_last()
        for unit in range(len(units)):
            here = unit_kv(unit, lane)
            remote(here, here, f_send.at[1, unit], f_recv.at[1, unit], core_peer).wait_recv()
            kv_out(unit)
            if unit:
                kv_forward(unit - 1)
            if planes - 1 <= unit < last:
                glob_add(unit - planes + 1)
        glob_add(planes - 2)
        kv_forward(last)
        for unit in range(len(units)):
            here = unit_q(unit)
            remote(here, here, f_send.at[0, unit], f_recv.at[0, unit], core_peer).wait_recv()

    glob_add(planes - 1)
    glob = glob_sum[: planes * LANES].astype(jnp.bfloat16)
    dev_in.wait()
    sub_in.wait()
    total_blocks = planes * LANES * nblk
    scale = HD ** (-0.5) * math.log2(math.e)
    keys = (3 + R) * BLOCK + glob.shape[0]
    key_row = lax.broadcasted_iota(jnp.int32, (keys, heads * BLOCK), 0)

    def ctx_copy(plane, index):
        return remote(
            ctx.at[plane],
            out_ref.at[:, pl.ds(pl.multiple_of(z * cols, cols), cols)],
            c_send.at[index], c_recv.at[z], at(plane, lane),
        )

    def attend(plane):
        for sub in range(nblk):
            block = (plane * LANES + lane) * nblk + sub
            starts = [
                jnp.maximum(block - 1, 0),
                block,
                jnp.minimum(block + 1, total_blocks - 1),
            ]
            q_rows = slice(sub * BLOCK, (sub + 1) * BLOCK)
            picked = []
            for j in range(R):
                picked.append([
                    dev_ref[j, z * heads + h, block] * nblk + sub_ref[j, z * heads + h, block]
                    for h in range(heads)
                ])

            def side_by_side(first):
                rows = [kv[w, :, first : first + cols] for w in starts]
                for choice in picked:
                    rows.append(jnp.concatenate(
                        [
                            kv[choice[h], :, first + h * HD : first + (h + 1) * HD]
                            for h in range(heads)
                        ],
                        axis=1,
                    ))
                rows.append(glob[:, first : first + cols])
                return jnp.concatenate(rows, axis=0)

            queries = jnp.concatenate(
                [
                    jnp.concatenate(
                        [
                            qry[plane, q_rows, k * HD : (k + 1) * HD]
                            if k == h
                            else jnp.zeros((BLOCK, HD), jnp.bfloat16)
                            for k in range(heads)
                        ],
                        axis=1,
                    )
                    for h in range(heads)
                ],
                axis=0,
            )
            score = lax.dot_general(
                side_by_side(0), queries, (((1,), (1,)), ((), ())),
                preferred_element_type=jnp.float32,
            )
            if sub == 0:
                score = jnp.where((key_row < BLOCK) & (block == 0), -jnp.inf, score)
            if sub == nblk - 1:
                after = (key_row >= 2 * BLOCK) & (key_row < 3 * BLOCK)
                score = jnp.where(after & (block == total_blocks - 1), -jnp.inf, score)
            expo = jnp.exp2((score - jnp.max(score, axis=0, keepdims=True)) * scale)
            soft = (expo * (1.0 / jnp.sum(expo, axis=0, keepdims=True))).astype(jnp.bfloat16)
            res = lax.dot_general(
                soft, side_by_side(cols), (((0,), (0,)), ((), ())),
                preferred_element_type=jnp.float32,
            ).astype(jnp.bfloat16)
            for h in range(heads):
                ctx[plane, q_rows, h * HD : (h + 1) * HD] = res[
                    h * BLOCK : (h + 1) * BLOCK, h * HD : (h + 1) * HD
                ]

    others = (far_end, far_worker, mate)
    for index, plane in enumerate(others):
        attend(plane)
        ctx_copy(plane, index).start()
    attend(z)
    own = pltpu.make_async_copy(
        ctx.at[z], out_ref.at[:, pl.ds(pl.multiple_of(z * cols, cols), cols)], local_sem.at[0]
    )
    own.start()
    own.wait()

    for index, plane in enumerate(others):
        ctx_copy(plane, index).wait_send()
        there = out_ref.at[:, pl.ds(pl.multiple_of(plane * cols, cols), cols)]
        remote(ctx.at[plane], there, c_send.at[index], c_recv.at[plane], core_peer).wait_recv()
    for index in range(2):
        @pl.when(z != workers[index])
        def _():
            for kind in range(2):
                for part in range(3):
                    weight_remote(index, kind, part).wait_send()
    for c in range(len(cuts)):
        own_out(c).wait_send()

    @pl.when(z == own_worker)
    def _():
        for c in range(len(cuts)):
            pass_out(c).wait_send()
        for kind in range(2):
            for index in range(len(moves)):
                gather_out(kind, index).wait_send()
        for unit in range(len(units)):
            for copy in far_copies(unit):
                copy.wait_send()

    for unit in range(len(units)):
        kv_copy(unit, 0, lane, y_peer).wait_send()
        kv_copy(unit, 1, lane, core_peer).wait_send()
        kv_copy(unit, 2, y_lane, core_peer).wait_send()
    for step in range(1, planes):
        pick_copy(step).wait_send()
    for index, (where, peer) in enumerate(partners):
        pick_lane(index, lane, peer).wait_send()


def fused(tokens, w_query, w_keyval, global_off, rand_dev, rand_sub):
    nseq = lax.axis_size("seq")
    ntok, width = tokens.shape
    planes = nseq // LANES
    nblk = ntok // BLOCK
    picked = -(-nseq // 16) * 16
    cols = H // planes * HD
    half = w_query.shape[0] // 2
    dev, sub = rand_dev.transpose(2, 1, 0), rand_sub.transpose(2, 1, 0)
    dma = pltpu.SemaphoreType.DMA
    cuts = chunks_of(ntok)
    units = planes - 1 + len(cuts)
    return pl.pallas_call(
        functools.partial(fused_kernel, planes),
        out_shape=jax.ShapeDtypeStruct((ntok, H * HD), jnp.bfloat16),
        in_specs=[pl.BlockSpec(memory_space=pl.ANY)] * 3
        + [pl.BlockSpec(memory_space=pltpu.SMEM)]
        + [pl.BlockSpec(memory_space=pl.ANY)] * 2,
        out_specs=pl.BlockSpec(memory_space=pl.ANY),
        scratch_shapes=[
            pltpu.VMEM((planes, ntok, width), jnp.bfloat16),
            pltpu.VMEM((2, planes, LANES, 2, half, 3 * cols), jnp.bfloat16),
            pltpu.VMEM((planes, ntok, cols), jnp.bfloat16),
            pltpu.VMEM((nseq * nblk, BLOCK, 2 * cols), jnp.bfloat16),
            pltpu.VMEM((planes, ntok, cols), jnp.bfloat16),
            pltpu.VMEM((planes * nblk, BLOCK, 2 * cols), jnp.bfloat16),
            pltpu.VMEM((LANES, planes, picked, ntok), jnp.bfloat16),
            pltpu.VMEM((planes, ntok, cols), jnp.bfloat16),
            pltpu.VMEM((picked, 2 * cols), jnp.float32),
            pltpu.SMEM(dev.shape, jnp.int32),
            pltpu.SMEM(sub.shape, jnp.int32),
            dma((3,)),
            dma((2, 2, 3)),
            dma((planes, 2, 3)),
            dma((2, 9)),
            dma((2, 9)),
            dma((2, len(cuts))),
            dma((planes, len(cuts))),
            dma((2, units)),
            dma((2, units)),
            dma((3, units)),
            dma((3, units)),
            dma((planes - 1,)),
            dma((planes,)),
            dma((3,)),
            dma((3,)),
            dma((planes - 1,)),
            dma((planes,)),
        ],
        compiler_params=pltpu.CompilerParams(
            collective_id=0, has_side_effects=True, vmem_limit_bytes=60 * 1024 * 1024
        ),
        cost_estimate=pl.CostEstimate(
            flops=2 * planes * ntok * width * 3 * cols,
            bytes_accessed=2 * planes * ntok * width,
            transcendentals=ntok * H * 400,
        ),
    )(tokens, w_query, w_keyval, global_off, dev, sub)


def solution(mesh):
    in_specs = (
        P(("groups", "seq"), None),
        P("seq", None),
        P("seq", None),
        P(("groups", "seq")),
        P("groups", None, None),
        P("groups", None, None),
    )
    out_specs = P(("groups", "seq"), None)
    nseq, groups = mesh.shape["seq"], mesh.shape["groups"]
    planes = nseq // LANES
    paired = groups == 2 and planes * LANES == nseq and planes == 4
    body = fused if paired else local
    return jax.shard_map(body, mesh=mesh, in_specs=in_specs, out_specs=out_specs, check_vma=False)
```
